32 devices in a mesh: pair: 2 (over x), rows: 16 (over z, y, core).
Axes of the slice: x: 2, y: 2, z: 4, core: 2. Of those that a mesh axis runs over, the one named last changes fastest.
Arguments:
- hidden_in: bfloat16 [64, 2, 256, 768], P('rows', 'pair'), may hold values from -6 to 6
- input_proj: float32 [768, 2304], P(('pair', 'rows')), may hold values from -0.21875 to 0.21875
- query_bias: float32 [768], P(('pair', 'rows')), may hold values from -1.5 to 1.5
- value_bias: float32 [768], P(('pair', 'rows')), may hold values from -1.5 to 1.5
- output_proj: float32 [768, 768], P(('pair', 'rows')), may hold values from -1.25 to 1.25
- output_bias: float32 [768], P(('pair', 'rows')), may hold values from -1.5 to 1.5
- first_gain: float32 [768], P(('pair', 'rows')), may hold values from 0.5 to 1.5
- first_shift: float32 [768], P(('pair', 'rows')), may hold values from -1.5 to 1.5
- inner_proj: float32 [768, 3072], P(('pair', 'rows')), may hold values from -0.21875 to 0.21875
- inner_bias: float32 [3072], P(('pair', 'rows')), may hold values from -1.5 to 1.5
- outer_proj: float32 [3072, 768], P(('pair', 'rows')), may hold values from -0.109375 to 0.109375
- outer_bias: float32 [768], P(('pair', 'rows')), may hold values from -1.5 to 1.5
- second_gain: float32 [768], P(('pair', 'rows')), may hold values from 0.5 to 1.5
- second_shift: float32 [768], P(('pair', 'rows')), may hold values from -1.5 to 1.5
- cotangent: bfloat16 [64, 2, 256, 768], P('rows', 'pair'), may hold values from -6 to 6
- pair_lengths: int32 [64, 2, 8], P('rows'), may hold values from 1 to 32, as said below
Outputs:
- layer_out: bfloat16 [64, 2, 256, 768], P('rows', 'pair')
- grad_input: float32 [64, 2, 256, 768], P('rows', 'pair')
- grad_input_proj: float32 [768, 2304], P(('pair', 'rows'))
- grad_query_bias: float32 [768], P(('pair', 'rows'))
- grad_value_bias: float32 [768], P(('pair', 'rows'))
- grad_output_proj: float32 [768, 768], P(('pair', 'rows'))
- grad_output_bias: float32 [768], P(('pair', 'rows'))
- grad_first_gain: float32 [768], P(('pair', 'rows'))
- grad_first_shift: float32 [768], P(('pair', 'rows'))
- grad_inner_proj: float32 [768, 3072], P(('pair', 'rows'))
- grad_inner_bias: float32 [3072], P(('pair', 'rows'))
- grad_outer_proj: float32 [3072, 768], P(('pair', 'rows'))
- grad_outer_bias: float32 [768], P(('pair', 'rows'))
- grad_second_gain: float32 [768], P(('pair', 'rows'))
- grad_second_shift: float32 [768], P(('pair', 'rows'))
The draws below stay inside these ranges and needn't reach their ends.
Inputs may be any that keep to these rules, and one draw needn't show every extreme that they name: pair_lengths[r, h, p] counts the tokens of pair p of row r on half h (0 premise, 1 hypothesis); the pairs of a half fill its slots from slot 0 in order and the rest of its 256 slots are padding; every pair has tokens on both halves; some entry equals 32.
All inputs are finite; a program needn't handle non-finite values.
Results may differ from the reference program's by a relative error of at most 0.013.
The reference program's roundings to bfloat16 on the way count: a program that leaves them out, or rounds other values in their place, can miss the bound.
Values may be sent and summed in bfloat16 or wider, within the bound.
A program may use at most 192 MiB of HBM per device.

```python
import jax
import jax.numpy as jnp
from jax import lax

D = 768
HEADS = 12
HEAD_DIM = 64
FF = 3072
SLOTS = 256
PAIRS = 8
MOST = 32
ROWS = 64


def draw_pair_lengths(key, part):
    key = jax.random.fold_in(key, 11)
    first_key, second_key, third_key = jax.random.split(key, 3)
    premise = jax.random.randint(first_key, (ROWS, 1, PAIRS), MOST // 4, MOST + 1, dtype=jnp.int32)
    hypothesis = jax.random.randint(second_key, (ROWS, 1, PAIRS), 1, MOST * 3 // 4 + 1, dtype=jnp.int32)
    lengths_all = jnp.concatenate([premise, hypothesis], axis=1)
    chosen = jax.random.randint(third_key, (), 0, PAIRS, dtype=jnp.int32)
    row_first = jnp.arange(ROWS, dtype=jnp.int32)[:, None, None] == 0
    half_first = jnp.arange(2, dtype=jnp.int32)[None, :, None] == 0
    pair_chosen = jnp.arange(PAIRS, dtype=jnp.int32)[None, None, :] == chosen
    marker = row_first & half_first & pair_chosen
    return jnp.where(marker, jnp.int32(MOST), lengths_all).astype(jnp.int32)


def with_spikes(values, stream_key, source, target, blocks, factor):
    def block_of(axis_at):
        return (jnp.arange(values.shape[axis_at]) // (values.shape[axis_at] // blocks)).reshape((-1,) + (1,) * (values.ndim - 1 - axis_at))

    near = jax.random.permutation(stream_key, blocks)[block_of(target)]
    other_side = (block_of(target) + blocks // 2) % blocks
    return jnp.where((block_of(source) == near) | (block_of(source) == other_side), factor * values, values)


def levels(stream_key, dims, shards, low, high):
    factor_of, own = 1.0, jax.random.fold_in(stream_key, 6)
    for position, parts in shards:
        heights = jnp.exp(jax.random.uniform(jax.random.fold_in(own, position), (parts,), jnp.float32, low / len(shards), high / len(shards)))
        factor_of = factor_of * jnp.repeat(heights, dims[position] // parts).reshape([-1 if axis == position else 1 for axis in range(len(dims))])
    return factor_of


def centred(key, shape, scale, most, shards=(), held_as=jnp.bfloat16):
    values = jax.random.normal(key, shape, jnp.float32) * scale
    if len(shards) > 0:
        values = levels(key, shape, shards, -0.22, 0.18) * values
    return jnp.clip(values, min=-most, max=most).astype(held_as)


def gaussian_with(rng, extent, scale, limit, shards, heavy, held_as=jnp.bfloat16):
    entries = scale * jax.random.normal(rng, extent, jnp.float32)
    if shards:
        entries = entries * levels(rng, extent, shards, -0.22, 0.18)
    return jnp.clip(with_spikes(entries, jax.random.fold_in(rng, 3), *heavy), -limit, limit).astype(held_as)


def setup_inputs(seed: int = 0) -> dict:
    key_list = jax.random.split(jax.random.key(seed), 17)
    hidden_in = gaussian_with(key_list[0], (ROWS, 2, SLOTS, D), 1.0, 6.0, ((0, 16), (1, 2)), (0, 3, 16, 2.0))
    input_proj = centred(key_list[1], (D, 3 * D), D ** -0.5, 0.21875, ((0, 32),), jnp.float32)
    query_bias = centred(key_list[2], (D,), 0.3, 1.5, ((0, 32),), jnp.float32)
    value_bias = centred(key_list[3], (D,), 0.3, 1.5, ((0, 32),), jnp.float32)
    output_proj = centred(key_list[4], (D, D), (D // 32) ** -0.5, 1.25, ((0, 32),), jnp.float32)
    output_bias = centred(key_list[5], (D,), 0.3, 1.5, ((0, 32),), jnp.float32)
    first_gain = jnp.clip(1.0 + 0.1 * jax.random.normal(key_list[6], (D,), jnp.float32), 0.5, 1.5)
    first_shift = centred(key_list[7], (D,), 0.3, 1.5, ((0, 32),), jnp.float32)
    inner_proj = centred(key_list[8], (D, FF), D ** -0.5, 0.21875, ((0, 32),), jnp.float32)
    inner_bias = centred(key_list[9], (FF,), 0.3, 1.5, ((0, 32),), jnp.float32)
    outer_proj = centred(key_list[10], (FF, D), FF ** -0.5, 0.109375, ((0, 32),), jnp.float32)
    outer_bias = centred(key_list[11], (D,), 0.3, 1.5, ((0, 32),), jnp.float32)
    second_gain = jnp.clip(1.0 + 0.1 * jax.random.normal(key_list[12], (D,), jnp.float32), 0.5, 1.5)
    second_shift = centred(key_list[13], (D,), 0.3, 1.5, ((0, 32),), jnp.float32)
    cotangent = gaussian_with(key_list[14], (ROWS, 2, SLOTS, D), 1.0, 6.0, ((0, 16), (1, 2)), (0, 3, 16, 2.0))
    pair_lengths = draw_pair_lengths(jax.random.fold_in(key_list[16], 71), 0)
    return {"hidden_in": hidden_in, "input_proj": input_proj, "query_bias": query_bias, "value_bias": value_bias, "output_proj": output_proj, "output_bias": output_bias, "first_gain": first_gain, "first_shift": first_shift, "inner_proj": inner_proj, "inner_bias": inner_bias, "outer_proj": outer_proj, "outer_bias": outer_bias, "second_gain": second_gain, "second_shift": second_shift, "cotangent": cotangent, "pair_lengths": pair_lengths}


norm_epsilon = 1e-12
highest = lax.Precision.HIGHEST

@jax.custom_vjp
def low(v):
    return lax.optimization_barrier(v.astype(jnp.bfloat16)).astype(jnp.float32)

@jax.custom_vjp
def low_back(v):
    return v

def low_keep(v):
    return (low(v), None)

def low_pass(kept, grad):
    return (grad,)

def back_keep(v):
    return (v, None)

def back_low(kept, grad):
    return (low(grad),)
low.defvjp(low_keep, low_pass)
low_back.defvjp(back_keep, back_low)

def group_ids(pair_lengths, slot_count):
    pair_ends = jnp.cumsum(pair_lengths, axis=-1)
    positions = jnp.arange(slot_count, dtype=jnp.int32)
    passed = lax.optimization_barrier(jnp.sum((positions[:, None] >= pair_ends[..., None, :]).astype(jnp.int32), axis=-1))
    halves = jnp.arange(2, dtype=jnp.int32)[None, :, None]
    return jnp.where(passed < pair_lengths.shape[-1], passed, -1 - halves)

def product(left, right):
    return jnp.dot(left, right, precision=highest, preferred_element_type=jnp.float32)

def normalize(totals, gain_row, shift_row):
    average = lax.optimization_barrier(jnp.mean(totals, axis=-1, keepdims=True))
    centered = totals - average
    spread = lax.optimization_barrier(jnp.mean(centered * centered, axis=-1, keepdims=True))
    return centered * lax.rsqrt(spread + norm_epsilon) * gain_row + shift_row

def attend(operands):
    packed_row, group_row = operands
    query_heads = packed_row[:, 0]
    key_heads = packed_row[:, 1]
    value_heads = packed_row[:, 2]
    score_scale = HEAD_DIM ** (-0.5)
    scores = jnp.einsum('qhd,khd->hqk', query_heads, key_heads, precision=highest) * score_scale
    scores = low_back(scores)
    allowed = group_row[:, None] == group_row[None, :]
    scores = jnp.where(allowed[None], scores, -1e+30)
    soft_weights = jax.nn.softmax(scores, axis=-1)
    context_row = jnp.einsum('hqk,khd->qhd', low(soft_weights), value_heads, precision=highest)
    return low(low_back(context_row))

def forward(hidden, parameters, groups):
    rounded = [low(entry) for entry in parameters]
    input_proj, query_bias, value_bias, output_proj, output_bias, first_gain, first_shift, inner_proj, inner_bias, outer_proj, outer_bias, second_gain, second_shift = rounded
    row_total = hidden.shape[0]
    model_width = hidden.shape[-1]
    flattened = hidden.reshape(-1, model_width)
    bias_packed = jnp.concatenate([query_bias, jnp.zeros_like(query_bias), value_bias])
    packed = low(low_back(product(flattened, input_proj) + bias_packed))
    packed = packed.reshape(row_total, 2 * SLOTS, 3, HEADS, HEAD_DIM)
    group_rows = groups.reshape(row_total, 2 * SLOTS)
    context = lax.map(jax.checkpoint(attend), (packed, group_rows)).reshape(-1, model_width)
    projected = low_back(product(context, output_proj) + output_bias)
    first_out = normalize(flattened + projected, first_gain, first_shift)
    inner_pre = low_back(product(low(first_out), inner_proj) + inner_bias)
    activated = low(jax.nn.gelu(inner_pre, approximate=False))
    outer_pre = low_back(product(activated, outer_proj) + outer_bias)
    result = normalize(first_out + outer_pre, second_gain, second_shift)
    return result.reshape(hidden.shape)

def reference(hidden_in, input_proj, query_bias, value_bias, output_proj, output_bias, first_gain, first_shift, inner_proj, inner_bias, outer_proj, outer_bias, second_gain, second_shift, cotangent, pair_lengths):
    groups = group_ids(pair_lengths, SLOTS)
    valid = (groups >= 0).astype(jnp.float32)[..., None]

    def apply_layer(hidden, *parameters):
        return forward(hidden, parameters, groups)
    result, pullback = jax.vjp(apply_layer, hidden_in.astype(jnp.float32), input_proj, query_bias, value_bias, output_proj, output_bias, first_gain, first_shift, inner_proj, inner_bias, outer_proj, outer_bias, second_gain, second_shift)
    gradients = pullback(cotangent.astype(jnp.float32) * valid)
    return (result.astype(jnp.bfloat16), gradients[0], gradients[1], gradients[2], gradients[3], gradients[4], gradients[5], gradients[6], gradients[7], gradients[8], gradients[9], gradients[10], gradients[11], gradients[12], gradients[13])
```

```python
import enum
import functools
import math

import jax
import jax.numpy as jnp
from jax import lax
from jax.experimental import pallas as pl
from jax.experimental.pallas import tpu as pltpu
from jax.sharding import PartitionSpec as P

HEADS = 12
EPSILON = 1e-12
MESH = pl.DeviceIdType.MESH
bf16 = jnp.bfloat16
f32 = jnp.float32
ALL = slice(None)
MASKED = -1e30
VECTORS = 16
Q_BIAS, V_BIAS, O_BIAS, GAIN_1, SHIFT_1, OUT_BIAS, GAIN_2, SHIFT_2, FF_ROW = range(9)


def contract(left, right, left_dim, right_dim):
    return lax.dot_general(
        left, right, (((left_dim,), (right_dim,)), ((), ())), preferred_element_type=f32
    )


def iota(shape, dim):
    return lax.broadcasted_iota(jnp.int32, shape, dim)


def rounded(v):
    return v.astype(bf16).astype(f32)


class Key(enum.Enum):
    active = 0
    attend_back = 1
    attend_padding = 2
    attend_pairs = 3
    back = 4
    col_sums = 5
    context = 6
    cot = 7
    cotangent = 8
    d_inner = 9
    d_outer = 10
    d_output = 11
    drain = 12
    event = 13
    ff_bias = 14
    ff_sums = 15
    final = 16
    first_back = 17
    first_norm = 18
    frame = 19
    framed = 20
    from_sibling = 21
    g_small = 22
    gain_sum = 23
    grad = 24
    grad_context = 25
    grad_hidden = 26
    grad_hidden_in = 27
    grad_inner = 28
    grad_input = 29
    grad_input_weight = 30
    grad_low = 31
    grad_outer = 32
    grad_output = 33
    hidden = 34
    hidden_in = 35
    hidden_units = 36
    inner = 37
    input = 38
    inverse = 39
    k_active = 40
    k_context = 41
    k_grad = 42
    k_inner = 43
    k_input = 44
    k_inverse = 45
    k_low = 46
    k_norm = 47
    k_other = 48
    k_outer = 49
    k_output = 50
    k_own = 51
    k_packed = 52
    k_pairs = 53
    k_slope = 54
    k_soft = 55
    k_sums = 56
    k_vectors = 57
    keep = 58
    keep_sem = 59
    landed = 60
    lay = 61
    layer_out = 62
    lengths = 63
    load = 64
    loaded = 65
    local_sem = 66
    low = 67
    low_sum = 68
    lower_norm = 69
    m_inner = 70
    m_input = 71
    m_outer = 72
    m_output = 73
    norm = 74
    other = 75
    out_sem = 76
    outer = 77
    output = 78
    own = 79
    packed = 80
    pairs = 81
    pairs_other = 82
    piece_recv = 83
    piece_send = 84
    project_other = 85
    project_own = 86
    put = 87
    return_other = 88
    row_recv = 89
    row_send = 90
    save = 91
    second_norm = 92
    send = 93
    shift_sum = 94
    slope = 95
    soft = 96
    sums = 97
    swap_recv = 98
    swap_send = 99
    swapped = 100
    table = 101
    table_in = 102
    table_recv = 103
    table_send = 104
    token_sums = 105
    total = 106
    vector = 107
    vectors = 108
    w_inner = 109
    w_input = 110
    w_outer = 111
    w_output = 112


def attributes(refs):
    return {key.name: ref for key, ref in refs.items() if isinstance(key, Key)}


class Place:
    def __init__(self, rows):
        self.nz = rows // 4
        r = lax.axis_index("rows")
        self.x = lax.axis_index("pair")
        self.z = r // 4
        self.y = (r // 2) % 2
        self.c = r % 2
        self.index = self.x * rows + r
        self.own = {"X": self.x, "Z": self.z, "Y": self.y}

    def device(self, **other):
        at = {"X": self.x, "Z": self.z, "Y": self.y, "C": self.c, **other}
        return {"pair": at["X"], "rows": (at["Z"] * 2 + at["Y"]) * 2 + at["C"]}

    def peers(self, dim):
        if dim == "Z":
            return [(self.z + k) % self.nz for k in range(1, self.nz)]
        return [1 - self.own[dim]]

    def sources(self, dim):
        if dim == "Z":
            return [(self.z + self.nz - k) % self.nz for k in range(1, self.nz)]
        return [1 - self.own[dim]]

    def first_slot(self, dim):
        return {"X": 0, "Y": 1, "Z": 2}[dim]

    def slots(self):
        return self.nz + 1


def slab(buf, place, gathered, at, rows, cols):
    own = {**place.own, **at}
    lead = tuple(ALL if d in gathered else own[d] for d in "XZY")
    return buf.at[lead + (rows, cols)]


class Gather:
    def __init__(self, buf, place, send, recv, routes, rows, col, width):
        self.buf, self.place, self.send, self.recv, self.routes = buf, place, send, recv, routes
        self.rows, self.col, self.width = rows, col, width
        self.half = buf.shape[-1] // 2

    def cols(self, core):
        return pl.ds(pl.multiple_of(core * self.half + self.col, 128), self.width)

    def per_core(self, act):
        if self.routes[0] == self.routes[1]:
            act(self.routes[0])
            return
        for core in range(2):
            pl.when(self.place.c == core)(functools.partial(act, self.routes[core]))

    def copy(self, view, slot, device):
        return pltpu.make_async_remote_copy(
            src_ref=view,
            dst_ref=view,
            send_sem=self.send.at[slot],
            recv_sem=self.recv.at[slot],
            device_id=device,
            device_id_type=MESH,
        )

    def sends(self, route, stage):
        dim, gathered = route[stage], route[:stage]
        view = slab(self.buf, self.place, gathered, {}, self.rows, self.cols(self.place.c))
        first = self.place.first_slot(dim)
        return [
            self.copy(view, first + k, self.place.device(**{dim: peer}))
            for k, peer in enumerate(self.place.peers(dim))
        ]

    def arrivals(self, route, stage, core):
        dim, gathered = route[stage], route[:stage]
        return [
            slab(self.buf, self.place, gathered, {dim: peer}, self.rows, self.cols(core))
            for peer in self.place.sources(dim)
        ]

    def hand_ons(self, route, stage, core):
        device = self.place.device(C=1 - self.place.c)
        base = self.place.slots()
        if stage == 0:
            view = slab(self.buf, self.place, route[:1], {}, self.rows, self.cols(core))
            return [self.copy(view, base, device)]
        first = base + 1 + (stage - 1) * (self.place.nz - 1)
        return [
            self.copy(view, first + k, device)
            for k, view in enumerate(self.arrivals(route, stage, core))
        ]

    def start(self, stage):
        def act(route):
            for copy in self.sends(route, stage):
                copy.start()

        self.per_core(act)

    def arrived(self, stage):
        def act(route):
            dim = route[stage]
            first = self.place.first_slot(dim)
            device = self.place.device()
            for k, view in enumerate(self.arrivals(route, stage, self.place.c)):
                self.copy(view, first + k, device).wait_recv()
            if stage < 2:
                for copy in self.sends(route, stage + 1):
                    copy.start()
            for copy in self.hand_ons(route, stage, self.place.c):
                copy.start()

        self.per_core(act)

    def event(self, number):
        if number == 0:
            self.start(0)
        elif number < 4:
            self.arrived(number - 1)
        else:
            self.complete()

    def complete(self):
        def other(route):
            for stage in range(3):
                for copy in self.hand_ons(route, stage, 1 - self.place.c):
                    copy.wait_recv()

        if self.routes[0] == self.routes[1]:
            other(self.routes[0])
        else:
            for core in range(2):
                pl.when(self.place.c == 1 - core)(functools.partial(other, self.routes[core]))

    def drain(self):
        def act(route):
            for stage in range(3):
                for copy in self.sends(route, stage) + self.hand_ons(route, stage, self.place.c):
                    copy.wait_send()

        self.per_core(act)


def greet(place, devices):
    barrier = pltpu.get_barrier_semaphore()
    for device in devices:
        pl.semaphore_signal(barrier, inc=1, device_id=device, device_id_type=MESH)
    pl.semaphore_wait(barrier, len(devices))


class Totals:
    def __init__(self, place, table, landed, send, recv):
        self.place, self.table, self.landed, self.send, self.recv = place, table, landed, send, recv
        x, y = 1 - place.x, 1 - place.y
        self.steps = [
            [place.device(C=1 - place.c)],
            [place.device(X=x), place.device(Y=y), place.device(X=x, Y=y)],
            [place.device(Z=peer) for peer in place.peers("Z")],
        ]

    def copies(self, step):
        first = sum(len(found) for found in self.steps[:step])
        return [
            pltpu.make_async_remote_copy(
                src_ref=self.table.at[step],
                dst_ref=self.landed.at[first + k],
                send_sem=self.send.at[first + k],
                recv_sem=self.recv.at[first + k],
                device_id=device,
                device_id_type=MESH,
            )
            for k, device in enumerate(self.steps[step])
        ]

    def start(self, step):
        for copy in self.copies(step):
            copy.start()

    def advance(self, step):
        first = sum(len(found) for found in self.steps[:step])
        total = self.table[step]
        for k, copy in enumerate(self.copies(step)):
            copy.wait_recv()
            total = total + self.landed[first + k]
        self.table[step + 1] = total
        if step + 1 < len(self.steps):
            self.start(step + 1)

    def drain(self):
        for step in range(len(self.steps)):
            for copy in self.copies(step):
                copy.wait_send()


def neighbours(place):
    x, y = 1 - place.x, 1 - place.y
    found = [place.device(C=1 - place.c), place.device(X=x), place.device(Y=y), place.device(X=x, Y=y)]
    return found + [place.device(Z=peer) for peer in place.peers("Z")]


def source_slots(slots, sizes, most):
    frame, offset = slots // most, slots % most
    total = sum(sizes[1:], sizes[0])
    found, start = slots, jnp.int32(0)
    for p, size in enumerate(sizes):
        mine = jnp.where(offset < size, start + offset, total + slots - (start + size))
        found = jnp.where(frame == p, mine, found)
        start = start + size
    return found


def holds_token(slots, sizes, most):
    frame, offset = slots // most, slots % most
    held = jnp.zeros(slots.shape, f32)
    for p, size in enumerate(sizes):
        held = jnp.where((frame == p) & (offset < size), 1.0, held)
    return held


def into_frames(sizes, slots, most):
    source = source_slots(iota((slots, 1), 0), sizes, most)
    return (iota((slots, slots), 1) == source).astype(f32).astype(bf16)


def out_of_frames(sizes, slots, most):
    source = source_slots(iota((1, slots), 1), sizes, most)
    return (iota((slots, slots), 0) == source).astype(f32).astype(bf16)


def folded(v):
    return jnp.sum(v.reshape(v.shape[0] // 8, 8, v.shape[1]), axis=0)


def spread_heads(tokens, span):
    shape = (4 * tokens, span)
    return iota(shape, 0) // tokens == iota(shape, 1) // (span // 4)


def block_rows(i, size):
    return pl.ds(pl.multiple_of(i * size, size), size)


class Forward:
    def __init__(self, refs, place, sizes):
        self.__dict__.update(attributes(refs))
        self.place = place
        self.rows, self.slots, self.width, self.pairs = sizes
        self.most = self.slots // self.pairs
        self.half = place.x
        self.bias_rows = self.ff_bias.shape[1] // self.width
        self.scale = (self.width // HEADS) ** (-0.5)

    def sizes_of(self, row, half):
        return [self.lengths[row, half, p] for p in range(self.pairs)]

    def row(self, r):
        return pl.ds(r * self.slots, self.slots)

    def vector(self, at, count=1):
        found = rounded(self.vectors[at : at + count, :])
        return found if count == 1 else found.reshape(1, count * self.width)

    def frame_hidden(self, r):
        frames = into_frames(self.sizes_of(r, self.half), self.slots, self.most)
        self.own[self.row(r), :] = contract(frames, self.hidden[self.row(r), :], 1, 0).astype(bf16)

    def frame_cotangent(self, r):
        sizes = self.sizes_of(r, self.half)
        frames = into_frames(sizes, self.slots, self.most)
        held = holds_token(iota((self.slots, 1), 0), sizes, self.most)
        moved = contract(frames, self.cot[self.row(r), :], 1, 0) * held
        self.cot[self.row(r), :] = moved.astype(bf16)

    def project_own(self, part):
        cols = slice(part * self.width, (part + 1) * self.width)
        weight = self.w_input[:, :, :, :, cols].reshape(self.width, self.width)
        acc = contract(self.own[...], weight, 1, 0)
        if part == 0:
            acc = acc + self.vector(Q_BIAS)
        if part == 2:
            acc = acc + self.vector(V_BIAS)
        self.packed[:, cols] = acc.astype(bf16)

    def project_other(self, r, part):
        cols = slice(part * self.width, (part + 1) * self.width)
        from_cols = slice((part + 1) * self.width, (part + 2) * self.width)
        weight = self.w_input[:, :, :, :, from_cols].reshape(self.width, self.width)
        acc = contract(self.other[self.row(r), :], weight, 1, 0)
        if part == 1:
            acc = acc + self.vector(V_BIAS)
        self.pairs_other[self.row(r), cols] = acc.astype(bf16)

    def attend_pairs(self, r, together=2):
        most, span, wide = self.most, 4 * (self.width // HEADS), 2 * self.most
        spread = spread_heads(wide, span)
        key, query = iota((2 * wide, 4 * wide), 0), iota((2 * wide, 4 * wide), 1)
        key_frame, same = key % wide // most, key % wide // most == query % wide // most
        slot = key % most

        def two_pairs(pair):
            rows = pl.ds(pl.multiple_of(r * self.slots + pair * wide, wide), wide)
            counts = [self.lengths[r, half, 2 * pair + k] for half in (self.half, 1 - self.half) for k in range(2)]
            mine = jnp.where(key_frame == 0, counts[0], counts[1])
            theirs = jnp.where(key_frame == 0, counts[2], counts[3])
            allowed = same & (slot < jnp.where(key < wide, mine, theirs))
            for at in range(0, self.width, span):
                queries = self.packed[rows, at : at + span]
                keys = jnp.concatenate(
                    [
                        self.packed[rows, self.width + at : self.width + at + span],
                        self.pairs_other[rows, at : at + span],
                    ],
                    axis=0,
                )
                values = jnp.concatenate(
                    [
                        self.packed[rows, 2 * self.width + at : 2 * self.width + at + span],
                        self.pairs_other[rows, self.width + at : self.width + at + span],
                    ],
                    axis=0,
                )
                tiled = jnp.where(spread, jnp.concatenate([queries] * 4, axis=0), 0).astype(bf16)
                scores = jnp.where(allowed, contract(keys, tiled, 1, 1) * self.scale, MASKED)
                raw = jnp.exp(scores - jnp.max(scores, axis=0, keepdims=True))
                soft = raw * (1.0 / jnp.sum(raw, axis=0, keepdims=True))
                kept = [soft[k * most : (k + 1) * most] + soft[(k + 1) * most : (k + 2) * most] for k in (0, 2)]
                self.soft[rows, at : at + span] = jnp.concatenate(kept, axis=0).astype(bf16)
                mixed = contract(soft.astype(bf16), values, 0, 0)
                mixed = jnp.where(spread, mixed, 0.0)
                context = sum(mixed[h * wide : (h + 1) * wide, :] for h in range(4))
                self.context[rows, at : at + span] = context.astype(bf16)

        @pl.loop(0, self.pairs // (2 * together))
        def _(several):
            for k in range(together):
                two_pairs(several * together + k)

    def attend_padding(self, r, together=3):
        sizes = self.sizes_of(r, self.half)
        head = self.width // HEADS
        held_key = holds_token(iota((1, self.slots), 1), sizes, self.most)
        held_query = holds_token(iota((self.slots, 1), 0), sizes, self.most)
        pad_key = jnp.broadcast_to(held_key, (2 * self.slots, self.slots)) < 0.5
        pad_query = jnp.broadcast_to(held_query, (self.slots, 2 * head)) < 0.5
        left = iota((self.slots, 2 * head), 1) < head
        rows = self.row(r)

        def two_heads(pair):
            at = pl.multiple_of(pair * 2 * head, 2 * head)
            queries = self.packed[rows, pl.ds(at, 2 * head)] * self.scale
            keys = self.packed[rows, pl.ds(pl.multiple_of(self.width + at, 2 * head), 2 * head)]
            values = self.packed[rows, pl.ds(pl.multiple_of(2 * self.width + at, 2 * head), 2 * head)]
            both = jnp.concatenate([jnp.where(left, queries, 0), jnp.where(left, 0, queries)], axis=0)
            scores = jnp.where(pad_key, contract(both.astype(bf16), keys, 1, 1), MASKED)
            raw = jnp.exp(scores - jnp.max(scores, axis=1, keepdims=True))
            total = jnp.sum(raw, axis=1, keepdims=True)
            found = contract(raw.astype(bf16), values, 1, 0) * (1.0 / total)
            padded = jnp.where(left, found[: self.slots], found[self.slots :]).astype(bf16)
            cols = pl.ds(at, 2 * head)
            self.context[rows, cols] = jnp.where(pad_query, padded, self.context[rows, cols])

        @pl.loop(0, HEADS // 2 // together)
        def _(several):
            for k in range(together):
                two_heads(several * together + k)

    def first_norm(self, r):
        rows = self.row(r)
        weight = self.w_output[...].reshape(self.width, self.width)
        self.sums[...] = contract(self.context[rows, :], weight, 1, 0)
        bias, gain, shift = self.vector(O_BIAS), self.vector(GAIN_1), self.vector(SHIFT_1)
        size = 32

        @pl.loop(0, self.slots // size, unroll=4)
        def _(i):
            here = block_rows(i, size)
            there = pl.ds(pl.multiple_of(r * self.slots + i * size, size), size)
            total = self.own[there, :].astype(f32) + self.sums[here, :] + bias
            centered = total - jnp.mean(total, axis=1, keepdims=True)
            inverse = lax.rsqrt(jnp.mean(centered * centered, axis=1, keepdims=True) + EPSILON)
            norm = centered * inverse
            self.norm[there, :] = norm
            self.inverse[there, :] = jnp.broadcast_to(inverse, (size, 128))
            self.low[there, :] = (norm * gain + shift).astype(bf16)

    def hidden_units(self, first, count, size=256):
        @pl.loop(first, first + count)
        def _(n):
            cols = pl.ds(pl.multiple_of(n * size, size), size)
            weight = self.w_inner[:, :, :, :, cols].reshape(self.width, size)
            bias = rounded(self.ff_bias[:, cols])
            for r in range(self.rows):
                inner = contract(self.low[self.row(r), :], weight, 1, 0) + bias
                share = 0.5 * (1.0 + lax.erf(inner * (0.5**0.5)))
                slope = share + inner * (jnp.exp(-0.5 * inner * inner) * ((2.0 * math.pi) ** -0.5))
                self.active[self.row(r), cols] = (inner * share).astype(bf16)
                self.slope[self.row(r), cols] = slope.astype(bf16)

    def second_norm(self, r):
        rows = self.row(r)
        weight = self.w_outer[...].reshape(self.w_inner.shape[-1], self.width)
        self.sums[...] = contract(self.active[rows, :], weight, 1, 0)
        gain_1, shift_1 = self.vector(GAIN_1), self.vector(SHIFT_1)
        bias, gain, shift = self.vector(OUT_BIAS), self.vector(GAIN_2), self.vector(SHIFT_2)
        size = 32

        @pl.loop(0, self.slots // size, unroll=4)
        def _(i):
            here = block_rows(i, size)
            there = pl.ds(pl.multiple_of(r * self.slots + i * size, size), size)
            total = (self.norm[there, :] * gain_1 + shift_1) + self.sums[here, :] + bias
            centered = total - jnp.mean(total, axis=1, keepdims=True)
            inverse = lax.rsqrt(jnp.mean(centered * centered, axis=1, keepdims=True) + EPSILON)
            norm = centered * inverse
            self.framed[here, :] = (norm * gain + shift).astype(bf16)
            upstream = self.cot[there, :].astype(f32)
            self.gain_sum[...] += folded(upstream * norm)
            self.shift_sum[...] += folded(upstream)
            incoming = upstream * gain
            plain = jnp.mean(incoming, axis=1, keepdims=True)
            along = jnp.mean(incoming * norm, axis=1, keepdims=True)
            grad = inverse * (incoming - plain - norm * along)
            low = grad.astype(bf16)
            self.grad[there, :] = grad
            self.grad_low[there, :] = low
            self.low_sum[...] += folded(low.astype(f32))

        back = out_of_frames(self.sizes_of(r, self.half), self.slots, self.most)
        self.hidden[rows, :] = contract(back, self.framed[...], 1, 0).astype(bf16)


FORWARD_VMEM = 61 * 2**20
ORDER = None


def forward_kernel(names, fast, sizes, routes, plan, *refs):
    refs = dict(zip(names, refs, strict=True))
    rows, slots, width, pairs = sizes
    place = Place(lax.axis_size("rows"))
    run = Forward(refs, place, sizes)
    sibling = place.device(C=1 - place.c)
    partner = place.device(X=1 - place.x)

    def local(src, dst, slot):
        return pltpu.make_async_copy(src, dst, run.local_sem.at[slot])

    load_hidden = local(run.hidden_in, run.hidden, 0)
    load_cot = local(run.cotangent, run.cot, 1)
    load_hidden.start()
    load_cot.start()

    if fast:
        greet(place, neighbours(place))
    else:
        greet(place, [partner])

    def hidden_copy(r):
        view = pl.ds(r * slots, slots)
        return pltpu.make_async_remote_copy(
            src_ref=run.own.at[view],
            dst_ref=run.other.at[view],
            send_sem=run.row_send.at[r],
            recv_sem=run.row_recv.at[r],
            device_id=partner,
            device_id_type=MESH,
        )

    weights = [Key.w_input, Key.w_output, Key.w_inner, Key.w_outer]
    masters = [Key.m_input, Key.m_output, Key.m_inner, Key.m_outer]
    gathers = {}
    drains = []
    if fast:
        totals = Totals(place, run.table, run.table_in, run.table_send, run.table_recv)
        for k, (weight, master) in enumerate(zip(weights, masters, strict=True)):
            buf = refs[weight]
            half = buf.shape[-1] // 2
            for j, (route, (row, count), (col, span)) in enumerate(routes.get(weight, ())):
                piece = Gather(
                    buf, place, run.piece_send.at[len(gathers)], run.piece_recv.at[len(gathers)],
                    route, pl.ds(row, count), col, span,
                )
                gathers[weight, j] = piece

        def swap(k):
            master = refs[masters[k]]
            half = master.shape[-1] // 2
            theirs = pl.ds(pl.multiple_of((1 - place.c) * half, 128), half)
            return pltpu.make_async_remote_copy(
                src_ref=master.at[:, theirs],
                dst_ref=refs[Key.from_sibling, k],
                send_sem=run.swap_send.at[k],
                recv_sem=run.swap_recv.at[k],
                device_id=sibling,
                device_id_type=MESH,
            )

        def lay(k):
            swap(k).wait_recv()
            master, buf = refs[masters[k]], refs[weights[k]]
            half = master.shape[-1] // 2
            cols = pl.ds(pl.multiple_of(place.c * half, 128), half)
            mine, theirs = master[:, cols], refs[Key.from_sibling, k][...]
            first = place.c == 0
            both = jnp.concatenate([jnp.where(first, mine, theirs), jnp.where(first, theirs, mine)], axis=0)
            buf[place.x, place.z, place.y, :, cols] = both.astype(bf16)

        for k in range(4):
            swap(k).start()
        run.table[0] = jnp.zeros((VECTORS, width), f32)
        for k in range(9):
            share = refs[Key.vector, k]
            run.table[0, k : k + 1, 0 : share.shape[1]] = share[...]
        piece = refs[Key.vector, 0].shape[1]
        wide = refs[Key.vector, 8].shape[1]
        per_row = width // wide
        upper = pltpu.roll(run.table[0, 0:8, :], place.index * piece, axis=1)
        lower = pltpu.roll(run.table[0, 8:16, :], (place.index % per_row) * wide, axis=1)
        lower = jnp.broadcast_to(lower[:1, :], (8, width))
        lower = jnp.where(iota((8, width), 0) == place.index // per_row, lower, 0.0)
        run.table[0, 0:8, :] = upper
        run.table[0, 8:16, :] = lower
        totals.start(0)

    def spread_vectors(table):
        run.vectors[...] = table
        for k in range(run.bias_rows):
            run.ff_bias[:, k * width : (k + 1) * width] = table[FF_ROW + k : FF_ROW + k + 1, :]

    if not fast:
        for k, weight in enumerate(weights):
            local(refs[masters[k]], refs[weight], 2 + k).start()
        spread_vectors(refs[Key.vector, 0][...])

    saved = [
        (Key.k_input, Key.w_input), (Key.k_output, Key.w_output), (Key.k_inner, Key.w_inner), (Key.k_outer, Key.w_outer),
        (Key.k_own, Key.own), (Key.k_other, Key.other), (Key.k_packed, Key.packed), (Key.k_pairs, Key.pairs_other),
        (Key.k_soft, Key.soft), (Key.k_context, Key.context), (Key.k_norm, Key.norm), (Key.k_inverse, Key.inverse),
        (Key.k_active, Key.active), (Key.k_slope, Key.slope), (Key.k_grad, Key.grad), (Key.k_vectors, Key.vectors), (Key.k_low, Key.grad_low),
        (Key.layer_out, Key.hidden),
    ]
    saves = {name: local(refs[src], refs[name], 6 + k) for k, (name, src) in enumerate(saved) if name in refs}
    started = []
    sent = []

    def save(name):
        if name in saves:
            saves[name].start()
            started.append(name)

    def step(what, *detail):
        if what == Key.event:
            if fast:
                gathers[detail[0], detail[1]].event(detail[2])
        elif what == Key.lay:
            if fast:
                lay(detail[0])
        elif what == Key.total:
            if fast:
                totals.advance(detail[0])
                if detail[0] + 1 == len(totals.steps):
                    spread_vectors(run.table[detail[0] + 1])
        elif what == Key.loaded:
            if not fast:
                k = weights.index(detail[0])
                local(refs[masters[k]], refs[detail[0]], 2 + k).wait()
        elif what == Key.frame:
            if detail[0] == 0:
                load_hidden.wait()
            run.frame_hidden(detail[0])
        elif what == Key.send:
            hidden_copy(detail[0]).start()
            sent.append(detail[0])
        elif what == Key.other:
            hidden_copy(detail[0]).wait_recv()
        elif what == Key.cot:
            if detail[0] == 0:
                load_cot.wait()
            run.frame_cotangent(detail[0])
        elif what == Key.save:
            save(detail[0])
        else:
            getattr(run, what.name)(*detail)

    run.gain_sum[...] = jnp.zeros_like(run.gain_sum)
    run.shift_sum[...] = jnp.zeros_like(run.shift_sum)
    run.low_sum[...] = jnp.zeros_like(run.low_sum)
    for entry in plan:
        step(*entry)
    run.k_sums[0:8, :] = run.gain_sum[...]
    run.k_sums[8:16, :] = run.shift_sum[...]
    run.k_sums[16:24, :] = run.low_sum[...]
    for r in sent:
        hidden_copy(r).wait_send()
    if fast:
        for gather in gathers.values():
            gather.drain()
        for k in range(4):
            swap(k).wait_send()
        totals.drain()
    for name in started:
        saves[name].wait()


def forward_plan(rows, units):
    plan = []
    for r in range(rows):
        plan += [(Key.frame, r), (Key.send, r)]
    for k in range(4):
        plan += [(Key.lay, k)]
    for n in range(5):
        plan += [(Key.total, n)]
    for r in range(rows):
        plan += [(Key.cot, r)]
    for w in (Key.w_input, Key.w_output, Key.w_inner, Key.w_outer):
        for e in range(5):
            plan += [(Key.event, w, 0, e)]
        plan += [(Key.loaded, w)]
    for part in range(3):
        plan += [(Key.project_own, part)]
    for r in range(rows):
        plan += [(Key.other, r), (Key.project_other, r, 0), (Key.project_other, r, 1)]
        plan += [(Key.attend_pairs, r), (Key.attend_padding, r), (Key.first_norm, r)]
    plan += [(Key.hidden_units, 0, units)]
    for r in range(rows):
        plan += [(Key.second_norm, r)]
    for name in (Key.layer_out, Key.k_input, Key.k_output, Key.k_inner, Key.k_outer, Key.k_own, Key.k_other, Key.k_packed, Key.k_pairs,
                 Key.k_soft, Key.k_context, Key.k_norm, Key.k_inverse, Key.k_active, Key.k_slope, Key.k_grad, Key.k_vectors):
        plan += [(Key.save, name)]
    return plan


def forward_call(mesh_rows, fast, hidden, cot, masters, small, lengths, routes, plan, with_saves=True):
    rows, slots, width = hidden.shape
    pairs = lengths.shape[2]
    tokens = rows * slots
    units = masters[2].shape[1]
    nz = mesh_rows // 4
    tall = [width, width, width, units]
    wide = [3 * width, width, units, width]
    if fast:
        shapes = [(2, nz, 2, tall[k] // (4 * nz), wide[k]) for k in range(4)]
    else:
        shapes = [(1, 1, 1, tall[k], wide[k]) for k in range(4)]
    weights = [Key.w_input, Key.w_output, Key.w_inner, Key.w_outer]
    ins = [Key.hidden_in, Key.cotangent, Key.m_input, Key.m_output, Key.m_inner, Key.m_outer]
    ins += [(Key.vector, k) for k in range(len(small))] + [Key.lengths]
    hbm, vmem, smem = (pl.BlockSpec(memory_space=s) for s in (pl.ANY, pltpu.VMEM, pltpu.SMEM))
    if fast:
        args = [hidden.reshape(tokens, width), cot.reshape(tokens, width), *masters, *small, lengths]
    else:
        args = [hidden.reshape(tokens, width), cot.reshape(tokens, width)]
        args += [m.reshape(s) for m, s in zip(masters, shapes, strict=True)] + [*small, lengths]
    in_specs = [hbm, hbm] + [vmem if fast else hbm] * 4 + [vmem] * len(small) + [smem]
    outs = {Key.layer_out: ((tokens, width), bf16), Key.k_sums: ((24, width), f32)}
    saved = {
        Key.k_input: (shapes[0], bf16), Key.k_output: (shapes[1], bf16), Key.k_inner: (shapes[2], bf16),
        Key.k_outer: (shapes[3], bf16), Key.k_own: ((tokens, width), bf16), Key.k_other: ((tokens, width), bf16),
        Key.k_packed: ((tokens, 3 * width), bf16), Key.k_pairs: ((tokens, 2 * width), bf16),
        Key.k_soft: ((tokens, width), bf16), Key.k_context: ((tokens, width), bf16),
        Key.k_norm: ((tokens, width), f32), Key.k_inverse: ((tokens, 128), f32),
        Key.k_active: ((tokens, units), bf16), Key.k_slope: ((tokens, units), bf16),
        Key.k_grad: ((tokens, width), f32), Key.k_low: ((tokens, width), bf16), Key.k_vectors: ((VECTORS, width), f32),
    }
    if with_saves:
        outs.update(saved)
    out_specs = [vmem if name == Key.k_sums else hbm for name in outs]
    scratch = {
        Key.w_input: pltpu.VMEM(shapes[0], bf16), Key.w_output: pltpu.VMEM(shapes[1], bf16),
        Key.w_inner: pltpu.VMEM(shapes[2], bf16), Key.w_outer: pltpu.VMEM(shapes[3], bf16),
        Key.hidden: pltpu.VMEM((tokens, width), bf16), Key.cot: pltpu.VMEM((tokens, width), bf16),
        Key.own: pltpu.VMEM((tokens, width), bf16), Key.other: pltpu.VMEM((tokens, width), bf16),
        Key.packed: pltpu.VMEM((tokens, 3 * width), bf16), Key.pairs_other: pltpu.VMEM((tokens, 2 * width), bf16),
        Key.context: pltpu.VMEM((tokens, width), bf16), Key.soft: pltpu.VMEM((tokens, width), bf16),
        Key.norm: pltpu.VMEM((tokens, width), f32), Key.inverse: pltpu.VMEM((tokens, 128), f32),
        Key.low: pltpu.VMEM((tokens, width), bf16), Key.active: pltpu.VMEM((tokens, units), bf16),
        Key.slope: pltpu.VMEM((tokens, units), bf16), Key.grad: pltpu.VMEM((tokens, width), f32),
        Key.sums: pltpu.VMEM((slots, width), f32), Key.framed: pltpu.VMEM((slots, width), bf16),
        Key.vectors: pltpu.VMEM((VECTORS, width), f32), Key.ff_bias: pltpu.VMEM((1, units), f32),
        Key.gain_sum: pltpu.VMEM((8, width), f32), Key.shift_sum: pltpu.VMEM((8, width), f32),
        Key.low_sum: pltpu.VMEM((8, width), f32), Key.grad_low: pltpu.VMEM((tokens, width), bf16),
        Key.local_sem: pltpu.SemaphoreType.DMA((6 + len(saved) + 1,)),
        Key.row_send: pltpu.SemaphoreType.DMA((rows,)), Key.row_recv: pltpu.SemaphoreType.DMA((rows,)),
    }
    if fast:
        steps, partners = 3, nz + 3
        pieces = sum(len(v) for v in routes.values())
        slots_each = nz + 1 + 1 + 2 * (nz - 1)
        scratch.update({
            Key.table: pltpu.VMEM((steps + 1, VECTORS, width), f32), Key.table_in: pltpu.VMEM((partners, VECTORS, width), f32),
            Key.table_send: pltpu.SemaphoreType.DMA((partners,)), Key.table_recv: pltpu.SemaphoreType.DMA((partners,)),
            Key.piece_send: pltpu.SemaphoreType.DMA((pieces, slots_each)),
            Key.piece_recv: pltpu.SemaphoreType.DMA((pieces, slots_each)),
            Key.swap_send: pltpu.SemaphoreType.DMA((4,)), Key.swap_recv: pltpu.SemaphoreType.DMA((4,)),
        })
        for k in range(4):
            scratch[Key.from_sibling, k] = pltpu.VMEM((masters[k].shape[0], wide[k] // 2), f32)
    names = ins + list(outs) + list(scratch)
    sizes = (rows, slots, width, pairs)
    body = functools.partial(forward_kernel, names, fast, sizes, routes, plan)
    found = pl.pallas_call(
        body,
        out_shape=[jax.ShapeDtypeStruct(*s) for s in outs.values()],
        in_specs=in_specs,
        out_specs=out_specs,
        scratch_shapes=list(scratch.values()),
        compiler_params=pltpu.CompilerParams(
            collective_id=0, has_side_effects=True, vmem_limit_bytes=FORWARD_VMEM
        ),
        name="forward",
    )(*args)
    return dict(zip(outs, found, strict=True))


class Scatter:
    def __init__(self, buf, place, swapped, landed, final, out, send, recv, routes, starts, width):
        self.buf, self.place, self.swapped, self.landed = buf, place, swapped, landed
        self.final, self.out, self.send, self.recv, self.routes = final, out, send, recv, routes
        self.starts, self.width = starts, width
        self.sizes = dict(zip("XZY", buf.shape[:3], strict=True))
        self.core_rows = buf.shape[3] // 2

    def cols(self, core):
        first, second = self.starts
        return pl.ds(pl.multiple_of(first + core * (second - first), 128), self.width)

    def remote(self, src, dst, slot, device):
        return pltpu.make_async_remote_copy(
            src_ref=src,
            dst_ref=dst,
            send_sem=self.send.at[slot],
            recv_sem=self.recv.at[slot],
            device_id=device,
            device_id_type=MESH,
        )

    def per_core(self, act):
        if self.routes[0] == self.routes[1]:
            act(self.routes[0])
            return
        for core in range(2):
            pl.when(self.place.c == core)(functools.partial(act, self.routes[core]))

    def lead(self, route, stage, at):
        own = {**self.place.own, **at}
        fixed = route[: stage + 1]
        return tuple(own[d] if d in fixed else ALL for d in "XZY")

    def swap(self):
        place = self.place
        src = self.buf.at[ALL, ALL, ALL, ALL, self.cols(1 - place.c)]
        return self.remote(src, self.swapped, 0, place.device(C=1 - place.c))

    def sends(self, route, stage):
        dim = route[stage]
        mine = self.landed.at[self.lead(route, stage, {})]
        found = []
        for k, peer in enumerate(self.place.peers(dim)):
            src = self.buf.at[self.lead(route, stage, {dim: peer}) + (ALL, self.cols(self.place.c))]
            found.append(self.remote(src, mine, 1 + self.place.first_slot(dim) + k, self.place.device(**{dim: peer})))
        return found

    def arrivals(self, route, stage):
        dim = route[stage]
        found = []
        for k, peer in enumerate(self.place.sources(dim)):
            view = self.landed.at[self.lead(route, stage, {dim: peer})]
            found.append(self.remote(view, view, 1 + self.place.first_slot(dim) + k, self.place.device()))
        return found

    def blocks(self, free, body):
        total = math.prod(self.sizes[d] for d in free)

        def visit(i):
            at = dict(self.place.own)
            for d in reversed(free):
                at[d] = i % self.sizes[d]
                i = i // self.sizes[d]
            body((at["X"], at["Z"], at["Y"]), at)

        if total == 1:
            visit(0)
        else:
            pl.loop(0, total)(visit)

    def start_swap(self):
        self.swap().start()

    def add_swapped(self):
        self.swap().wait_recv()
        cols = self.cols(self.place.c)

        def body(block, at):
            there = block + (ALL, cols)
            total = self.buf[there].astype(f32) + self.swapped[block].astype(f32)
            self.buf[there] = total.astype(bf16)

        self.blocks("XZY", body)

        def act(route):
            for copy in self.sends(route, 0):
                copy.start()

        self.per_core(act)

    def add_stage(self, stage):
        cols = self.cols(self.place.c)

        def act(route):
            dim = route[stage]
            for copy in self.arrivals(route, stage):
                copy.wait_recv()
            sources = self.place.sources(dim)

            def body(block, at):
                total = self.buf[block + (ALL, cols)].astype(f32)
                for peer in sources:
                    theirs = {**at, dim: peer}
                    total = total + self.landed[theirs["X"], theirs["Z"], theirs["Y"]].astype(f32)
                if stage < 2:
                    self.buf[block + (ALL, cols)] = total.astype(bf16)
                else:
                    self.final[...] = total

            self.blocks("".join(d for d in "XZY" if d not in route[: stage + 1]), body)
            if stage < 2:
                for copy in self.sends(route, stage + 1):
                    copy.start()

        self.per_core(act)
        if stage == 2:
            for copy in self.hand_over():
                copy.start()

    def hand_over(self):
        place, count = self.place, self.core_rows
        cols = self.cols(place.c)
        mine = self.final.at[pl.ds(pl.multiple_of(place.c * count, 8), count)]
        theirs = self.final.at[pl.ds(pl.multiple_of((1 - place.c) * count, 8), count)]
        there = self.remote(theirs, self.out.at[:, cols], 1 + place.slots(), place.device(C=1 - place.c))
        here = pltpu.make_async_copy(mine, self.out.at[:, cols], self.send.at[2 + place.slots()])
        return [there, here]

    def finish(self):
        there, here = self.hand_over()
        here.wait()
        there.wait_send()
        view = self.out.at[:, self.cols(1 - self.place.c)]
        self.remote(view, view, 1 + self.place.slots(), self.place.device()).wait_recv()

    def drain(self):
        self.swap().wait_send()

        def act(route):
            for stage in range(3):
                for copy in self.sends(route, stage):
                    copy.wait_send()

        self.per_core(act)

    def event(self, number):
        if number == 0:
            self.start_swap()
        elif number == 1:
            self.add_swapped()
        elif number < 5:
            self.add_stage(number - 2)
        else:
            self.finish()


class Backward:
    def __init__(self, refs, place, sizes):
        self.__dict__.update(attributes(refs))
        self.place = place
        self.rows, self.slots, self.width, self.pairs = sizes
        self.most = self.slots // self.pairs
        self.half = place.x
        self.scale = (self.width // HEADS) ** (-0.5)
        self.tokens = self.rows * self.slots
        self.units = self.active.shape[1]

    def sizes_of(self, row, half):
        return [self.lengths[row, half, p] for p in range(self.pairs)]

    def row(self, r):
        return pl.ds(r * self.slots, self.slots)

    def vector(self, at):
        return rounded(self.vectors[at : at + 1, :])

    def lower_norm(self):
        gain, shift = self.vector(GAIN_1), self.vector(SHIFT_1)

        @pl.loop(0, self.tokens // 64)
        def _(i):
            rows = block_rows(i, 64)
            self.low[rows, :] = (self.norm[rows, :] * gain + shift).astype(bf16)

    def grad_outer(self):
        nz = self.d_outer.shape[1]
        parts = self.d_outer.shape[0] * nz
        size = self.units // parts

        @pl.loop(0, parts)
        def _(i):
            found = contract(self.active[:, pl.ds(pl.multiple_of(i * size, 128), size)], self.grad_low[...], 0, 0)
            self.d_outer[i // nz, i % nz] = found.astype(bf16).reshape(self.d_outer.shape[2:])

    def grad_hidden(self, first, count, size=384):
        @pl.loop(first, first + count)
        def _(n):
            cols = pl.ds(pl.multiple_of(n * size, size), size)
            weight = self.w_outer[cols, :]
            total = jnp.zeros((8, size), f32)
            for r in range(self.rows):
                found = contract(self.grad_low[self.row(r), :], weight, 1, 1)
                low = (found * self.slope[self.row(r), cols].astype(f32)).astype(bf16)
                self.slope[self.row(r), cols] = low
                total = total + folded(low.astype(f32))
            self.ff_sums[:, cols] = total

    def grad_inner(self, core, part, size=768):
        half = self.units // 2
        cols = pl.ds(pl.multiple_of(core * half + part * size, 128), size)
        found = contract(self.low[...], self.slope[:, cols], 0, 0).astype(bf16)
        self.d_inner[:, :, :, :, cols] = found.reshape(self.d_inner.shape[:4] + (size,))

    def first_back(self, r):
        rows = self.row(r)
        weight = self.w_inner[...].reshape(self.width, self.units)
        self.sums[...] = contract(self.slope[rows, :], weight, 1, 1)
        gain = self.vector(GAIN_1)
        if isinstance(r, int) and r == 0:
            for at in (GAIN_1, SHIFT_1, O_BIAS):
                self.col_sums[at] = jnp.zeros((8, self.width), f32)

        @pl.loop(0, self.slots // 64)
        def _(i):
            here = block_rows(i, 64)
            there = pl.ds(pl.multiple_of(r * self.slots + i * 64, 64), 64)
            grad = self.grad[there, :] + self.sums[here, :]
            norm = self.norm[there, :]
            self.col_sums[GAIN_1] += folded(grad * norm)
            self.col_sums[SHIFT_1] += folded(grad)
            incoming = grad * gain
            plain = jnp.mean(incoming, axis=1, keepdims=True)
            along = jnp.mean(incoming * norm, axis=1, keepdims=True)
            attn = self.inverse[there, 0:1] * (incoming - plain - norm * along)
            self.grad[there, :] = attn
            low = attn.astype(bf16)
            self.grad_low[there, :] = low
            self.col_sums[O_BIAS] += folded(low.astype(f32))

    def grad_output(self):
        context = self.w_outer[2 * self.tokens : 3 * self.tokens, :]
        found = contract(context, self.grad_low[...], 0, 0).astype(bf16)
        self.d_output[...] = found.reshape(self.d_output.shape)

    def grad_context(self, r):
        rows = self.row(r)
        weight = self.w_output[...].reshape(self.width, self.width)
        self.low[rows, :] = contract(self.grad_low[rows, :], weight, 1, 1).astype(bf16)

    def attend_back(self, r, together=2):
        most, span, width, wide = self.most, 4 * (self.width // HEADS), self.width, 2 * self.most
        spread = spread_heads(wide, span)
        first = iota((most, 4 * wide), 1) % wide < most

        def tiled(v):
            return jnp.where(spread, jnp.concatenate([v] * 4, axis=0), 0).astype(bf16)

        def two_pairs(pair):
            rows = pl.ds(pl.multiple_of(r * self.slots + pair * wide, wide), wide)
            for at in range(0, width, span):
                here = [slice(part * width + at, part * width + at + span) for part in range(4)]
                queries = tiled(self.active[rows, here[0]])
                keys = jnp.concatenate([self.active[rows, here[1]], self.slope[rows, here[0]]], axis=0)
                values = jnp.concatenate([self.active[rows, here[2]], self.slope[rows, here[1]]], axis=0)
                kept = self.active[rows, here[3]].astype(f32)
                mine, theirs = kept[:most], kept[most:]
                soft = jnp.concatenate(
                    [
                        jnp.where(first, mine, 0.0), jnp.where(first, 0.0, mine),
                        jnp.where(first, theirs, 0.0), jnp.where(first, 0.0, theirs),
                    ],
                    axis=0,
                )
                grad = tiled(self.low[rows, here[0]])
                grad_soft = contract(values, grad, 1, 1)
                delta = jnp.sum(soft * grad_soft, axis=0, keepdims=True)
                grad_scores = (soft * (grad_soft - delta)).astype(bf16)
                grad_values = contract(soft.astype(bf16), grad, 1, 0).astype(bf16)
                grad_keys = (contract(grad_scores, queries, 1, 0) * self.scale).astype(bf16)
                mixed = jnp.where(spread, contract(grad_scores, keys, 0, 0), 0.0)
                grad_queries = sum(mixed[h * wide : (h + 1) * wide, :] for h in range(4)) * self.scale
                self.active[rows, here[0]] = grad_queries.astype(bf16)
                self.active[rows, here[1]] = grad_keys[:wide]
                self.active[rows, here[2]] = grad_values[:wide]
                self.slope[rows, here[0]] = grad_keys[wide:]
                self.slope[rows, here[1]] = grad_values[wide:]

        @pl.loop(0, self.pairs // (2 * together))
        def _(several):
            for k in range(together):
                two_pairs(several * together + k)

    def input_weight(self, first, last):
        weight = self.w_inner[:, :, :, :, first:last] if self.fast else self.w_input[:, :, :, :, first:last]
        return weight.reshape(self.width, last - first)

    def return_other(self, r):
        rows = self.row(r)
        weight = self.input_weight(self.width, 3 * self.width)
        self.grad_low[rows, :] = contract(self.slope[rows, : 2 * self.width], weight, 1, 1).astype(bf16)

    def token_sums(self):
        width = self.width
        self.col_sums[Q_BIAS] = jnp.zeros((8, width), f32)
        self.col_sums[V_BIAS] = jnp.zeros((8, width), f32)

        @pl.loop(0, self.tokens // 64)
        def _(i):
            rows = block_rows(i, 64)
            self.col_sums[Q_BIAS] += folded(self.active[rows, :width].astype(f32))
            both = self.active[rows, 2 * width : 3 * width].astype(f32) + self.slope[rows, width : 2 * width].astype(f32)
            self.col_sums[V_BIAS] += folded(both)

        self.col_sums[GAIN_2] = self.k_sums[0:8, :]
        self.col_sums[SHIFT_2] = self.k_sums[8:16, :]
        self.col_sums[OUT_BIAS] = self.k_sums[16:24, :]
        rows = [jnp.sum(self.col_sums[at], axis=0, keepdims=True) for at in range(8)]
        units = jnp.sum(self.ff_sums[...], axis=0, keepdims=True)
        count = self.units // width
        rows += [units[:, k * width : (k + 1) * width] for k in range(count)]
        rows += [jnp.zeros((VECTORS - 8 - count, width), f32)]
        self.table[0] = jnp.concatenate(rows, axis=0)

    def grad_input_weight(self, part):
        width = self.width
        cols = pl.ds(pl.multiple_of(part * width, 128), width)
        target = self.d_inner

        def keep(found):
            target[:, :, :, :, cols] = found.astype(bf16).reshape(target.shape[:4] + (width,))

        if isinstance(part, int) and part == 0:
            keep(contract(self.w_outer[: self.tokens, :], self.active[:, :width], 0, 0))
            return
        there = pl.ds(pl.multiple_of((part - 1) * width, 128), width)
        found = contract(self.w_outer[: self.tokens, :], self.active[:, cols], 0, 0)
        keep(found + contract(self.w_outer[self.tokens : 2 * self.tokens, :], self.slope[:, there], 0, 0))

    def grad_hidden_in(self, r):
        rows = self.row(r)
        found = contract(self.active[rows, : 3 * self.width], self.input_weight(0, 3 * self.width), 1, 1)
        found = found + self.grad[rows, :] + self.back[rows, :].astype(f32)
        high = found.astype(bf16)
        rest = (found - high.astype(f32)).astype(bf16)
        back = out_of_frames(self.sizes_of(r, self.half), self.slots, self.most)
        self.norm[rows, :] = contract(back, high, 1, 0) + contract(back, rest, 1, 0)


BACKWARD_VMEM = 127 * 2**19


def backward_kernel(names, fast, sizes, routes, plan, *refs):
    refs = dict(zip(names, refs, strict=True))
    rows, slots, width, pairs = sizes
    tokens = rows * slots
    place = Place(lax.axis_size("rows"))
    run = Backward(refs, place, sizes)
    run.fast = fast
    partner = place.device(X=1 - place.x)
    in_outer = [run.w_outer.at[pl.ds(k * tokens, tokens)] for k in range(3)]
    loads = {
        Key.grad: (run.k_grad, run.grad), Key.low: (run.k_low, run.grad_low), Key.active: (run.k_active, run.active), Key.outer: (run.k_outer, run.w_outer),
        Key.slope: (run.k_slope, run.slope), Key.norm: (run.k_norm, run.norm), Key.inner: (run.k_inner, run.w_inner),
        Key.inverse: (run.k_inverse, run.inverse), Key.output: (run.k_output, run.w_output),
        Key.vectors: (run.k_vectors, run.vectors),
        Key.packed: (run.k_packed, run.active.at[:, pl.ds(0, 3 * width)]),
        Key.soft: (run.k_soft, run.active.at[:, pl.ds(3 * width, width)]),
        Key.pairs: (run.k_pairs, run.slope.at[:, pl.ds(0, 2 * width)]),
        Key.own: (run.k_own, in_outer[0]), Key.other: (run.k_other, in_outer[1]), Key.context: (run.k_context, in_outer[2]),
        Key.input: (run.k_input, run.w_inner.at[:, :, :, :, pl.ds(0, 3 * width)] if fast else run.w_input),
    }
    order = {name: k for k, name in enumerate(loads)}

    def load(name):
        return pltpu.make_async_copy(*loads[name], run.local_sem.at[order[name]])

    scatters = {}
    for name in (Key.low, Key.active):
        load(name).start()
    if fast:
        greet(place, neighbours(place))
        totals = Totals(place, run.table, run.table_in, run.table_send, run.table_recv)
        targets = {Key.outer: run.d_outer, Key.inner: run.d_inner, Key.output: run.d_output, Key.input: run.d_inner}
        for name, pieces in routes.items():
            for j, (route, starts, span) in enumerate(pieces):
                at = len(scatters)
                scatters[name, j] = Scatter(
                    targets[name], place, refs[Key.swapped, name, j], refs[Key.landed, name, j],
                    refs[Key.final, name, j], refs["g", name], run.piece_send.at[at], run.piece_recv.at[at],
                    route, starts, span,
                )
    else:
        greet(place, [partner])

    def returned(r):
        view = pl.ds(r * slots, slots)
        return pltpu.make_async_remote_copy(
            src_ref=run.grad_low.at[view],
            dst_ref=run.back.at[view],
            send_sem=run.row_send.at[r],
            recv_sem=run.row_recv.at[r],
            device_id=partner,
            device_id_type=MESH,
        )

    def put(r):
        view = pl.ds(r * slots, slots)
        return pltpu.make_async_copy(run.norm.at[view], run.grad_input.at[view], run.out_sem.at[r])

    whole = {Key.outer: Key.d_outer, Key.inner: Key.d_inner, Key.output: Key.d_output, Key.input: Key.d_inner}

    def keep(name):
        src = refs[whole[name]]
        if name == Key.input:
            src = src.at[:, :, :, :, pl.ds(0, 3 * width)]
        return pltpu.make_async_copy(src, refs["g", name], run.keep_sem.at[list(whole).index(name)])

    sent, written, summed = [], [], []

    def step(what, *detail):
        if what == Key.load:
            load(detail[0]).start()
        elif what == Key.loaded:
            load(detail[0]).wait()
        elif what == Key.event:
            if fast:
                scatters[detail[0], detail[1]].event(detail[2])
        elif what == Key.drain:
            if fast:
                for (name, _), scatter in scatters.items():
                    if name == detail[0]:
                        scatter.drain()
            else:
                keep(detail[0]).wait()
        elif what == Key.keep:
            if not fast:
                keep(detail[0]).start()
        elif what == Key.grad_inner:
            core = 1 - place.c if detail[0] == 0 else place.c
            run.grad_inner(core, *detail[1:])
        elif what == Key.grad_input_weight:
            run.grad_input_weight(detail[0])
        elif what == Key.send:
            returned(detail[0]).start()
            sent.append(detail[0])
        elif what == Key.back:
            returned(detail[0]).wait_recv()
        elif what == Key.total:
            if not fast:
                return
            if detail[0] < 0:
                totals.start(0)
                summed.append(True)
            else:
                totals.advance(detail[0])
        elif what == Key.put:
            put(detail[0]).start()
            written.append(detail[0])
        else:
            getattr(run, what.name)(*detail)

    for entry in plan:
        step(*entry)
    for r in sent:
        returned(r).wait_send()
    for r in written:
        put(r).wait()
    if fast:
        if summed: totals.drain()
        table = run.table[len(totals.steps)]
        devices = 2 * lax.axis_size("rows")
        piece = width // devices
        wide = piece * (run.units // width)
        per_row = width // wide
        upper = pltpu.roll(table[:8], (devices - place.index) * piece % width, axis=1)
        lower = jnp.where(iota((8, width), 0) == place.index // per_row, table[8:], 0.0)
        lower = jnp.sum(lower, axis=0, keepdims=True)
        lower = pltpu.roll(jnp.broadcast_to(lower, (8, width)), (per_row - place.index % per_row) * wide % width, axis=1)
        run.g_small[...] = jnp.concatenate([upper[:, :128], lower[:, :128]], axis=0)
    else:
        run.g_small[...] = run.table[0]


def backward_call(mesh_rows, fast, kept, lengths, routes, plan, sizes, units):
    rows, slots, width, pairs = sizes
    tokens = rows * slots
    nz = mesh_rows // 4
    hbm, vmem, smem = (pl.BlockSpec(memory_space=s) for s in (pl.ANY, pltpu.VMEM, pltpu.SMEM))
    ins = [
        Key.k_input, Key.k_output, Key.k_inner, Key.k_outer, Key.k_own, Key.k_other, Key.k_packed, Key.k_pairs, Key.k_soft, Key.k_context,
        Key.k_norm, Key.k_inverse, Key.k_active, Key.k_slope, Key.k_grad, Key.k_vectors, Key.k_low,
    ]
    kept = dict(kept)
    kept[Key.k_outer] = kept[Key.k_outer].reshape(units, width)
    args = [kept[name] for name in ins] + [kept[Key.k_sums], lengths]
    in_specs = [hbm] * len(ins) + [vmem, smem]
    tall = {Key.outer: units, Key.inner: width, Key.output: width, Key.input: width}
    wide = {Key.outer: width, Key.inner: units, Key.output: width, Key.input: 3 * width}
    lead = (2, nz, 2) if fast else (1, 1, 1)
    blocks = math.prod(lead)
    outs = {Key.grad_input: ((tokens, width), f32)}
    for name in tall:
        if fast:
            outs["g", name] = ((tall[name] // (2 * blocks), wide[name]), f32)
        else:
            outs["g", name] = (lead + (tall[name], wide[name]), bf16)
    outs[Key.g_small] = ((VECTORS, 128 if fast else width), f32)
    out_specs = [vmem if name == Key.g_small else hbm for name in outs]
    steps, partners = (3, nz + 3) if fast else (0, 0)
    scratch = {
        Key.w_outer: pltpu.VMEM((units, width), bf16), Key.w_inner: pltpu.VMEM(lead + (width // blocks, units), bf16),
        Key.w_output: pltpu.VMEM(lead + (width // blocks, width), bf16),
        Key.active: pltpu.VMEM((tokens, units), bf16), Key.slope: pltpu.VMEM((tokens, units), bf16),
        Key.grad: pltpu.VMEM((tokens, width), f32), Key.norm: pltpu.VMEM((tokens, width), f32),
        Key.inverse: pltpu.VMEM((tokens, 128), f32), Key.vectors: pltpu.VMEM((VECTORS, width), f32),
        Key.grad_low: pltpu.VMEM((tokens, width), bf16), Key.low: pltpu.VMEM((tokens, width), bf16),
        Key.back: pltpu.VMEM((tokens, width), bf16),
        Key.sums: pltpu.VMEM((slots, width), f32), Key.col_sums: pltpu.VMEM((8, 8, width), f32),
        Key.ff_sums: pltpu.VMEM((8, units), f32),
        Key.d_outer: pltpu.VMEM(lead + (units // blocks, width), bf16),
        Key.d_inner: pltpu.VMEM(lead + (width // blocks, units), bf16),
        Key.d_output: pltpu.VMEM(lead + (width // blocks, width), bf16),
        Key.table: pltpu.VMEM((steps + 1, VECTORS, width), f32),
        Key.local_sem: pltpu.SemaphoreType.DMA((17,)), Key.out_sem: pltpu.SemaphoreType.DMA((rows,)),
        Key.row_send: pltpu.SemaphoreType.DMA((rows,)), Key.row_recv: pltpu.SemaphoreType.DMA((rows,)),
    }
    if fast:
        pieces = sum(len(v) for v in routes.values())
        scratch.update({
            Key.table_in: pltpu.VMEM((partners, VECTORS, width), f32),
            Key.table_send: pltpu.SemaphoreType.DMA((partners,)), Key.table_recv: pltpu.SemaphoreType.DMA((partners,)),
            Key.piece_send: pltpu.SemaphoreType.DMA((pieces, nz + 4)),
            Key.piece_recv: pltpu.SemaphoreType.DMA((pieces, nz + 4)),
        })
        for name, found in routes.items():
            height = tall[name] // blocks
            for j, (_, _, span) in enumerate(found):
                scratch[Key.swapped, name, j] = pltpu.VMEM(lead + (height, span), bf16)
                scratch[Key.landed, name, j] = pltpu.VMEM(lead + (height, span), bf16)
                scratch[Key.final, name, j] = pltpu.VMEM((height, span), f32)
    else:
        scratch[Key.w_input] = pltpu.VMEM(lead + (width, 3 * width), bf16)
        scratch[Key.keep_sem] = pltpu.SemaphoreType.DMA((4,))
    names = ins + [Key.k_sums, Key.lengths] + list(outs) + list(scratch)
    found = pl.pallas_call(
        functools.partial(backward_kernel, names, fast, sizes, routes, plan),
        out_shape=[jax.ShapeDtypeStruct(*s) for s in outs.values()],
        in_specs=in_specs,
        out_specs=out_specs,
        scratch_shapes=list(scratch.values()),
        compiler_params=pltpu.CompilerParams(
            collective_id=1, has_side_effects=True, vmem_limit_bytes=BACKWARD_VMEM
        ),
        name="backward",
    )(*args)
    return dict(zip(outs, found, strict=True))


def plain_forward(rows, units):
    plan = []
    for r in range(rows):
        plan += [(Key.frame, r), (Key.send, r), (Key.cot, r)]
    plan += [(Key.loaded, Key.w_input), (Key.save, Key.k_vectors)]
    plan += [(Key.project_own, part) for part in range(3)] + [(Key.loaded, Key.w_output)]
    for r in range(rows):
        plan += [(Key.other, r), (Key.project_other, r, 0), (Key.project_other, r, 1)]
        plan += [(Key.attend_pairs, r), (Key.attend_padding, r), (Key.first_norm, r)]
    plan += [(Key.loaded, Key.w_inner), (Key.hidden_units, 0, units // 256), (Key.loaded, Key.w_outer)]
    plan += [(Key.second_norm, r) for r in range(rows)]
    saved = (Key.layer_out, Key.k_input, Key.k_output, Key.k_inner, Key.k_outer, Key.k_own, Key.k_other, Key.k_packed, Key.k_pairs)
    saved += (Key.k_soft, Key.k_context, Key.k_norm, Key.k_inverse, Key.k_active, Key.k_slope, Key.k_grad, Key.k_low)
    return plan + [(Key.save, name) for name in saved]


def plain_backward(rows, units):
    first = (Key.vectors, Key.grad, Key.outer, Key.slope, Key.norm, Key.inner, Key.inverse, Key.output)
    plan = [(Key.load, name) for name in first] + [(Key.loaded, name) for name in first + (Key.low, Key.active)]
    plan += [(Key.lower_norm,), (Key.grad_outer,)]
    plan += [(Key.grad_hidden, 0, units // 384), (Key.keep, Key.outer)]
    plan += [(Key.grad_inner, core, part) for core in range(2) for part in range(units // 1536)] + [(Key.keep, Key.inner)]
    plan += [(Key.load, name) for name in (Key.own, Key.other, Key.context, Key.packed, Key.soft)]
    plan += [(Key.first_back, r) for r in range(rows)]
    plan += [(Key.load, Key.pairs), (Key.load, Key.input)]
    plan += [(Key.loaded, name) for name in (Key.own, Key.other, Key.context, Key.packed, Key.soft, Key.pairs, Key.input)]
    plan += [(Key.grad_output,), (Key.keep, Key.output)]
    plan += [(Key.grad_context, r) for r in range(rows)] + [(Key.drain, Key.inner)]
    for r in range(rows):
        plan += [(Key.attend_back, r), (Key.return_other, r), (Key.send, r)]
    plan += [(Key.token_sums,)] + [(Key.grad_input_weight, part) for part in range(3)]
    plan += [(Key.keep, Key.input)]
    for r in range(rows):
        plan += [(Key.back, r), (Key.grad_hidden_in, r), (Key.put, r)]
    return plan + [(Key.drain, Key.outer), (Key.drain, Key.output), (Key.drain, Key.input)]


GATHER = {
    Key.w_input: (
        (("XZY", "ZXY"), 0, 640, 0, 48),
        (("ZXY", "XZY"), 640, 512, 0, 48),
    ),
    Key.w_output: (
        (("XZY", "ZXY"), 0, 384, 0, 48),
    ),
    Key.w_inner: (
        (("XYZ", "XZY"), 0, 768, 0, 48),
        (("ZXY", "ZYX"), 768, 768, 0, 48),
    ),
    Key.w_outer: (
        (("ZYX", "YXZ"), 0, 384, 0, 96),
        (("ZYX", "ZXY"), 0, 384, 96, 96),
    ),
}
SCATTER = {
    Key.outer: (
        (("XZY", "ZXY"), (0, 512), 256),
        (("YXZ", "XYZ"), (256, 384), 128),
    ),
    Key.inner: (
        (("YXZ", "XZY"), (0, 1536), 768),
        (("XYZ", "YXZ"), (768, 2304), 768),
    ),
    Key.output: (
        (("ZYX", "ZYX"), (0, 384), 384),
    ),
    Key.input: (
        (("ZYX", "YXZ"), (0, 1536), 768),
        (("YXZ", "XYZ"), (768, 1152), 384),
    ),
}
FORWARD_PLAN = (
    (Key.lay, 0), (Key.event, Key.w_input, 1, 0), (Key.event, Key.w_input, 0, 0), (Key.frame, 0), (Key.frame, 1),
    (Key.frame, 2), (Key.frame, 3), (Key.lay, 1), (Key.lay, 2), (Key.lay, 3), (Key.cot, 0), (Key.cot, 1), (Key.cot, 2),
    (Key.total, 0), (Key.cot, 3), (Key.event, Key.w_input, 1, 1), (Key.event, Key.w_output, 0, 0),
    (Key.event, Key.w_input, 0, 1), (Key.total, 1), (Key.send, 0), (Key.event, Key.w_inner, 0, 0),
    (Key.event, Key.w_input, 1, 2), (Key.event, Key.w_output, 0, 1), (Key.event, Key.w_inner, 1, 0),
    (Key.event, Key.w_outer, 1, 0), (Key.event, Key.w_input, 0, 2), (Key.send, 1), (Key.send, 2),
    (Key.event, Key.w_input, 1, 3), (Key.event, Key.w_inner, 0, 1), (Key.event, Key.w_outer, 0, 0),
    (Key.event, Key.w_input, 1, 4), (Key.total, 2), (Key.send, 3), (Key.event, Key.w_output, 0, 2),
    (Key.event, Key.w_inner, 1, 1), (Key.event, Key.w_input, 0, 3), (Key.event, Key.w_input, 0, 4), (Key.save, Key.k_input),
    (Key.save, Key.k_own), (Key.project_own, 0), (Key.project_own, 1), (Key.project_own, 2), (Key.save, Key.k_packed),
    (Key.save, Key.k_vectors), (Key.event, Key.w_outer, 1, 1), (Key.other, 0), (Key.project_other, 0, 0),
    (Key.project_other, 0, 1), (Key.attend_pairs, 0), (Key.event, Key.w_output, 0, 3), (Key.attend_padding, 0),
    (Key.event, Key.w_output, 0, 4), (Key.save, Key.k_output), (Key.other, 1), (Key.project_other, 1, 0),
    (Key.project_other, 1, 1), (Key.event, Key.w_inner, 0, 2), (Key.attend_pairs, 1), (Key.attend_padding, 1),
    (Key.event, Key.w_outer, 0, 1), (Key.other, 2), (Key.project_other, 2, 0), (Key.project_other, 2, 1),
    (Key.attend_pairs, 2), (Key.event, Key.w_inner, 1, 2), (Key.attend_padding, 2), (Key.other, 3),
    (Key.project_other, 3, 0), (Key.project_other, 3, 1), (Key.save, Key.k_pairs), (Key.save, Key.k_other),
    (Key.event, Key.w_outer, 1, 2), (Key.attend_pairs, 3), (Key.save, Key.k_soft), (Key.event, Key.w_outer, 0, 2),
    (Key.attend_padding, 3), (Key.save, Key.k_context), (Key.first_norm, 0), (Key.event, Key.w_inner, 0, 3),
    (Key.first_norm, 1), (Key.first_norm, 2), (Key.event, Key.w_inner, 1, 3), (Key.event, Key.w_inner, 0, 4),
    (Key.first_norm, 3), (Key.save, Key.k_norm), (Key.save, Key.k_inverse), (Key.event, Key.w_inner, 1, 4),
    (Key.save, Key.k_inner), (Key.hidden_units, 0, 2), (Key.hidden_units, 2, 2), (Key.event, Key.w_outer, 1, 3),
    (Key.hidden_units, 4, 2), (Key.hidden_units, 6, 2), (Key.event, Key.w_outer, 1, 4), (Key.hidden_units, 8, 2),
    (Key.event, Key.w_outer, 0, 3), (Key.hidden_units, 10, 2), (Key.save, Key.k_active), (Key.save, Key.k_slope),
    (Key.event, Key.w_outer, 0, 4), (Key.save, Key.k_outer), (Key.second_norm, 0), (Key.second_norm, 1),
    (Key.second_norm, 2), (Key.second_norm, 3), (Key.save, Key.layer_out), (Key.save, Key.k_grad), (Key.save, Key.k_low),
)
BACKWARD_PLAN = (
    (Key.loaded, Key.low), (Key.loaded, Key.active), (Key.load, Key.outer), (Key.load, Key.slope), (Key.load, Key.vectors),
    (Key.load, Key.norm), (Key.load, Key.inner), (Key.load, Key.grad), (Key.load, Key.inverse), (Key.load, Key.output),
    (Key.grad_outer,), (Key.event, Key.outer, 0, 0), (Key.loaded, Key.outer), (Key.loaded, Key.slope),
    (Key.loaded, Key.vectors), (Key.load, Key.packed), (Key.load, Key.soft), (Key.grad_hidden, 0, 2),
    (Key.grad_hidden, 2, 2), (Key.event, Key.outer, 1, 0), (Key.event, Key.outer, 0, 1), (Key.grad_hidden, 4, 2),
    (Key.event, Key.outer, 1, 1), (Key.grad_hidden, 6, 2), (Key.load, Key.own), (Key.load, Key.other), (Key.load, Key.context),
    (Key.loaded, Key.norm), (Key.lower_norm,), (Key.grad_inner, 0, 0), (Key.event, Key.inner, 0, 0),
    (Key.grad_inner, 1, 0), (Key.grad_inner, 0, 1), (Key.event, Key.inner, 0, 1), (Key.event, Key.inner, 1, 0),
    (Key.grad_inner, 1, 1), (Key.loaded, Key.inner), (Key.loaded, Key.inverse), (Key.loaded, Key.grad), (Key.first_back, 0),
    (Key.event, Key.inner, 1, 1), (Key.event, Key.outer, 1, 2), (Key.first_back, 1), (Key.event, Key.outer, 0, 2),
    (Key.event, Key.inner, 0, 2), (Key.first_back, 2), (Key.first_back, 3), (Key.event, Key.inner, 1, 2),
    (Key.load, Key.pairs), (Key.load, Key.input), (Key.loaded, Key.context), (Key.loaded, Key.output), (Key.grad_output,),
    (Key.event, Key.outer, 1, 3), (Key.grad_context, 0), (Key.grad_context, 1), (Key.grad_context, 2),
    (Key.grad_context, 3), (Key.event, Key.outer, 0, 3), (Key.loaded, Key.packed), (Key.loaded, Key.soft),
    (Key.loaded, Key.pairs), (Key.loaded, Key.input), (Key.attend_back, 0), (Key.return_other, 0), (Key.send, 0),
    (Key.attend_back, 1), (Key.event, Key.inner, 0, 3), (Key.event, Key.inner, 1, 3), (Key.event, Key.outer, 0, 4),
    (Key.event, Key.output, 0, 0), (Key.return_other, 1), (Key.send, 1), (Key.attend_back, 2),
    (Key.event, Key.outer, 1, 4), (Key.event, Key.outer, 0, 5), (Key.event, Key.output, 0, 1), (Key.event, Key.inner, 0, 4),
    (Key.return_other, 2), (Key.send, 2), (Key.event, Key.outer, 1, 5), (Key.attend_back, 3), (Key.event, Key.inner, 0, 5),
    (Key.return_other, 3), (Key.send, 3), (Key.token_sums,), (Key.total, -1), (Key.loaded, Key.own), (Key.loaded, Key.other),
    (Key.event, Key.inner, 1, 4), (Key.drain, Key.inner), (Key.grad_input_weight, 0), (Key.grad_input_weight, 2),
    (Key.total, 0), (Key.event, Key.inner, 1, 5), (Key.event, Key.input, 0, 0), (Key.grad_input_weight, 1),
    (Key.event, Key.input, 1, 0), (Key.event, Key.input, 0, 1), (Key.back, 0), (Key.grad_hidden_in, 0), (Key.put, 0),
    (Key.event, Key.input, 1, 1), (Key.event, Key.output, 0, 2), (Key.back, 1), (Key.grad_hidden_in, 1), (Key.put, 1),
    (Key.back, 2), (Key.grad_hidden_in, 2), (Key.put, 2), (Key.back, 3), (Key.grad_hidden_in, 3), (Key.put, 3),
    (Key.total, 1), (Key.event, Key.output, 0, 3), (Key.event, Key.input, 1, 2), (Key.event, Key.input, 0, 2),
    (Key.event, Key.output, 0, 4), (Key.event, Key.input, 1, 3), (Key.event, Key.output, 0, 5), (Key.event, Key.input, 0, 3),
    (Key.total, 2), (Key.event, Key.input, 1, 4), (Key.event, Key.input, 1, 5), (Key.event, Key.input, 0, 4),
    (Key.event, Key.input, 0, 5), (Key.drain, Key.outer), (Key.drain, Key.output), (Key.drain, Key.input),
)


def gather_routes(masters):
    return {
        name: [(route, (row, count), (col, span)) for route, col, span, row, count in found]
        for name, found in GATHER.items()
    }


def scatter_routes(width, units):
    return SCATTER


def forward_steps(rows, nz, units):
    return FORWARD_PLAN


def backward_steps(rows, nz):
    return BACKWARD_PLAN


def spread(masters, vectors):
    gathered = [lax.all_gather(v.astype(bf16), ("pair", "rows"), axis=0, tiled=True) for v in masters]
    rows = [lax.all_gather(v, ("pair", "rows"), axis=0, tiled=True) for v in vectors]
    width = rows[0].shape[0]
    table = jnp.concatenate(rows).reshape(-1, width)
    return gathered, [jnp.pad(table, ((0, VECTORS - table.shape[0]), (0, 0)))]


def gather_sums(found, units):
    def summed(v):
        return lax.psum_scatter(v.astype(f32), ("pair", "rows"), scatter_dimension=0, tiled=True)

    weights = {name: summed(found[name].reshape(found[name].shape[3:])) for name in found if name != Key.g_small}
    table = found[Key.g_small]
    width = table.shape[1]
    small = [summed(table[k]) for k in range(8)] + [summed(table[8 : 8 + units // width].reshape(units))]
    return weights, small


def shards(rows_axis, *args):
    (
        hidden_in, input_proj, query_bias, value_bias, output_proj, output_bias, first_gain, first_shift,
        inner_proj, inner_bias, outer_proj, outer_bias, second_gain, second_shift, cotangent, pair_lengths,
    ) = args
    row_count, _, slots, width = hidden_in.shape
    units = inner_proj.shape[1]
    share = input_proj.shape[0]
    fast = rows_axis % 4 == 0 and share % 8 == 0
    masters = (input_proj, output_proj, inner_proj, outer_proj)
    vectors = (
        query_bias, value_bias, output_bias, first_gain, first_shift, outer_bias, second_gain, second_shift,
        inner_bias,
    )
    if fast:
        routes_f, plan_f = gather_routes(masters), forward_steps(row_count, rows_axis // 4, units)
        routes_b, plan_b = scatter_routes(width, units), backward_steps(row_count, rows_axis // 4)
        small = [v.reshape(1, -1) for v in vectors]
    else:
        routes_f, routes_b = {}, {}
        plan_f, plan_b = plain_forward(row_count, units), plain_backward(row_count, units)
        masters, small = spread(masters, vectors)
    sizes = (row_count, slots, width, pair_lengths.shape[2])
    kept = forward_call(
        rows_axis, fast, hidden_in[:, 0], cotangent[:, 0], masters, small, pair_lengths, routes_f, plan_f
    )
    found = backward_call(rows_axis, fast, kept, pair_lengths, routes_b, plan_b, sizes, units)
    layer_out = kept[Key.layer_out].reshape(hidden_in.shape)
    grad_input = found.pop(Key.grad_input).reshape(hidden_in.shape)
    if fast:
        table = found[Key.g_small]
        sums = [table[k, :share] for k in range(8)] + [table[8, : inner_bias.shape[0]]]
    else:
        found, sums = gather_sums(found, units)
    return (
        layer_out, grad_input, found["g", Key.input], sums[Q_BIAS], sums[V_BIAS], found["g", Key.output], sums[O_BIAS],
        sums[GAIN_1], sums[SHIFT_1], found["g", Key.inner], sums[FF_ROW], found["g", Key.outer], sums[OUT_BIAS],
        sums[GAIN_2], sums[SHIFT_2],
    )


def solution(mesh):
    tokens = P("rows", "pair", None, None)
    matrix = P(("pair", "rows"), None)
    vector = P(("pair", "rows"))
    weights = (
        matrix, vector, vector, matrix, vector, vector, vector, matrix, vector, matrix, vector, vector, vector
    )
    return jax.shard_map(
        functools.partial(shards, mesh.shape["rows"]),
        mesh=mesh,
        in_specs=(tokens, *weights, tokens, P("rows", None, None)),
        out_specs=(tokens, tokens, *weights),
        check_vma=False,
    )
```

```python
import enum
import functools
import math

import jax
import jax.numpy as jnp
from jax import lax
from jax.experimental import pallas as pl
from jax.experimental.pallas import tpu as pltpu
from jax.sharding import PartitionSpec as P

HEADS = 12
EPSILON = 1e-12
MESH = pl.DeviceIdType.MESH
bf16 = jnp.bfloat16
f32 = jnp.float32
ALL = slice(None)
MASKED = -1e30
VECTORS = 16
Q_BIAS, V_BIAS, O_BIAS, GAIN_1, SHIFT_1, OUT_BIAS, GAIN_2, SHIFT_2, FF_ROW = range(9)


def contract(left, right, left_dim, right_dim):
    return lax.dot_general(
        left, right, (((left_dim,), (right_dim,)), ((), ())), preferred_element_type=f32
    )


def iota(shape, dim):
    return lax.broadcasted_iota(jnp.int32, shape, dim)


def rounded(v):
    return v.astype(bf16).astype(f32)


class Key(enum.Enum):
    active = 0
    attend_back = 1
    attend_padding = 2
    attend_pairs = 3
    back = 4
    col_sums = 5
    context = 6
    cot = 7
    cotangent = 8
    d_inner = 9
    d_outer = 10
    d_output = 11
    drain = 12
    event = 13
    ff_bias = 14
    ff_sums = 15
    final = 16
    first_back = 17
    first_norm = 18
    frame = 19
    framed = 20
    from_sibling = 21
    g_small = 22
    gain_sum = 23
    grad = 24
    grad_context = 25
    grad_hidden = 26
    grad_hidden_in = 27
    grad_inner = 28
    grad_input = 29
    grad_input_weight = 30
    grad_low = 31
    grad_outer = 32
    grad_output = 33
    hidden = 34
    hidden_in = 35
    hidden_units = 36
    inner = 37
    input = 38
    inverse = 39
    k_active = 40
    k_context = 41
    k_grad = 42
    k_inner = 43
    k_input = 44
    k_inverse = 45
    k_low = 46
    k_norm = 47
    k_other = 48
    k_outer = 49
    k_output = 50
    k_own = 51
    k_packed = 52
    k_pairs = 53
    k_slope = 54
    k_soft = 55
    k_sums = 56
    k_vectors = 57
    keep = 58
    keep_sem = 59
    landed = 60
    lay = 61
    layer_out = 62
    lengths = 63
    load = 64
    loaded = 65
    local_sem = 66
    low = 67
    low_sum = 68
    lower_norm = 69
    m_inner = 70
    m_input = 71
    m_outer = 72
    m_output = 73
    norm = 74
    other = 75
    out_sem = 76
    outer = 77
    output = 78
    own = 79
    packed = 80
    pairs = 81
    pairs_other = 82
    piece_recv = 83
    piece_send = 84
    project_other = 85
    project_own = 86
    put = 87
    return_other = 88
    row_recv = 89
    row_send = 90
    save = 91
    saved = 92
    second_norm = 93
    send = 94
    shift_sum = 95
    slope = 96
    soft = 97
    sums = 98
    swap_recv = 99
    swap_send = 100
    swapped = 101
    table = 102
    table_in = 103
    table_recv = 104
    table_send = 105
    token_sums = 106
    total = 107
    vector = 108
    vectors = 109
    w_inner = 110
    w_input = 111
    w_outer = 112
    w_output = 113


def attributes(refs):
    return {key.name: ref for key, ref in refs.items() if isinstance(key, Key)}


class Place:
    def __init__(self, rows):
        self.nz = rows // 4
        r = lax.axis_index("rows")
        self.x = lax.axis_index("pair")
        self.z = r // 4
        self.y = (r // 2) % 2
        self.c = r % 2
        self.index = self.x * rows + r
        self.own = {"X": self.x, "Z": self.z, "Y": self.y}

    def device(self, **other):
        at = {"X": self.x, "Z": self.z, "Y": self.y, "C": self.c, **other}
        return {"pair": at["X"], "rows": (at["Z"] * 2 + at["Y"]) * 2 + at["C"]}

    def peers(self, dim):
        if dim == "Z":
            return [(self.z + k) % self.nz for k in range(1, self.nz)]
        return [1 - self.own[dim]]

    def sources(self, dim):
        if dim == "Z":
            return [(self.z + self.nz - k) % self.nz for k in range(1, self.nz)]
        return [1 - self.own[dim]]

    def first_slot(self, dim):
        return {"X": 0, "Y": 1, "Z": 2}[dim]

    def slots(self):
        return self.nz + 1


def slab(buf, place, gathered, at, rows, cols):
    own = {**place.own, **at}
    lead = tuple(ALL if d in gathered else own[d] for d in "XZY")
    return buf.at[lead + (rows, cols)]


class Gather:
    def __init__(self, buf, place, send, recv, routes, rows, col, width):
        self.buf, self.place, self.send, self.recv, self.routes = buf, place, send, recv, routes
        self.rows, self.col, self.width = rows, col, width
        self.half = buf.shape[-1] // 2

    def cols(self, core):
        return pl.ds(pl.multiple_of(core * self.half + self.col, 128), self.width)

    def per_core(self, act):
        if self.routes[0] == self.routes[1]:
            act(self.routes[0])
            return
        for core in range(2):
            pl.when(self.place.c == core)(functools.partial(act, self.routes[core]))

    def copy(self, view, slot, device):
        return pltpu.make_async_remote_copy(
            src_ref=view,
            dst_ref=view,
            send_sem=self.send.at[slot],
            recv_sem=self.recv.at[slot],
            device_id=device,
            device_id_type=MESH,
        )

    def sends(self, route, stage):
        dim, gathered = route[stage], route[:stage]
        view = slab(self.buf, self.place, gathered, {}, self.rows, self.cols(self.place.c))
        first = self.place.first_slot(dim)
        return [
            self.copy(view, first + k, self.place.device(**{dim: peer}))
            for k, peer in enumerate(self.place.peers(dim))
        ]

    def arrivals(self, route, stage, core):
        dim, gathered = route[stage], route[:stage]
        return [
            slab(self.buf, self.place, gathered, {dim: peer}, self.rows, self.cols(core))
            for peer in self.place.sources(dim)
        ]

    def hand_ons(self, route, stage, core):
        device = self.place.device(C=1 - self.place.c)
        base = self.place.slots()
        if stage == 0:
            view = slab(self.buf, self.place, route[:1], {}, self.rows, self.cols(core))
            return [self.copy(view, base, device)]
        first = base + 1 + (stage - 1) * (self.place.nz - 1)
        return [
            self.copy(view, first + k, device)
            for k, view in enumerate(self.arrivals(route, stage, core))
        ]

    def start(self, stage):
        def act(route):
            for copy in self.sends(route, stage):
                copy.start()

        self.per_core(act)

    def arrived(self, stage):
        def act(route):
            dim = route[stage]
            first = self.place.first_slot(dim)
            device = self.place.device()
            for k, view in enumerate(self.arrivals(route, stage, self.place.c)):
                self.copy(view, first + k, device).wait_recv()
            if stage < 2:
                for copy in self.sends(route, stage + 1):
                    copy.start()
            for copy in self.hand_ons(route, stage, self.place.c):
                copy.start()

        self.per_core(act)

    def event(self, number):
        if number == 0:
            self.start(0)
        elif number < 4:
            self.arrived(number - 1)
        else:
            self.complete()

    def complete(self):
        def other(route):
            for stage in range(3):
                for copy in self.hand_ons(route, stage, 1 - self.place.c):
                    copy.wait_recv()

        if self.routes[0] == self.routes[1]:
            other(self.routes[0])
        else:
            for core in range(2):
                pl.when(self.place.c == 1 - core)(functools.partial(other, self.routes[core]))

    def drain(self):
        def act(route):
            for stage in range(3):
                for copy in self.sends(route, stage) + self.hand_ons(route, stage, self.place.c):
                    copy.wait_send()

        self.per_core(act)


def greet(place, devices):
    barrier = pltpu.get_barrier_semaphore()
    for device in devices:
        pl.semaphore_signal(barrier, inc=1, device_id=device, device_id_type=MESH)
    pl.semaphore_wait(barrier, len(devices))


class Totals:
    def __init__(self, place, table, landed, send, recv):
        self.place, self.table, self.landed, self.send, self.recv = place, table, landed, send, recv
        x, y = 1 - place.x, 1 - place.y
        self.steps = [
            [place.device(C=1 - place.c)],
            [place.device(X=x), place.device(Y=y), place.device(X=x, Y=y)],
            [place.device(Z=peer) for peer in place.peers("Z")],
        ]

    def copies(self, step):
        first = sum(len(found) for found in self.steps[:step])
        return [
            pltpu.make_async_remote_copy(
                src_ref=self.table.at[step],
                dst_ref=self.landed.at[first + k],
                send_sem=self.send.at[first + k],
                recv_sem=self.recv.at[first + k],
                device_id=device,
                device_id_type=MESH,
            )
            for k, device in enumerate(self.steps[step])
        ]

    def start(self, step):
        for copy in self.copies(step):
            copy.start()

    def advance(self, step):
        first = sum(len(found) for found in self.steps[:step])
        total = self.table[step]
        for k, copy in enumerate(self.copies(step)):
            copy.wait_recv()
            total = total + self.landed[first + k]
        self.table[step + 1] = total
        if step + 1 < len(self.steps):
            self.start(step + 1)

    def drain(self):
        for step in range(len(self.steps)):
            for copy in self.copies(step):
                copy.wait_send()


def neighbours(place):
    x, y = 1 - place.x, 1 - place.y
    found = [place.device(C=1 - place.c), place.device(X=x), place.device(Y=y), place.device(X=x, Y=y)]
    return found + [place.device(Z=peer) for peer in place.peers("Z")]


def source_slots(slots, sizes, most):
    frame, offset = slots // most, slots % most
    total = sum(sizes[1:], sizes[0])
    found, start = slots, jnp.int32(0)
    for p, size in enumerate(sizes):
        mine = jnp.where(offset < size, start + offset, total + slots - (start + size))
        found = jnp.where(frame == p, mine, found)
        start = start + size
    return found


def holds_token(slots, sizes, most):
    frame, offset = slots // most, slots % most
    held = jnp.zeros(slots.shape, f32)
    for p, size in enumerate(sizes):
        held = jnp.where((frame == p) & (offset < size), 1.0, held)
    return held


def into_frames(sizes, slots, most):
    source = source_slots(iota((slots, 1), 0), sizes, most)
    return (iota((slots, slots), 1) == source).astype(f32).astype(bf16)


def out_of_frames(sizes, slots, most):
    source = source_slots(iota((1, slots), 1), sizes, most)
    return (iota((slots, slots), 0) == source).astype(f32).astype(bf16)


def folded(v):
    return jnp.sum(v.reshape(v.shape[0] // 8, 8, v.shape[1]), axis=0)


def spread_heads(tokens, span):
    shape = (4 * tokens, span)
    return iota(shape, 0) // tokens == iota(shape, 1) // (span // 4)


def block_rows(i, size):
    return pl.ds(pl.multiple_of(i * size, size), size)


class Forward:
    def __init__(self, refs, place, sizes):
        self.__dict__.update(attributes(refs))
        self.place = place
        self.rows, self.slots, self.width, self.pairs = sizes
        self.most = self.slots // self.pairs
        self.half = place.x
        self.bias_rows = self.ff_bias.shape[1] // self.width
        self.scale = (self.width // HEADS) ** (-0.5)

    def sizes_of(self, row, half):
        return [self.lengths[row, half, p] for p in range(self.pairs)]

    def row(self, r):
        return pl.ds(r * self.slots, self.slots)

    def vector(self, at, count=1):
        found = rounded(self.vectors[at : at + count, :])
        return found if count == 1 else found.reshape(1, count * self.width)

    def frame_hidden(self, r):
        frames = into_frames(self.sizes_of(r, self.half), self.slots, self.most)
        self.own[self.row(r), :] = contract(frames, self.hidden[self.row(r), :], 1, 0).astype(bf16)

    def frame_cotangent(self, r):
        sizes = self.sizes_of(r, self.half)
        frames = into_frames(sizes, self.slots, self.most)
        held = holds_token(iota((self.slots, 1), 0), sizes, self.most)
        moved = contract(frames, self.cot[self.row(r), :], 1, 0) * held
        self.cot[self.row(r), :] = moved.astype(bf16)

    def project_own(self, part):
        cols = slice(part * self.width, (part + 1) * self.width)
        weight = self.w_input[:, :, :, :, cols].reshape(self.width, self.width)
        acc = contract(self.own[...], weight, 1, 0)
        if part == 0:
            acc = acc + self.vector(Q_BIAS)
        if part == 2:
            acc = acc + self.vector(V_BIAS)
        self.packed[:, cols] = acc.astype(bf16)

    def project_other(self, r, part):
        cols = slice(part * self.width, (part + 1) * self.width)
        from_cols = slice((part + 1) * self.width, (part + 2) * self.width)
        weight = self.w_input[:, :, :, :, from_cols].reshape(self.width, self.width)
        acc = contract(self.other[self.row(r), :], weight, 1, 0)
        if part == 1:
            acc = acc + self.vector(V_BIAS)
        self.pairs_other[self.row(r), cols] = acc.astype(bf16)

    def attend_pairs(self, r, together=4):
        most, span, wide = self.most, 4 * (self.width // HEADS), 2 * self.most
        spread = spread_heads(wide, span)
        key, query = iota((2 * wide, 4 * wide), 0), iota((2 * wide, 4 * wide), 1)
        key_frame, same = key % wide // most, key % wide // most == query % wide // most
        slot = key % most

        def two_pairs(pair):
            rows = pl.ds(pl.multiple_of(r * self.slots + pair * wide, wide), wide)
            counts = [self.lengths[r, half, 2 * pair + k] for half in (self.half, 1 - self.half) for k in range(2)]
            mine = jnp.where(key_frame == 0, counts[0], counts[1])
            theirs = jnp.where(key_frame == 0, counts[2], counts[3])
            allowed = same & (slot < jnp.where(key < wide, mine, theirs))
            for at in range(0, self.width, span):
                queries = self.packed[rows, at : at + span]
                keys = jnp.concatenate(
                    [
                        self.packed[rows, self.width + at : self.width + at + span],
                        self.pairs_other[rows, at : at + span],
                    ],
                    axis=0,
                )
                values = jnp.concatenate(
                    [
                        self.packed[rows, 2 * self.width + at : 2 * self.width + at + span],
                        self.pairs_other[rows, self.width + at : self.width + at + span],
                    ],
                    axis=0,
                )
                tiled = jnp.where(spread, jnp.concatenate([queries] * 4, axis=0), 0).astype(bf16)
                scores = jnp.where(allowed, contract(keys, tiled, 1, 1) * self.scale, MASKED)
                raw = jnp.exp(scores - jnp.max(scores, axis=0, keepdims=True))
                soft = raw * (1.0 / jnp.sum(raw, axis=0, keepdims=True))
                kept = [soft[k * most : (k + 1) * most] + soft[(k + 1) * most : (k + 2) * most] for k in (0, 2)]
                self.soft[rows, at : at + span] = jnp.concatenate(kept, axis=0).astype(bf16)
                mixed = contract(soft.astype(bf16), values, 0, 0)
                mixed = jnp.where(spread, mixed, 0.0)
                context = sum(mixed[h * wide : (h + 1) * wide, :] for h in range(4))
                self.context[rows, at : at + span] = context.astype(bf16)

        @pl.loop(0, self.pairs // (2 * together))
        def _(several):
            for k in range(together):
                two_pairs(several * together + k)

    def attend_padding(self, r, together=6):
        sizes = self.sizes_of(r, self.half)
        head = self.width // HEADS
        held_key = holds_token(iota((1, self.slots), 1), sizes, self.most)
        held_query = holds_token(iota((self.slots, 1), 0), sizes, self.most)
        pad_key = jnp.broadcast_to(held_key, (2 * self.slots, self.slots)) < 0.5
        pad_query = jnp.broadcast_to(held_query, (self.slots, 2 * head)) < 0.5
        left = iota((self.slots, 2 * head), 1) < head
        rows = self.row(r)

        def two_heads(pair):
            at = pl.multiple_of(pair * 2 * head, 2 * head)
            queries = self.packed[rows, pl.ds(at, 2 * head)] * self.scale
            keys = self.packed[rows, pl.ds(pl.multiple_of(self.width + at, 2 * head), 2 * head)]
            values = self.packed[rows, pl.ds(pl.multiple_of(2 * self.width + at, 2 * head), 2 * head)]
            both = jnp.concatenate([jnp.where(left, queries, 0), jnp.where(left, 0, queries)], axis=0)
            scores = jnp.where(pad_key, contract(both.astype(bf16), keys, 1, 1), MASKED)
            raw = jnp.exp(scores - jnp.max(scores, axis=1, keepdims=True))
            total = jnp.sum(raw, axis=1, keepdims=True)
            found = contract(raw.astype(bf16), values, 1, 0) * (1.0 / total)
            padded = jnp.where(left, found[: self.slots], found[self.slots :]).astype(bf16)
            cols = pl.ds(at, 2 * head)
            self.context[rows, cols] = jnp.where(pad_query, padded, self.context[rows, cols])

        @pl.loop(0, HEADS // 2 // together)
        def _(several):
            for k in range(together):
                two_heads(several * together + k)

    def first_norm(self, r):
        if r < self.rows:
            weight = self.w_output[...].reshape(self.width, self.width)
            self.sums[r % 2] = contract(self.context[self.row(r), :], weight, 1, 0)
        if r == 0:
            return
        bias, gain, shift = self.vector(O_BIAS), self.vector(GAIN_1), self.vector(SHIFT_1)
        size = 32
        for i in range(0, self.slots, size):
            there = pl.ds((r - 1) * self.slots + i, size)
            total = self.own[there, :].astype(f32) + self.sums[(r - 1) % 2, i : i + size, :] + bias
            centered = total - jnp.mean(total, axis=1, keepdims=True)
            inverse = lax.rsqrt(jnp.mean(centered * centered, axis=1, keepdims=True) + EPSILON)
            norm = centered * inverse
            self.norm[there, :] = norm
            self.inverse[there, :] = jnp.broadcast_to(inverse, (size, 128))
            self.low[there, :] = (norm * gain + shift).astype(bf16)

    def hidden_units(self, first, count, size=256):
        @pl.loop(first, first + count)
        def _(n):
            cols = pl.ds(pl.multiple_of(n * size, size), size)
            weight = self.w_inner[:, :, :, :, cols].reshape(self.width, size)
            bias = rounded(self.ff_bias[:, cols])
            for r in range(self.rows):
                inner = contract(self.low[self.row(r), :], weight, 1, 0) + bias
                share = 0.5 * (1.0 + lax.erf(inner * (0.5**0.5)))
                slope = share + inner * (jnp.exp(-0.5 * inner * inner) * ((2.0 * math.pi) ** -0.5))
                self.active[self.row(r), cols] = (inner * share).astype(bf16)
                self.slope[self.row(r), cols] = slope.astype(bf16)

    def second_norm(self, r):
        if r < self.rows:
            weight = self.w_outer[...].reshape(self.w_inner.shape[-1], self.width)
            self.sums[r % 2] = contract(self.active[self.row(r), :], weight, 1, 0)
        if r == 0:
            return
        gain_1, shift_1 = self.vector(GAIN_1), self.vector(SHIFT_1)
        bias, gain, shift = self.vector(OUT_BIAS), self.vector(GAIN_2), self.vector(SHIFT_2)
        size = 32
        sums = [self.gain_sum[...], self.shift_sum[...], self.low_sum[...]]
        for i in range(0, self.slots, size):
            there = pl.ds((r - 1) * self.slots + i, size)
            total = (self.norm[there, :] * gain_1 + shift_1) + self.sums[(r - 1) % 2, i : i + size, :] + bias
            centered = total - jnp.mean(total, axis=1, keepdims=True)
            inverse = lax.rsqrt(jnp.mean(centered * centered, axis=1, keepdims=True) + EPSILON)
            norm = centered * inverse
            self.framed[i : i + size, :] = (norm * gain + shift).astype(bf16)
            upstream = self.cot[there, :].astype(f32)
            incoming = upstream * gain
            plain = jnp.mean(incoming, axis=1, keepdims=True)
            along = jnp.mean(incoming * norm, axis=1, keepdims=True)
            grad = inverse * (incoming - plain - norm * along)
            low = grad.astype(bf16)
            self.grad[there, :] = grad
            self.soft[there, :] = low
            parts = (upstream * norm, upstream, low.astype(f32))
            sums = [total + folded(part) for total, part in zip(sums, parts, strict=True)]
        self.gain_sum[...], self.shift_sum[...], self.low_sum[...] = sums
        back = out_of_frames(self.sizes_of(r - 1, self.half), self.slots, self.most)
        self.hidden[self.row(r - 1), :] = contract(back, self.framed[...], 1, 0).astype(bf16)


FORWARD_VMEM = 127 * 2**19
ORDER = None


def forward_kernel(names, fast, sizes, routes, plan, *refs):
    refs = dict(zip(names, refs, strict=True))
    rows, slots, width, pairs = sizes
    place = Place(lax.axis_size("rows"))
    run = Forward(refs, place, sizes)
    sibling = place.device(C=1 - place.c)
    partner = place.device(X=1 - place.x)

    def local(src, dst, slot):
        return pltpu.make_async_copy(src, dst, run.local_sem.at[slot])

    load_hidden = local(run.hidden_in, run.hidden, 0)
    load_cot = local(run.cotangent, run.cot, 1)
    load_hidden.start()
    load_cot.start()

    if fast:
        greet(place, neighbours(place))
    else:
        greet(place, [partner])

    def hidden_copy(r):
        view = pl.ds(r * slots, slots)
        return pltpu.make_async_remote_copy(
            src_ref=run.own.at[view],
            dst_ref=run.other.at[view],
            send_sem=run.row_send.at[r],
            recv_sem=run.row_recv.at[r],
            device_id=partner,
            device_id_type=MESH,
        )

    weights = [Key.w_input, Key.w_output, Key.w_inner, Key.w_outer]
    masters = [Key.m_input, Key.m_output, Key.m_inner, Key.m_outer]
    gathers = {}
    drains = []
    if fast:
        totals = Totals(place, run.table, run.table_in, run.table_send, run.table_recv)
        for k, (weight, master) in enumerate(zip(weights, masters, strict=True)):
            buf = refs[weight]
            half = buf.shape[-1] // 2
            for j, (route, (row, count), (col, span)) in enumerate(routes.get(weight, ())):
                piece = Gather(
                    buf, place, run.piece_send.at[len(gathers)], run.piece_recv.at[len(gathers)],
                    route, pl.ds(row, count), col, span,
                )
                gathers[weight, j] = piece

        def swap(k):
            master = refs[masters[k]]
            half = master.shape[-1] // 2
            theirs = pl.ds(pl.multiple_of((1 - place.c) * half, 128), half)
            return pltpu.make_async_remote_copy(
                src_ref=master.at[:, theirs],
                dst_ref=refs[Key.from_sibling, k],
                send_sem=run.swap_send.at[k],
                recv_sem=run.swap_recv.at[k],
                device_id=sibling,
                device_id_type=MESH,
            )

        def lay(k):
            swap(k).wait_recv()
            master, buf = refs[masters[k]], refs[weights[k]]
            half = master.shape[-1] // 2
            cols = pl.ds(pl.multiple_of(place.c * half, 128), half)
            mine, theirs = master[:, cols], refs[Key.from_sibling, k][...]
            first = place.c == 0
            both = jnp.concatenate([jnp.where(first, mine, theirs), jnp.where(first, theirs, mine)], axis=0)
            buf[place.x, place.z, place.y, :, cols] = both.astype(bf16)

        for k in range(4):
            swap(k).start()
        run.table[0] = jnp.zeros((VECTORS, width), f32)
        for k in range(9):
            share = refs[Key.vector, k]
            run.table[0, k : k + 1, 0 : share.shape[1]] = share[...]
        piece = refs[Key.vector, 0].shape[1]
        wide = refs[Key.vector, 8].shape[1]
        per_row = width // wide
        upper = pltpu.roll(run.table[0, 0:8, :], place.index * piece, axis=1)
        lower = pltpu.roll(run.table[0, 8:16, :], (place.index % per_row) * wide, axis=1)
        lower = jnp.broadcast_to(lower[:1, :], (8, width))
        lower = jnp.where(iota((8, width), 0) == place.index // per_row, lower, 0.0)
        run.table[0, 0:8, :] = upper
        run.table[0, 8:16, :] = lower
        totals.start(0)

    def spread_vectors(table):
        run.vectors[...] = table
        for k in range(run.bias_rows):
            run.ff_bias[:, k * width : (k + 1) * width] = table[FF_ROW + k : FF_ROW + k + 1, :]

    if not fast:
        for k, weight in enumerate(weights):
            local(refs[masters[k]], refs[weight], 2 + k).start()
        spread_vectors(refs[Key.vector, 0][...])

    saved = [
        (Key.k_input, Key.w_input), (Key.k_output, Key.w_output), (Key.k_inner, Key.w_inner), (Key.k_outer, Key.w_outer),
        (Key.k_own, Key.own), (Key.k_other, Key.other), (Key.k_packed, Key.packed), (Key.k_pairs, Key.pairs_other),
        (Key.k_soft, Key.soft), (Key.k_context, Key.context), (Key.k_norm, Key.norm), (Key.k_inverse, Key.inverse),
        (Key.k_active, Key.active), (Key.k_slope, Key.slope), (Key.k_grad, Key.grad), (Key.k_vectors, Key.vectors), (Key.k_low, Key.soft),
        (Key.layer_out, Key.hidden),
    ]
    saves = {name: local(refs[src], refs[name], 6 + k) for k, (name, src) in enumerate(saved) if name in refs}
    started = []
    sent = []

    def save(name):
        if name in saves:
            saves[name].start()
            started.append(name)

    def step(what, *detail):
        if what == Key.event:
            if fast:
                gathers[detail[0], detail[1]].event(detail[2])
        elif what == Key.lay:
            if fast:
                lay(detail[0])
        elif what == Key.total:
            if fast:
                totals.advance(detail[0])
                if detail[0] + 1 == len(totals.steps):
                    spread_vectors(run.table[detail[0] + 1])
        elif what == Key.loaded:
            if not fast:
                k = weights.index(detail[0])
                local(refs[masters[k]], refs[detail[0]], 2 + k).wait()
        elif what == Key.frame:
            if detail[0] == 0:
                load_hidden.wait()
            run.frame_hidden(detail[0])
        elif what == Key.send:
            hidden_copy(detail[0]).start()
            sent.append(detail[0])
        elif what == Key.other:
            hidden_copy(detail[0]).wait_recv()
        elif what == Key.cot:
            if detail[0] == 0:
                load_cot.wait()
            run.frame_cotangent(detail[0])
        elif what == Key.save:
            save(detail[0])
        elif what == Key.saved:
            saves[detail[0]].wait()
            started.remove(detail[0])
        else:
            getattr(run, what.name)(*detail)

    run.gain_sum[...] = jnp.zeros_like(run.gain_sum)
    run.shift_sum[...] = jnp.zeros_like(run.shift_sum)
    run.low_sum[...] = jnp.zeros_like(run.low_sum)
    for entry in plan:
        step(*entry)
    run.k_sums[0:8, :] = run.gain_sum[...]
    run.k_sums[8:16, :] = run.shift_sum[...]
    run.k_sums[16:24, :] = run.low_sum[...]
    for r in sent:
        hidden_copy(r).wait_send()
    if fast:
        for gather in gathers.values():
            gather.drain()
        for k in range(4):
            swap(k).wait_send()
        totals.drain()
    for name in started:
        saves[name].wait()


def forward_plan(rows, units):
    plan = []
    for r in range(rows):
        plan += [(Key.frame, r), (Key.send, r)]
    for k in range(4):
        plan += [(Key.lay, k)]
    for n in range(5):
        plan += [(Key.total, n)]
    for r in range(rows):
        plan += [(Key.cot, r)]
    for w in (Key.w_input, Key.w_output, Key.w_inner, Key.w_outer):
        for e in range(5):
            plan += [(Key.event, w, 0, e)]
        plan += [(Key.loaded, w)]
    for part in range(3):
        plan += [(Key.project_own, part)]
    for r in range(rows):
        plan += [(Key.other, r), (Key.project_other, r, 0), (Key.project_other, r, 1)]
        plan += [(Key.attend_pairs, r), (Key.attend_padding, r), (Key.first_norm, r)]
    plan += [(Key.hidden_units, 0, units)]
    for r in range(rows):
        plan += [(Key.second_norm, r)]
    for name in (Key.layer_out, Key.k_input, Key.k_output, Key.k_inner, Key.k_outer, Key.k_own, Key.k_other, Key.k_packed, Key.k_pairs,
                 Key.k_soft, Key.k_context, Key.k_norm, Key.k_inverse, Key.k_active, Key.k_slope, Key.k_grad, Key.k_vectors):
        plan += [(Key.save, name)]
    return plan


def forward_call(mesh_rows, fast, hidden, cot, masters, small, lengths, routes, plan, with_saves=True):
    rows, slots, width = hidden.shape
    pairs = lengths.shape[2]
    tokens = rows * slots
    units = masters[2].shape[1]
    nz = mesh_rows // 4
    tall = [width, width, width, units]
    wide = [3 * width, width, units, width]
    if fast:
        shapes = [(2, nz, 2, tall[k] // (4 * nz), wide[k]) for k in range(4)]
    else:
        shapes = [(1, 1, 1, tall[k], wide[k]) for k in range(4)]
    weights = [Key.w_input, Key.w_output, Key.w_inner, Key.w_outer]
    ins = [Key.hidden_in, Key.cotangent, Key.m_input, Key.m_output, Key.m_inner, Key.m_outer]
    ins += [(Key.vector, k) for k in range(len(small))] + [Key.lengths]
    hbm, vmem, smem = (pl.BlockSpec(memory_space=s) for s in (pl.ANY, pltpu.VMEM, pltpu.SMEM))
    if fast:
        args = [hidden.reshape(tokens, width), cot.reshape(tokens, width), *masters, *small, lengths]
    else:
        args = [hidden.reshape(tokens, width), cot.reshape(tokens, width)]
        args += [m.reshape(s) for m, s in zip(masters, shapes, strict=True)] + [*small, lengths]
    in_specs = [hbm, hbm] + [vmem if fast else hbm] * 4 + [vmem] * len(small) + [smem]
    outs = {Key.layer_out: ((tokens, width), bf16), Key.k_sums: ((24, width), f32)}
    saved = {
        Key.k_input: (shapes[0], bf16), Key.k_output: (shapes[1], bf16), Key.k_inner: (shapes[2], bf16),
        Key.k_outer: (shapes[3], bf16), Key.k_own: ((tokens, width), bf16), Key.k_other: ((tokens, width), bf16),
        Key.k_packed: ((tokens, 3 * width), bf16), Key.k_pairs: ((tokens, 2 * width), bf16),
        Key.k_soft: ((tokens, width), bf16), Key.k_context: ((tokens, width), bf16),
        Key.k_norm: ((tokens, width), f32), Key.k_inverse: ((tokens, 128), f32),
        Key.k_active: ((tokens, units), bf16), Key.k_slope: ((tokens, units), bf16),
        Key.k_grad: ((tokens, width), f32), Key.k_low: ((tokens, width), bf16), Key.k_vectors: ((VECTORS, width), f32),
    }
    if with_saves:
        outs.update(saved)
    out_specs = [vmem if name == Key.k_sums else hbm for name in outs]
    scratch = {
        Key.w_input: pltpu.VMEM(shapes[0], bf16), Key.w_output: pltpu.VMEM(shapes[1], bf16),
        Key.w_inner: pltpu.VMEM(shapes[2], bf16), Key.w_outer: pltpu.VMEM(shapes[3], bf16),
        Key.hidden: pltpu.VMEM((tokens, width), bf16), Key.cot: pltpu.VMEM((tokens, width), bf16),
        Key.own: pltpu.VMEM((tokens, width), bf16), Key.other: pltpu.VMEM((tokens, width), bf16),
        Key.packed: pltpu.VMEM((tokens, 3 * width), bf16), Key.pairs_other: pltpu.VMEM((tokens, 2 * width), bf16),
        Key.context: pltpu.VMEM((tokens, width), bf16), Key.soft: pltpu.VMEM((tokens, width), bf16),
        Key.norm: pltpu.VMEM((tokens, width), f32), Key.inverse: pltpu.VMEM((tokens, 128), f32),
        Key.low: pltpu.VMEM((tokens, width), bf16), Key.active: pltpu.VMEM((tokens, units), bf16),
        Key.slope: pltpu.VMEM((tokens, units), bf16), Key.grad: pltpu.VMEM((tokens, width), f32),
        Key.sums: pltpu.VMEM((2, slots, width), f32), Key.framed: pltpu.VMEM((slots, width), bf16),
        Key.vectors: pltpu.VMEM((VECTORS, width), f32), Key.ff_bias: pltpu.VMEM((1, units), f32),
        Key.gain_sum: pltpu.VMEM((8, width), f32), Key.shift_sum: pltpu.VMEM((8, width), f32),
        Key.low_sum: pltpu.VMEM((8, width), f32),
        Key.local_sem: pltpu.SemaphoreType.DMA((6 + len(saved) + 1,)),
        Key.row_send: pltpu.SemaphoreType.DMA((rows,)), Key.row_recv: pltpu.SemaphoreType.DMA((rows,)),
    }
    if fast:
        steps, partners = 3, nz + 3
        pieces = sum(len(v) for v in routes.values())
        slots_each = nz + 1 + 1 + 2 * (nz - 1)
        scratch.update({
            Key.table: pltpu.VMEM((steps + 1, VECTORS, width), f32), Key.table_in: pltpu.VMEM((partners, VECTORS, width), f32),
            Key.table_send: pltpu.SemaphoreType.DMA((partners,)), Key.table_recv: pltpu.SemaphoreType.DMA((partners,)),
            Key.piece_send: pltpu.SemaphoreType.DMA((pieces, slots_each)),
            Key.piece_recv: pltpu.SemaphoreType.DMA((pieces, slots_each)),
            Key.swap_send: pltpu.SemaphoreType.DMA((4,)), Key.swap_recv: pltpu.SemaphoreType.DMA((4,)),
        })
        for k in range(4):
            scratch[Key.from_sibling, k] = pltpu.VMEM((masters[k].shape[0], wide[k] // 2), f32)
    names = ins + list(outs) + list(scratch)
    sizes = (rows, slots, width, pairs)
    body = functools.partial(forward_kernel, names, fast, sizes, routes, plan)
    found = pl.pallas_call(
        body,
        out_shape=[jax.ShapeDtypeStruct(*s) for s in outs.values()],
        in_specs=in_specs,
        out_specs=out_specs,
        scratch_shapes=list(scratch.values()),
        compiler_params=pltpu.CompilerParams(
            collective_id=0, has_side_effects=True, vmem_limit_bytes=FORWARD_VMEM
        ),
        name="forward",
    )(*args)
    return dict(zip(outs, found, strict=True))


class Scatter:
    def __init__(self, buf, place, swapped, landed, final, out, send, recv, routes, starts, width):
        self.buf, self.place, self.swapped, self.landed = buf, place, swapped, landed
        self.final, self.out, self.send, self.recv, self.routes = final, out, send, recv, routes
        self.starts, self.width = starts, width
        self.sizes = dict(zip("XZY", buf.shape[:3], strict=True))
        self.core_rows = buf.shape[3] // 2

    def cols(self, core):
        first, second = self.starts
        return pl.ds(pl.multiple_of(first + core * (second - first), 128), self.width)

    def remote(self, src, dst, slot, device):
        return pltpu.make_async_remote_copy(
            src_ref=src,
            dst_ref=dst,
            send_sem=self.send.at[slot],
            recv_sem=self.recv.at[slot],
            device_id=device,
            device_id_type=MESH,
        )

    def per_core(self, act):
        if self.routes[0] == self.routes[1]:
            act(self.routes[0])
            return
        for core in range(2):
            pl.when(self.place.c == core)(functools.partial(act, self.routes[core]))

    def lead(self, route, stage, at):
        own = {**self.place.own, **at}
        fixed = route[: stage + 1]
        return tuple(own[d] if d in fixed else ALL for d in "XZY")

    def swap(self):
        place = self.place
        src = self.buf.at[ALL, ALL, ALL, ALL, self.cols(1 - place.c)]
        return self.remote(src, self.swapped, 0, place.device(C=1 - place.c))

    def sends(self, route, stage):
        dim = route[stage]
        mine = self.landed.at[self.lead(route, stage, {})]
        found = []
        for k, peer in enumerate(self.place.peers(dim)):
            src = self.buf.at[self.lead(route, stage, {dim: peer}) + (ALL, self.cols(self.place.c))]
            found.append(self.remote(src, mine, 1 + self.place.first_slot(dim) + k, self.place.device(**{dim: peer})))
        return found

    def arrivals(self, route, stage):
        dim = route[stage]
        found = []
        for k, peer in enumerate(self.place.sources(dim)):
            view = self.landed.at[self.lead(route, stage, {dim: peer})]
            found.append(self.remote(view, view, 1 + self.place.first_slot(dim) + k, self.place.device()))
        return found

    def blocks(self, free, body):
        total = math.prod(self.sizes[d] for d in free)

        def visit(i):
            at = dict(self.place.own)
            for d in reversed(free):
                at[d] = i % self.sizes[d]
                i = i // self.sizes[d]
            body((at["X"], at["Z"], at["Y"]), at)

        if total == 1:
            visit(0)
        else:
            pl.loop(0, total)(visit)

    def start_swap(self):
        self.swap().start()

    def add_swapped(self):
        self.swap().wait_recv()
        cols = self.cols(self.place.c)

        def body(block, at):
            there = block + (ALL, cols)
            total = self.buf[there].astype(f32) + self.swapped[block].astype(f32)
            self.buf[there] = total.astype(bf16)

        self.blocks("XZY", body)

        def act(route):
            for copy in self.sends(route, 0):
                copy.start()

        self.per_core(act)

    def add_stage(self, stage):
        cols = self.cols(self.place.c)

        def act(route):
            dim = route[stage]
            for copy in self.arrivals(route, stage):
                copy.wait_recv()
            sources = self.place.sources(dim)

            def body(block, at):
                total = self.buf[block + (ALL, cols)].astype(f32)
                for peer in sources:
                    theirs = {**at, dim: peer}
                    total = total + self.landed[theirs["X"], theirs["Z"], theirs["Y"]].astype(f32)
                if stage < 2:
                    self.buf[block + (ALL, cols)] = total.astype(bf16)
                else:
                    self.final[...] = total

            self.blocks("".join(d for d in "XZY" if d not in route[: stage + 1]), body)
            if stage < 2:
                for copy in self.sends(route, stage + 1):
                    copy.start()

        self.per_core(act)
        if stage == 2:
            for copy in self.hand_over():
                copy.start()

    def hand_over(self):
        place, count = self.place, self.core_rows
        cols = self.cols(place.c)
        mine = self.final.at[pl.ds(pl.multiple_of(place.c * count, 8), count)]
        theirs = self.final.at[pl.ds(pl.multiple_of((1 - place.c) * count, 8), count)]
        there = self.remote(theirs, self.out.at[:, cols], 1 + place.slots(), place.device(C=1 - place.c))
        here = pltpu.make_async_copy(mine, self.out.at[:, cols], self.send.at[2 + place.slots()])
        return [there, here]

    def finish(self):
        there, here = self.hand_over()
        here.wait()
        there.wait_send()
        view = self.out.at[:, self.cols(1 - self.place.c)]
        self.remote(view, view, 1 + self.place.slots(), self.place.device()).wait_recv()

    def drain(self):
        self.swap().wait_send()

        def act(route):
            for stage in range(3):
                for copy in self.sends(route, stage):
                    copy.wait_send()

        self.per_core(act)

    def event(self, number):
        if number == 0:
            self.start_swap()
        elif number == 1:
            self.add_swapped()
        elif number < 5:
            self.add_stage(number - 2)
        else:
            self.finish()


class Backward:
    def __init__(self, refs, place, sizes):
        self.__dict__.update(attributes(refs))
        self.place = place
        self.rows, self.slots, self.width, self.pairs = sizes
        self.most = self.slots // self.pairs
        self.half = place.x
        self.scale = (self.width // HEADS) ** (-0.5)
        self.tokens = self.rows * self.slots
        self.units = self.active.shape[1]

    def sizes_of(self, row, half):
        return [self.lengths[row, half, p] for p in range(self.pairs)]

    def row(self, r):
        return pl.ds(r * self.slots, self.slots)

    def vector(self, at):
        return rounded(self.vectors[at : at + 1, :])

    def lower_norm(self):
        gain, shift = self.vector(GAIN_1), self.vector(SHIFT_1)

        @pl.loop(0, self.tokens // 64)
        def _(i):
            rows = block_rows(i, 64)
            self.low[rows, :] = (self.norm[rows, :] * gain + shift).astype(bf16)

    def grad_outer(self):
        nz = self.d_outer.shape[1]
        parts = self.d_outer.shape[0] * nz
        size = self.units // parts

        @pl.loop(0, parts)
        def _(i):
            found = contract(self.active[:, pl.ds(pl.multiple_of(i * size, 128), size)], self.grad_low[...], 0, 0)
            self.d_outer[i // nz, i % nz] = found.astype(bf16).reshape(self.d_outer.shape[2:])

    def grad_hidden(self, first, count, size=384):
        @pl.loop(first, first + count)
        def _(n):
            cols = pl.ds(pl.multiple_of(n * size, size), size)
            weight = self.w_outer[cols, :]
            total = jnp.zeros((8, size), f32)
            for r in range(self.rows):
                found = contract(self.grad_low[self.row(r), :], weight, 1, 1)
                low = (found * self.slope[self.row(r), cols].astype(f32)).astype(bf16)
                self.slope[self.row(r), cols] = low
                total = total + folded(low.astype(f32))
            self.ff_sums[:, cols] = total

    def grad_inner(self, core, part, size=768):
        half = self.units // 2
        cols = pl.ds(pl.multiple_of(core * half + part * size, 128), size)
        found = contract(self.low[...], self.slope[:, cols], 0, 0).astype(bf16)
        self.d_inner[:, :, :, :, cols] = found.reshape(self.d_inner.shape[:4] + (size,))

    def first_back(self, r):
        if r < self.rows:
            rows = self.row(r)
            weight = self.w_inner[...].reshape(self.width, self.units)
            self.grad[rows, :] = self.grad[rows, :] + contract(self.slope[rows, :], weight, 1, 1)
        if r == 0:
            for at in (GAIN_1, SHIFT_1, O_BIAS):
                self.col_sums[at] = jnp.zeros((8, self.width), f32)
            return
        gain = self.vector(GAIN_1)
        kinds = (GAIN_1, SHIFT_1, O_BIAS)
        sums = [self.col_sums[at] for at in kinds]
        for i in range(0, self.slots, 32):
            there = pl.ds((r - 1) * self.slots + i, 32)
            grad = self.grad[there, :]
            norm = self.norm[there, :]
            incoming = grad * gain
            plain = jnp.mean(incoming, axis=1, keepdims=True)
            along = jnp.mean(incoming * norm, axis=1, keepdims=True)
            attn = self.inverse[there, 0:1] * (incoming - plain - norm * along)
            self.grad[there, :] = attn
            low = attn.astype(bf16)
            self.grad_low[there, :] = low
            parts = (grad * norm, grad, low.astype(f32))
            sums = [total + folded(part) for total, part in zip(sums, parts, strict=True)]
        for at, total in zip(kinds, sums, strict=True):
            self.col_sums[at] = total

    def grad_output(self):
        context = self.w_outer[2 * self.tokens : 3 * self.tokens, :]
        found = contract(context, self.grad_low[...], 0, 0).astype(bf16)
        self.d_output[...] = found.reshape(self.d_output.shape)

    def grad_context(self, r):
        rows = self.row(r)
        weight = self.w_output[...].reshape(self.width, self.width)
        self.low[rows, :] = contract(self.grad_low[rows, :], weight, 1, 1).astype(bf16)

    def attend_back(self, r, together=4):
        most, span, width, wide = self.most, 4 * (self.width // HEADS), self.width, 2 * self.most
        spread = spread_heads(wide, span)
        first = iota((most, 4 * wide), 1) % wide < most

        def tiled(v):
            return jnp.where(spread, jnp.concatenate([v] * 4, axis=0), 0).astype(bf16)

        def two_pairs(pair):
            rows = pl.ds(pl.multiple_of(r * self.slots + pair * wide, wide), wide)
            for at in range(0, width, span):
                here = [slice(part * width + at, part * width + at + span) for part in range(4)]
                queries = tiled(self.active[rows, here[0]])
                keys = jnp.concatenate([self.active[rows, here[1]], self.slope[rows, here[0]]], axis=0)
                values = jnp.concatenate([self.active[rows, here[2]], self.slope[rows, here[1]]], axis=0)
                kept = self.active[rows, here[3]].astype(f32)
                mine, theirs = kept[:most], kept[most:]
                soft = jnp.concatenate(
                    [
                        jnp.where(first, mine, 0.0), jnp.where(first, 0.0, mine),
                        jnp.where(first, theirs, 0.0), jnp.where(first, 0.0, theirs),
                    ],
                    axis=0,
                )
                grad = tiled(self.low[rows, here[0]])
                grad_soft = contract(values, grad, 1, 1)
                delta = jnp.sum(soft * grad_soft, axis=0, keepdims=True)
                grad_scores = (soft * (grad_soft - delta)).astype(bf16)
                grad_values = contract(soft.astype(bf16), grad, 1, 0).astype(bf16)
                grad_keys = (contract(grad_scores, queries, 1, 0) * self.scale).astype(bf16)
                mixed = jnp.where(spread, contract(grad_scores, keys, 0, 0), 0.0)
                grad_queries = sum(mixed[h * wide : (h + 1) * wide, :] for h in range(4)) * self.scale
                self.active[rows, here[0]] = grad_queries.astype(bf16)
                self.active[rows, here[1]] = grad_keys[:wide]
                self.active[rows, here[2]] = grad_values[:wide]
                self.slope[rows, here[0]] = grad_keys[wide:]
                self.slope[rows, here[1]] = grad_values[wide:]

        @pl.loop(0, self.pairs // (2 * together))
        def _(several):
            for k in range(together):
                two_pairs(several * together + k)

    def input_weight(self, first, last):
        weight = self.w_inner[:, :, :, :, first:last] if self.fast else self.w_input[:, :, :, :, first:last]
        return weight.reshape(self.width, last - first)

    def return_other(self, r):
        rows = self.row(r)
        weight = self.input_weight(self.width, 3 * self.width)
        self.grad_low[rows, :] = contract(self.slope[rows, : 2 * self.width], weight, 1, 1).astype(bf16)

    def token_sums(self):
        width = self.width
        self.col_sums[Q_BIAS] = jnp.zeros((8, width), f32)
        self.col_sums[V_BIAS] = jnp.zeros((8, width), f32)

        @pl.loop(0, self.tokens // 64)
        def _(i):
            rows = block_rows(i, 64)
            self.col_sums[Q_BIAS] += folded(self.active[rows, :width].astype(f32))
            both = self.active[rows, 2 * width : 3 * width].astype(f32) + self.slope[rows, width : 2 * width].astype(f32)
            self.col_sums[V_BIAS] += folded(both)

        self.col_sums[GAIN_2] = self.k_sums[0:8, :]
        self.col_sums[SHIFT_2] = self.k_sums[8:16, :]
        self.col_sums[OUT_BIAS] = self.k_sums[16:24, :]
        rows = [jnp.sum(self.col_sums[at], axis=0, keepdims=True) for at in range(8)]
        units = jnp.sum(self.ff_sums[...], axis=0, keepdims=True)
        count = self.units // width
        rows += [units[:, k * width : (k + 1) * width] for k in range(count)]
        rows += [jnp.zeros((VECTORS - 8 - count, width), f32)]
        self.table[0] = jnp.concatenate(rows, axis=0)

    def grad_input_weight(self, part):
        width = self.width
        cols = pl.ds(pl.multiple_of(part * width, 128), width)
        target = self.d_inner

        def keep(found):
            target[:, :, :, :, cols] = found.astype(bf16).reshape(target.shape[:4] + (width,))

        if isinstance(part, int) and part == 0:
            keep(contract(self.w_outer[: self.tokens, :], self.active[:, :width], 0, 0))
            return
        there = pl.ds(pl.multiple_of((part - 1) * width, 128), width)
        found = contract(self.w_outer[: self.tokens, :], self.active[:, cols], 0, 0)
        keep(found + contract(self.w_outer[self.tokens : 2 * self.tokens, :], self.slope[:, there], 0, 0))

    def grad_hidden_in(self, r):
        rows = self.row(r)
        found = contract(self.active[rows, : 3 * self.width], self.input_weight(0, 3 * self.width), 1, 1)
        found = found + self.grad[rows, :] + self.back[rows, :].astype(f32)
        high = found.astype(bf16)
        rest = (found - high.astype(f32)).astype(bf16)
        back = out_of_frames(self.sizes_of(r, self.half), self.slots, self.most)
        self.norm[rows, :] = contract(back, high, 1, 0) + contract(back, rest, 1, 0)


BACKWARD_VMEM = 127 * 2**19


def backward_kernel(names, fast, sizes, routes, plan, *refs):
    refs = dict(zip(names, refs, strict=True))
    rows, slots, width, pairs = sizes
    tokens = rows * slots
    place = Place(lax.axis_size("rows"))
    run = Backward(refs, place, sizes)
    run.fast = fast
    partner = place.device(X=1 - place.x)
    in_outer = [run.w_outer.at[pl.ds(k * tokens, tokens)] for k in range(3)]
    loads = {
        Key.grad: (run.k_grad, run.grad), Key.low: (run.k_low, run.grad_low), Key.active: (run.k_active, run.active), Key.outer: (run.k_outer, run.w_outer),
        Key.slope: (run.k_slope, run.slope), Key.norm: (run.k_norm, run.norm), Key.inner: (run.k_inner, run.w_inner),
        Key.inverse: (run.k_inverse, run.inverse), Key.output: (run.k_output, run.w_output),
        Key.vectors: (run.k_vectors, run.vectors),
        Key.packed: (run.k_packed, run.active.at[:, pl.ds(0, 3 * width)]),
        Key.soft: (run.k_soft, run.active.at[:, pl.ds(3 * width, width)]),
        Key.pairs: (run.k_pairs, run.slope.at[:, pl.ds(0, 2 * width)]),
        Key.own: (run.k_own, in_outer[0]), Key.other: (run.k_other, in_outer[1]), Key.context: (run.k_context, in_outer[2]),
        Key.input: (run.k_input, run.w_inner.at[:, :, :, :, pl.ds(0, 3 * width)] if fast else run.w_input),
    }
    order = {name: k for k, name in enumerate(loads)}

    def load(name):
        return pltpu.make_async_copy(*loads[name], run.local_sem.at[order[name]])

    scatters = {}
    for name in (Key.low, Key.active):
        load(name).start()
    if fast:
        greet(place, neighbours(place))
        totals = Totals(place, run.table, run.table_in, run.table_send, run.table_recv)
        targets = {Key.outer: run.d_outer, Key.inner: run.d_inner, Key.output: run.d_output, Key.input: run.d_inner}
        for name, pieces in routes.items():
            for j, (route, starts, span) in enumerate(pieces):
                at = len(scatters)
                scatters[name, j] = Scatter(
                    targets[name], place, refs[Key.swapped, name, j], refs[Key.landed, name, j],
                    refs[Key.final, name, j], refs["g", name], run.piece_send.at[at], run.piece_recv.at[at],
                    route, starts, span,
                )
    else:
        greet(place, [partner])

    def returned(r):
        view = pl.ds(r * slots, slots)
        return pltpu.make_async_remote_copy(
            src_ref=run.grad_low.at[view],
            dst_ref=run.back.at[view],
            send_sem=run.row_send.at[r],
            recv_sem=run.row_recv.at[r],
            device_id=partner,
            device_id_type=MESH,
        )

    def put(r):
        view = pl.ds(r * slots, slots)
        return pltpu.make_async_copy(run.norm.at[view], run.grad_input.at[view], run.out_sem.at[r])

    whole = {Key.outer: Key.d_outer, Key.inner: Key.d_inner, Key.output: Key.d_output, Key.input: Key.d_inner}

    def keep(name):
        src = refs[whole[name]]
        if name == Key.input:
            src = src.at[:, :, :, :, pl.ds(0, 3 * width)]
        return pltpu.make_async_copy(src, refs["g", name], run.keep_sem.at[list(whole).index(name)])

    sent, written, summed = [], [], []

    def step(what, *detail):
        if what == Key.load:
            load(detail[0]).start()
        elif what == Key.loaded:
            load(detail[0]).wait()
        elif what == Key.event:
            if fast:
                scatters[detail[0], detail[1]].event(detail[2])
        elif what == Key.drain:
            if fast:
                for (name, _), scatter in scatters.items():
                    if name == detail[0]:
                        scatter.drain()
            else:
                keep(detail[0]).wait()
        elif what == Key.keep:
            if not fast:
                keep(detail[0]).start()
        elif what == Key.grad_inner:
            core = 1 - place.c if detail[0] == 0 else place.c
            run.grad_inner(core, *detail[1:])
        elif what == Key.grad_input_weight:
            run.grad_input_weight(detail[0])
        elif what == Key.send:
            returned(detail[0]).start()
            sent.append(detail[0])
        elif what == Key.back:
            returned(detail[0]).wait_recv()
        elif what == Key.total:
            if not fast:
                return
            if detail[0] < 0:
                totals.start(0)
                summed.append(True)
            else:
                totals.advance(detail[0])
        elif what == Key.put:
            put(detail[0]).start()
            written.append(detail[0])
        else:
            getattr(run, what.name)(*detail)

    for entry in plan:
        step(*entry)
    for r in sent:
        returned(r).wait_send()
    for r in written:
        put(r).wait()
    if fast:
        if summed: totals.drain()
        table = run.table[len(totals.steps)]
        devices = 2 * lax.axis_size("rows")
        piece = width // devices
        wide = piece * (run.units // width)
        per_row = width // wide
        upper = pltpu.roll(table[:8], (devices - place.index) * piece % width, axis=1)
        lower = jnp.where(iota((8, width), 0) == place.index // per_row, table[8:], 0.0)
        lower = jnp.sum(lower, axis=0, keepdims=True)
        lower = pltpu.roll(jnp.broadcast_to(lower, (8, width)), (per_row - place.index % per_row) * wide % width, axis=1)
        run.g_small[...] = jnp.concatenate([upper[:, :128], lower[:, :128]], axis=0)
    else:
        run.g_small[...] = run.table[0]


def backward_call(mesh_rows, fast, kept, lengths, routes, plan, sizes, units):
    rows, slots, width, pairs = sizes
    tokens = rows * slots
    nz = mesh_rows // 4
    hbm, vmem, smem = (pl.BlockSpec(memory_space=s) for s in (pl.ANY, pltpu.VMEM, pltpu.SMEM))
    ins = [
        Key.k_input, Key.k_output, Key.k_inner, Key.k_outer, Key.k_own, Key.k_other, Key.k_packed, Key.k_pairs, Key.k_soft, Key.k_context,
        Key.k_norm, Key.k_inverse, Key.k_active, Key.k_slope, Key.k_grad, Key.k_vectors, Key.k_low,
    ]
    kept = dict(kept)
    kept[Key.k_outer] = kept[Key.k_outer].reshape(units, width)
    args = [kept[name] for name in ins] + [kept[Key.k_sums], lengths]
    in_specs = [hbm] * len(ins) + [vmem, smem]
    tall = {Key.outer: units, Key.inner: width, Key.output: width, Key.input: width}
    wide = {Key.outer: width, Key.inner: units, Key.output: width, Key.input: 3 * width}
    lead = (2, nz, 2) if fast else (1, 1, 1)
    blocks = math.prod(lead)
    outs = {Key.grad_input: ((tokens, width), f32)}
    for name in tall:
        if fast:
            outs["g", name] = ((tall[name] // (2 * blocks), wide[name]), f32)
        else:
            outs["g", name] = (lead + (tall[name], wide[name]), bf16)
    outs[Key.g_small] = ((VECTORS, 128 if fast else width), f32)
    out_specs = [vmem if name == Key.g_small else hbm for name in outs]
    steps, partners = (3, nz + 3) if fast else (0, 0)
    scratch = {
        Key.w_outer: pltpu.VMEM((units, width), bf16), Key.w_inner: pltpu.VMEM(lead + (width // blocks, units), bf16),
        Key.w_output: pltpu.VMEM(lead + (width // blocks, width), bf16),
        Key.active: pltpu.VMEM((tokens, units), bf16), Key.slope: pltpu.VMEM((tokens, units), bf16),
        Key.grad: pltpu.VMEM((tokens, width), f32), Key.norm: pltpu.VMEM((tokens, width), f32),
        Key.inverse: pltpu.VMEM((tokens, 128), f32), Key.vectors: pltpu.VMEM((VECTORS, width), f32),
        Key.grad_low: pltpu.VMEM((tokens, width), bf16), Key.low: pltpu.VMEM((tokens, width), bf16),
        Key.back: pltpu.VMEM((tokens, width), bf16),
        Key.col_sums: pltpu.VMEM((8, 8, width), f32),
        Key.ff_sums: pltpu.VMEM((8, units), f32),
        Key.d_outer: pltpu.VMEM(lead + (units // blocks, width), bf16),
        Key.d_inner: pltpu.VMEM(lead + (width // blocks, units), bf16),
        Key.d_output: pltpu.VMEM(lead + (width // blocks, width), bf16),
        Key.table: pltpu.VMEM((steps + 1, VECTORS, width), f32),
        Key.local_sem: pltpu.SemaphoreType.DMA((17,)), Key.out_sem: pltpu.SemaphoreType.DMA((rows,)),
        Key.row_send: pltpu.SemaphoreType.DMA((rows,)), Key.row_recv: pltpu.SemaphoreType.DMA((rows,)),
    }
    if fast:
        pieces = sum(len(v) for v in routes.values())
        scratch.update({
            Key.table_in: pltpu.VMEM((partners, VECTORS, width), f32),
            Key.table_send: pltpu.SemaphoreType.DMA((partners,)), Key.table_recv: pltpu.SemaphoreType.DMA((partners,)),
            Key.piece_send: pltpu.SemaphoreType.DMA((pieces, nz + 4)),
            Key.piece_recv: pltpu.SemaphoreType.DMA((pieces, nz + 4)),
        })
        for name, found in routes.items():
            height = tall[name] // blocks
            for j, (_, _, span) in enumerate(found):
                scratch[Key.swapped, name, j] = pltpu.VMEM(lead + (height, span), bf16)
                scratch[Key.landed, name, j] = pltpu.VMEM(lead + (height, span), bf16)
                scratch[Key.final, name, j] = pltpu.VMEM((height, span), f32)
    else:
        scratch[Key.w_input] = pltpu.VMEM(lead + (width, 3 * width), bf16)
        scratch[Key.keep_sem] = pltpu.SemaphoreType.DMA((4,))
    names = ins + [Key.k_sums, Key.lengths] + list(outs) + list(scratch)
    found = pl.pallas_call(
        functools.partial(backward_kernel, names, fast, sizes, routes, plan),
        out_shape=[jax.ShapeDtypeStruct(*s) for s in outs.values()],
        in_specs=in_specs,
        out_specs=out_specs,
        scratch_shapes=list(scratch.values()),
        compiler_params=pltpu.CompilerParams(
            collective_id=1, has_side_effects=True, vmem_limit_bytes=BACKWARD_VMEM
        ),
        name="backward",
    )(*args)
    return dict(zip(outs, found, strict=True))


def plain_forward(rows, units):
    plan = []
    for r in range(rows):
        plan += [(Key.frame, r), (Key.send, r), (Key.cot, r)]
    plan += [(Key.loaded, Key.w_input), (Key.save, Key.k_vectors)]
    plan += [(Key.project_own, part) for part in range(3)] + [(Key.loaded, Key.w_output)]
    for r in range(rows):
        plan += [(Key.other, r), (Key.project_other, r, 0), (Key.project_other, r, 1)]
        plan += [(Key.attend_pairs, r), (Key.attend_padding, r)]
    plan += [(Key.first_norm, r) for r in range(rows + 1)]
    plan += [(Key.loaded, Key.w_inner), (Key.hidden_units, 0, units // 256), (Key.loaded, Key.w_outer)]
    plan += [(Key.save, Key.k_soft), (Key.saved, Key.k_soft)] + [(Key.second_norm, r) for r in range(rows + 1)]
    saved = (Key.layer_out, Key.k_input, Key.k_output, Key.k_inner, Key.k_outer, Key.k_own, Key.k_other, Key.k_packed, Key.k_pairs)
    saved += (Key.k_context, Key.k_norm, Key.k_inverse, Key.k_active, Key.k_slope, Key.k_grad, Key.k_low)
    return plan + [(Key.save, name) for name in saved]


def plain_backward(rows, units):
    first = (Key.vectors, Key.grad, Key.outer, Key.slope, Key.norm, Key.inner, Key.inverse, Key.output)
    plan = [(Key.load, name) for name in first] + [(Key.loaded, name) for name in first + (Key.low, Key.active)]
    plan += [(Key.lower_norm,), (Key.grad_outer,)]
    plan += [(Key.grad_hidden, 0, units // 384), (Key.keep, Key.outer)]
    plan += [(Key.grad_inner, core, part) for core in range(2) for part in range(units // 1536)] + [(Key.keep, Key.inner)]
    plan += [(Key.load, name) for name in (Key.own, Key.other, Key.context, Key.packed, Key.soft)]
    plan += [(Key.first_back, r) for r in range(rows + 1)]
    plan += [(Key.load, Key.pairs), (Key.load, Key.input)]
    plan += [(Key.loaded, name) for name in (Key.own, Key.other, Key.context, Key.packed, Key.soft, Key.pairs, Key.input)]
    plan += [(Key.grad_output,), (Key.keep, Key.output)]
    plan += [(Key.grad_context, r) for r in range(rows)] + [(Key.drain, Key.inner)]
    for r in range(rows):
        plan += [(Key.attend_back, r), (Key.return_other, r), (Key.send, r)]
    plan += [(Key.token_sums,)] + [(Key.grad_input_weight, part) for part in range(3)]
    plan += [(Key.keep, Key.input)]
    for r in range(rows):
        plan += [(Key.back, r), (Key.grad_hidden_in, r), (Key.put, r)]
    return plan + [(Key.drain, Key.outer), (Key.drain, Key.output), (Key.drain, Key.input)]


GATHER = {
    Key.w_input: (
        (("XZY", "ZXY"), 0, 640, 0, 48),
        (("ZXY", "XZY"), 640, 512, 0, 48),
    ),
    Key.w_output: (
        (("ZXY", "XZY"), 0, 384, 0, 48),
    ),
    Key.w_inner: (
        (("ZXY", "YZX"), 0, 768, 0, 48),
        (("XZY", "ZXY"), 768, 768, 0, 48),
    ),
    Key.w_outer: (
        (("YXZ", "ZYX"), 0, 384, 0, 96),
        (("YZX", "XZY"), 0, 384, 96, 96),
    ),
}
SCATTER = {
    Key.outer: (
        (("XYZ", "ZXY"), (0, 512), 256),
        (("YXZ", "YZX"), (256, 384), 128),
    ),
    Key.inner: (
        (("YZX", "XYZ"), (0, 1536), 768),
        (("XZY", "YXZ"), (768, 2304), 768),
    ),
    Key.output: (
        (("XZY", "YZX"), (0, 384), 384),
    ),
    Key.input: (
        (("ZYX", "YXZ"), (0, 1536), 768),
        (("YZX", "YXZ"), (768, 1152), 384),
    ),
}
FORWARD_PLAN = (
    (Key.lay, 0), (Key.event, Key.w_input, 1, 0), (Key.event, Key.w_input, 0, 0), (Key.frame, 0), (Key.frame, 1),
    (Key.frame, 2), (Key.frame, 3), (Key.lay, 1), (Key.lay, 2), (Key.lay, 3), (Key.cot, 0), (Key.cot, 1), (Key.total, 0),
    (Key.cot, 2), (Key.cot, 3), (Key.event, Key.w_input, 1, 1), (Key.event, Key.w_output, 0, 0),
    (Key.event, Key.w_input, 0, 1), (Key.total, 1), (Key.send, 1), (Key.event, Key.w_input, 1, 2),
    (Key.event, Key.w_inner, 1, 0), (Key.event, Key.w_output, 0, 1), (Key.event, Key.w_input, 0, 2), (Key.send, 0),
    (Key.event, Key.w_input, 1, 3), (Key.event, Key.w_input, 1, 4), (Key.event, Key.w_inner, 0, 0),
    (Key.event, Key.w_outer, 0, 0), (Key.total, 2), (Key.event, Key.w_inner, 1, 1), (Key.event, Key.w_outer, 1, 0),
    (Key.send, 2), (Key.event, Key.w_output, 0, 2), (Key.event, Key.w_input, 0, 3), (Key.event, Key.w_inner, 0, 1),
    (Key.event, Key.w_input, 0, 4), (Key.save, Key.k_input), (Key.save, Key.k_own), (Key.project_own, 0),
    (Key.event, Key.w_outer, 1, 1), (Key.event, Key.w_outer, 0, 1), (Key.send, 3), (Key.project_own, 1),
    (Key.project_own, 2), (Key.save, Key.k_packed), (Key.save, Key.k_vectors), (Key.other, 0), (Key.project_other, 0, 0),
    (Key.project_other, 0, 1), (Key.attend_pairs, 0), (Key.event, Key.w_output, 0, 3), (Key.event, Key.w_inner, 1, 2),
    (Key.attend_padding, 0), (Key.event, Key.w_output, 0, 4), (Key.save, Key.k_output), (Key.other, 1),
    (Key.project_other, 1, 0), (Key.project_other, 1, 1), (Key.attend_pairs, 1), (Key.attend_padding, 1),
    (Key.event, Key.w_inner, 0, 2), (Key.event, Key.w_outer, 0, 2), (Key.other, 2), (Key.project_other, 2, 0),
    (Key.project_other, 2, 1), (Key.attend_pairs, 2), (Key.attend_padding, 2), (Key.other, 3),
    (Key.project_other, 3, 0), (Key.project_other, 3, 1), (Key.save, Key.k_pairs), (Key.save, Key.k_other),
    (Key.event, Key.w_inner, 1, 3), (Key.attend_pairs, 3), (Key.save, Key.k_soft), (Key.attend_padding, 3),
    (Key.save, Key.k_context), (Key.event, Key.w_outer, 1, 2), (Key.event, Key.w_inner, 1, 4), (Key.first_norm, 0),
    (Key.first_norm, 1), (Key.first_norm, 2), (Key.first_norm, 3), (Key.first_norm, 4), (Key.save, Key.k_norm),
    (Key.save, Key.k_inverse), (Key.event, Key.w_inner, 0, 3), (Key.event, Key.w_inner, 0, 4), (Key.save, Key.k_inner),
    (Key.hidden_units, 0, 2), (Key.hidden_units, 2, 2), (Key.hidden_units, 4, 2), (Key.hidden_units, 6, 2),
    (Key.hidden_units, 8, 2), (Key.event, Key.w_outer, 0, 3), (Key.hidden_units, 10, 2), (Key.save, Key.k_active),
    (Key.save, Key.k_slope), (Key.event, Key.w_outer, 1, 3), (Key.event, Key.w_outer, 0, 4), (Key.event, Key.w_outer, 1, 4),
    (Key.save, Key.k_outer), (Key.saved, Key.k_soft), (Key.second_norm, 0), (Key.second_norm, 1), (Key.second_norm, 2),
    (Key.second_norm, 3), (Key.second_norm, 4), (Key.save, Key.layer_out), (Key.save, Key.k_grad), (Key.save, Key.k_low),
)
BACKWARD_PLAN = (
    (Key.loaded, Key.low), (Key.loaded, Key.active), (Key.load, Key.outer), (Key.load, Key.slope), (Key.load, Key.vectors),
    (Key.load, Key.norm), (Key.load, Key.inner), (Key.load, Key.grad), (Key.load, Key.inverse), (Key.load, Key.output),
    (Key.grad_outer,), (Key.event, Key.outer, 0, 0), (Key.loaded, Key.outer), (Key.loaded, Key.slope),
    (Key.loaded, Key.vectors), (Key.load, Key.packed), (Key.load, Key.soft), (Key.grad_hidden, 0, 2),
    (Key.grad_hidden, 2, 2), (Key.grad_hidden, 4, 2), (Key.event, Key.outer, 0, 1), (Key.grad_hidden, 6, 2),
    (Key.load, Key.own), (Key.load, Key.other), (Key.load, Key.context), (Key.loaded, Key.norm), (Key.lower_norm,),
    (Key.grad_inner, 0, 0), (Key.event, Key.inner, 0, 0), (Key.grad_inner, 1, 0), (Key.grad_inner, 0, 1),
    (Key.event, Key.inner, 1, 0), (Key.event, Key.inner, 0, 1), (Key.grad_inner, 1, 1), (Key.loaded, Key.inner),
    (Key.loaded, Key.inverse), (Key.loaded, Key.grad), (Key.first_back, 0), (Key.event, Key.inner, 1, 1),
    (Key.first_back, 1), (Key.first_back, 2), (Key.event, Key.outer, 1, 0), (Key.first_back, 3), (Key.first_back, 4),
    (Key.load, Key.pairs), (Key.load, Key.input), (Key.loaded, Key.context), (Key.loaded, Key.output), (Key.grad_output,),
    (Key.event, Key.output, 0, 0), (Key.event, Key.inner, 0, 2), (Key.event, Key.outer, 1, 1), (Key.event, Key.outer, 0, 2),
    (Key.event, Key.output, 0, 1), (Key.grad_context, 0), (Key.grad_context, 1), (Key.grad_context, 2),
    (Key.grad_context, 3), (Key.loaded, Key.packed), (Key.loaded, Key.soft), (Key.loaded, Key.pairs), (Key.loaded, Key.input),
    (Key.attend_back, 0), (Key.event, Key.inner, 1, 2), (Key.return_other, 0), (Key.send, 0), (Key.attend_back, 1),
    (Key.event, Key.inner, 0, 3), (Key.return_other, 1), (Key.send, 1), (Key.attend_back, 2), (Key.return_other, 2),
    (Key.send, 2), (Key.attend_back, 3), (Key.event, Key.inner, 1, 3), (Key.event, Key.outer, 1, 2), (Key.return_other, 3),
    (Key.send, 3), (Key.token_sums,), (Key.total, -1), (Key.loaded, Key.own), (Key.loaded, Key.other),
    (Key.event, Key.outer, 0, 3), (Key.event, Key.inner, 0, 4), (Key.event, Key.output, 0, 2), (Key.total, 0),
    (Key.event, Key.inner, 1, 4), (Key.event, Key.inner, 0, 5), (Key.drain, Key.inner), (Key.grad_input_weight, 0),
    (Key.event, Key.inner, 1, 5), (Key.grad_input_weight, 2), (Key.event, Key.input, 0, 0), (Key.grad_input_weight, 1),
    (Key.event, Key.input, 1, 0), (Key.event, Key.input, 0, 1), (Key.event, Key.outer, 0, 4), (Key.event, Key.input, 1, 1),
    (Key.back, 0), (Key.grad_hidden_in, 0), (Key.put, 0), (Key.event, Key.outer, 0, 5), (Key.back, 1),
    (Key.grad_hidden_in, 1), (Key.put, 1), (Key.event, Key.output, 0, 3), (Key.event, Key.outer, 1, 3), (Key.back, 2),
    (Key.grad_hidden_in, 2), (Key.put, 2), (Key.back, 3), (Key.grad_hidden_in, 3), (Key.put, 3),
    (Key.event, Key.input, 1, 2), (Key.event, Key.input, 0, 2), (Key.event, Key.output, 0, 4), (Key.total, 1),
    (Key.event, Key.outer, 1, 4), (Key.event, Key.output, 0, 5), (Key.event, Key.outer, 1, 5), (Key.event, Key.input, 1, 3),
    (Key.event, Key.input, 0, 3), (Key.event, Key.input, 1, 4), (Key.total, 2), (Key.event, Key.input, 1, 5),
    (Key.event, Key.input, 0, 4), (Key.event, Key.input, 0, 5), (Key.drain, Key.outer), (Key.drain, Key.output),
    (Key.drain, Key.input),
)


def gather_routes(masters):
    return {
        name: [(route, (row, count), (col, span)) for route, col, span, row, count in found]
        for name, found in GATHER.items()
    }


def scatter_routes(width, units):
    return SCATTER


def forward_steps(rows, nz, units):
    return FORWARD_PLAN


def backward_steps(rows, nz):
    return BACKWARD_PLAN


def spread(masters, vectors):
    gathered = [lax.all_gather(v.astype(bf16), ("pair", "rows"), axis=0, tiled=True) for v in masters]
    rows = [lax.all_gather(v, ("pair", "rows"), axis=0, tiled=True) for v in vectors]
    width = rows[0].shape[0]
    table = jnp.concatenate(rows).reshape(-1, width)
    return gathered, [jnp.pad(table, ((0, VECTORS - table.shape[0]), (0, 0)))]


def gather_sums(found, units):
    def summed(v):
        return lax.psum_scatter(v.astype(f32), ("pair", "rows"), scatter_dimension=0, tiled=True)

    weights = {name: summed(found[name].reshape(found[name].shape[3:])) for name in found if name != Key.g_small}
    table = found[Key.g_small]
    width = table.shape[1]
    small = [summed(table[k]) for k in range(8)] + [summed(table[8 : 8 + units // width].reshape(units))]
    return weights, small


def settle(arrays):
    def kernel(*refs):
        count = len(refs) // 2
        copies = [
            pltpu.make_async_copy(refs[k], refs[count + k], refs[-1].at[k]) for k in range(count)
        ]
        for copy in copies:
            copy.start()
        for copy in copies:
            copy.wait()

    return pl.pallas_call(
        kernel,
        out_shape=[jax.ShapeDtypeStruct(v.shape, v.dtype) for v in arrays],
        in_specs=[pl.BlockSpec(memory_space=pl.ANY)] * len(arrays),
        out_specs=[pl.BlockSpec(memory_space=pl.ANY)] * len(arrays),
        scratch_shapes=[pltpu.SemaphoreType.DMA((len(arrays),))],
        compiler_params=pltpu.CompilerParams(vmem_limit_bytes=2**22),
        name="k_settle",
    )(*arrays)


def shards(rows_axis, *args):
    (
        hidden_in, input_proj, query_bias, value_bias, output_proj, output_bias, first_gain, first_shift,
        inner_proj, inner_bias, outer_proj, outer_bias, second_gain, second_shift, cotangent, pair_lengths,
    ) = args
    row_count, _, slots, width = hidden_in.shape
    units = inner_proj.shape[1]
    share = input_proj.shape[0]
    fast = rows_axis % 4 == 0 and share % 8 == 0
    masters = (input_proj, output_proj, inner_proj, outer_proj)
    vectors = (
        query_bias, value_bias, output_bias, first_gain, first_shift, outer_bias, second_gain, second_shift,
        inner_bias,
    )
    if fast:
        routes_f, plan_f = gather_routes(masters), forward_steps(row_count, rows_axis // 4, units)
        routes_b, plan_b = scatter_routes(width, units), backward_steps(row_count, rows_axis // 4)
        small = [v.reshape(1, -1) for v in vectors]
    else:
        routes_f, routes_b = {}, {}
        plan_f, plan_b = plain_forward(row_count, units), plain_backward(row_count, units)
        masters, small = spread(masters, vectors)
    sizes = (row_count, slots, width, pair_lengths.shape[2])
    kept = forward_call(
        rows_axis, fast, hidden_in[:, 0], cotangent[:, 0], masters, small, pair_lengths, routes_f, plan_f
    )
    found = backward_call(rows_axis, fast, kept, pair_lengths, routes_b, plan_b, sizes, units)
    layer_out, grad_input = kept[Key.layer_out], found.pop(Key.grad_input)
    if fast:
        weights = (Key.input, Key.output, Key.inner, Key.outer)
        results = settle([layer_out, grad_input] + [found["g", name] for name in weights])
        layer_out, grad_input = results[:2]
        found.update(zip([("g", name) for name in weights], results[2:], strict=True))
        table = found[Key.g_small]
        sums = [table[k, :share] for k in range(8)] + [table[8, : inner_bias.shape[0]]]
    else:
        found, sums = gather_sums(found, units)
    return (
        layer_out.reshape(hidden_in.shape), grad_input.reshape(hidden_in.shape), found["g", Key.input], sums[Q_BIAS], sums[V_BIAS], found["g", Key.output], sums[O_BIAS],
        sums[GAIN_1], sums[SHIFT_1], found["g", Key.inner], sums[FF_ROW], found["g", Key.outer], sums[OUT_BIAS],
        sums[GAIN_2], sums[SHIFT_2],
    )


def solution(mesh):
    tokens = P("rows", "pair", None, None)
    matrix = P(("pair", "rows"), None)
    vector = P(("pair", "rows"))
    weights = (
        matrix, vector, vector, matrix, vector, vector, vector, matrix, vector, matrix, vector, vector, vector
    )
    return jax.shard_map(
        functools.partial(shards, mesh.shape["rows"]),
        mesh=mesh,
        in_specs=(tokens, *weights, tokens, P("rows", None, None)),
        out_specs=(tokens, tokens, *weights),
        check_vma=False,
    )
```

```python
import enum
import functools
import math

import jax
import jax.numpy as jnp
from jax import lax
from jax.experimental import pallas as pl
from jax.experimental.pallas import tpu as pltpu
from jax.sharding import PartitionSpec as P

HEADS = 12
EPSILON = 1e-12
MESH = pl.DeviceIdType.MESH
bf16 = jnp.bfloat16
f32 = jnp.float32
ALL = slice(None)
MASKED = -1e30
VECTORS = 16
Q_BIAS, V_BIAS, O_BIAS, GAIN_1, SHIFT_1, OUT_BIAS, GAIN_2, SHIFT_2, FF_ROW = range(9)


def contract(left, right, left_dim, right_dim):
    return lax.dot_general(
        left, right, (((left_dim,), (right_dim,)), ((), ())), preferred_element_type=f32
    )


def iota(shape, dim):
    return lax.broadcasted_iota(jnp.int32, shape, dim)


def rounded(v):
    return v.astype(bf16).astype(f32)


class Key(enum.Enum):
    active = 0
    attend_back = 1
    attend_padding = 2
    attend_pairs = 3
    back = 4
    col_sums = 5
    context = 6
    cot = 7
    cotangent = 8
    d_inner = 9
    d_outer = 10
    d_output = 11
    drain = 12
    event = 13
    ff_bias = 14
    ff_sums = 15
    final = 16
    first_back = 17
    first_norm = 18
    frame = 19
    framed = 20
    from_sibling = 21
    g_small = 22
    gain_sum = 23
    grad = 24
    grad_context = 25
    grad_hidden = 26
    grad_hidden_in = 27
    grad_inner = 28
    grad_input = 29
    grad_input_weight = 30
    grad_low = 31
    grad_outer = 32
    grad_output = 33
    hidden = 34
    hidden_in = 35
    hidden_units = 36
    inner = 37
    input = 38
    inverse = 39
    k_active = 40
    k_context = 41
    k_grad = 42
    k_inner = 43
    k_input = 44
    k_inverse = 45
    k_low = 46
    k_norm = 47
    k_other = 48
    k_outer = 49
    k_output = 50
    k_own = 51
    k_packed = 52
    k_pairs = 53
    k_slope = 54
    k_soft = 55
    k_sums = 56
    k_vectors = 57
    keep = 58
    keep_sem = 59
    landed = 60
    lay = 61
    layer_out = 62
    lengths = 63
    load = 64
    loaded = 65
    local_sem = 66
    low = 67
    low_sum = 68
    lower_norm = 69
    m_inner = 70
    m_input = 71
    m_outer = 72
    m_output = 73
    norm = 74
    other = 75
    out_sem = 76
    outer = 77
    output = 78
    own = 79
    packed = 80
    pairs = 81
    pairs_other = 82
    piece_recv = 83
    piece_send = 84
    project_other = 85
    project_own = 86
    put = 87
    return_other = 88
    row_recv = 89
    row_send = 90
    save = 91
    saved = 92
    second_norm = 93
    send = 94
    shift_sum = 95
    slope = 96
    soft = 97
    sums = 98
    swap_recv = 99
    swap_send = 100
    swapped = 101
    table = 102
    table_in = 103
    table_recv = 104
    table_send = 105
    token_sums = 106
    total = 107
    vector = 108
    vectors = 109
    w_inner = 110
    w_input = 111
    w_outer = 112
    w_output = 113


def attributes(refs):
    return {key.name: ref for key, ref in refs.items() if isinstance(key, Key)}


class Place:
    def __init__(self, rows):
        self.nz = rows // 4
        r = lax.axis_index("rows")
        self.x = lax.axis_index("pair")
        self.z = r // 4
        self.y = (r // 2) % 2
        self.c = r % 2
        self.index = self.x * rows + r
        self.own = {"X": self.x, "Z": self.z, "Y": self.y}

    def device(self, **other):
        at = {"X": self.x, "Z": self.z, "Y": self.y, "C": self.c, **other}
        return {"pair": at["X"], "rows": (at["Z"] * 2 + at["Y"]) * 2 + at["C"]}

    def peers(self, dim):
        if dim == "Z":
            return [(self.z + k) % self.nz for k in range(1, self.nz)]
        return [1 - self.own[dim]]

    def sources(self, dim):
        if dim == "Z":
            return [(self.z + self.nz - k) % self.nz for k in range(1, self.nz)]
        return [1 - self.own[dim]]

    def first_slot(self, dim):
        return {"X": 0, "Y": 1, "Z": 2}[dim]

    def slots(self):
        return self.nz + 1


def slab(buf, place, gathered, at, rows, cols):
    own = {**place.own, **at}
    lead = tuple(ALL if d in gathered else own[d] for d in "XZY")
    return buf.at[lead + (rows, cols)]


class Gather:
    def __init__(self, buf, place, send, recv, routes, rows, col, width):
        self.buf, self.place, self.send, self.recv, self.routes = buf, place, send, recv, routes
        self.rows, self.col, self.width = rows, col, width
        self.half = buf.shape[-1] // 2

    def cols(self, core):
        return pl.ds(pl.multiple_of(core * self.half + self.col, 128), self.width)

    def per_core(self, act):
        if self.routes[0] == self.routes[1]:
            act(self.routes[0])
            return
        for core in range(2):
            pl.when(self.place.c == core)(functools.partial(act, self.routes[core]))

    def copy(self, view, slot, device):
        return pltpu.make_async_remote_copy(
            src_ref=view,
            dst_ref=view,
            send_sem=self.send.at[slot],
            recv_sem=self.recv.at[slot],
            device_id=device,
            device_id_type=MESH,
        )

    def sends(self, route, stage):
        dim, gathered = route[stage], route[:stage]
        view = slab(self.buf, self.place, gathered, {}, self.rows, self.cols(self.place.c))
        first = self.place.first_slot(dim)
        return [
            self.copy(view, first + k, self.place.device(**{dim: peer}))
            for k, peer in enumerate(self.place.peers(dim))
        ]

    def arrivals(self, route, stage, core):
        dim, gathered = route[stage], route[:stage]
        return [
            slab(self.buf, self.place, gathered, {dim: peer}, self.rows, self.cols(core))
            for peer in self.place.sources(dim)
        ]

    def hand_ons(self, route, stage, core):
        device = self.place.device(C=1 - self.place.c)
        base = self.place.slots()
        if stage == 0:
            view = slab(self.buf, self.place, route[:1], {}, self.rows, self.cols(core))
            return [self.copy(view, base, device)]
        first = base + 1 + (stage - 1) * (self.place.nz - 1)
        return [
            self.copy(view, first + k, device)
            for k, view in enumerate(self.arrivals(route, stage, core))
        ]

    def start(self, stage):
        def act(route):
            for copy in self.sends(route, stage):
                copy.start()

        self.per_core(act)

    def arrived(self, stage):
        def act(route):
            dim = route[stage]
            first = self.place.first_slot(dim)
            device = self.place.device()
            for k, view in enumerate(self.arrivals(route, stage, self.place.c)):
                self.copy(view, first + k, device).wait_recv()
            if stage < 2:
                for copy in self.sends(route, stage + 1):
                    copy.start()
            for copy in self.hand_ons(route, stage, self.place.c):
                copy.start()

        self.per_core(act)

    def event(self, number):
        if number == 0:
            self.start(0)
        elif number < 4:
            self.arrived(number - 1)
        else:
            self.complete()

    def complete(self):
        def other(route):
            for stage in range(3):
                for copy in self.hand_ons(route, stage, 1 - self.place.c):
                    copy.wait_recv()

        if self.routes[0] == self.routes[1]:
            other(self.routes[0])
        else:
            for core in range(2):
                pl.when(self.place.c == 1 - core)(functools.partial(other, self.routes[core]))

    def drain(self):
        def act(route):
            for stage in range(3):
                for copy in self.sends(route, stage) + self.hand_ons(route, stage, self.place.c):
                    copy.wait_send()

        self.per_core(act)


def greet(place, devices):
    barrier = pltpu.get_barrier_semaphore()
    for device in devices:
        pl.semaphore_signal(barrier, inc=1, device_id=device, device_id_type=MESH)
    pl.semaphore_wait(barrier, len(devices))


class Totals:
    def __init__(self, place, table, landed, send, recv):
        self.place, self.table, self.landed, self.send, self.recv = place, table, landed, send, recv
        x, y = 1 - place.x, 1 - place.y
        self.steps = [
            [place.device(C=1 - place.c)],
            [place.device(X=x), place.device(Y=y), place.device(X=x, Y=y)],
            [place.device(Z=peer) for peer in place.peers("Z")],
        ]

    def copies(self, step):
        first = sum(len(found) for found in self.steps[:step])
        return [
            pltpu.make_async_remote_copy(
                src_ref=self.table.at[step],
                dst_ref=self.landed.at[first + k],
                send_sem=self.send.at[first + k],
                recv_sem=self.recv.at[first + k],
                device_id=device,
                device_id_type=MESH,
            )
            for k, device in enumerate(self.steps[step])
        ]

    def start(self, step):
        for copy in self.copies(step):
            copy.start()

    def advance(self, step):
        first = sum(len(found) for found in self.steps[:step])
        total = self.table[step]
        for k, copy in enumerate(self.copies(step)):
            copy.wait_recv()
            total = total + self.landed[first + k]
        self.table[step + 1] = total
        if step + 1 < len(self.steps):
            self.start(step + 1)

    def drain(self):
        for step in range(len(self.steps)):
            for copy in self.copies(step):
                copy.wait_send()


def neighbours(place):
    x, y = 1 - place.x, 1 - place.y
    found = [place.device(C=1 - place.c), place.device(X=x), place.device(Y=y), place.device(X=x, Y=y)]
    return found + [place.device(Z=peer) for peer in place.peers("Z")]


def source_slots(slots, sizes, most):
    frame, offset = slots // most, slots % most
    total = sum(sizes[1:], sizes[0])
    found, start = slots, jnp.int32(0)
    for p, size in enumerate(sizes):
        mine = jnp.where(offset < size, start + offset, total + slots - (start + size))
        found = jnp.where(frame == p, mine, found)
        start = start + size
    return found


def holds_token(slots, sizes, most):
    frame, offset = slots // most, slots % most
    held = jnp.zeros(slots.shape, f32)
    for p, size in enumerate(sizes):
        held = jnp.where((frame == p) & (offset < size), 1.0, held)
    return held


def into_frames(sizes, slots, most):
    source = source_slots(iota((slots, 1), 0), sizes, most)
    return (iota((slots, slots), 1) == source).astype(f32).astype(bf16)


def out_of_frames(sizes, slots, most):
    source = source_slots(iota((1, slots), 1), sizes, most)
    return (iota((slots, slots), 0) == source).astype(f32).astype(bf16)


def folded(v):
    return jnp.sum(v.reshape(v.shape[0] // 8, 8, v.shape[1]), axis=0)


def spread_heads(tokens, span):
    shape = (4 * tokens, span)
    return iota(shape, 0) // tokens == iota(shape, 1) // (span // 4)


def block_rows(i, size):
    return pl.ds(pl.multiple_of(i * size, size), size)


class Forward:
    def __init__(self, refs, place, sizes):
        self.__dict__.update(attributes(refs))
        self.place = place
        self.rows, self.slots, self.width, self.pairs = sizes
        self.most = self.slots // self.pairs
        self.half = place.x
        self.bias_rows = self.ff_bias.shape[1] // self.width
        self.scale = (self.width // HEADS) ** (-0.5)

    def sizes_of(self, row, half):
        return [self.lengths[row, half, p] for p in range(self.pairs)]

    def row(self, r):
        return pl.ds(r * self.slots, self.slots)

    def vector(self, at, count=1):
        found = rounded(self.vectors[at : at + count, :])
        return found if count == 1 else found.reshape(1, count * self.width)

    def frame_hidden(self, r):
        frames = into_frames(self.sizes_of(r, self.half), self.slots, self.most)
        self.own[self.row(r), :] = contract(frames, self.hidden[self.row(r), :], 1, 0).astype(bf16)

    def frame_cotangent(self, r):
        sizes = self.sizes_of(r, self.half)
        frames = into_frames(sizes, self.slots, self.most)
        held = holds_token(iota((self.slots, 1), 0), sizes, self.most)
        moved = contract(frames, self.cot[self.row(r), :], 1, 0) * held
        self.cot[self.row(r), :] = moved.astype(bf16)

    def project_own(self, part):
        cols = slice(part * self.width, (part + 1) * self.width)
        weight = self.w_input[:, :, :, :, cols].reshape(self.width, self.width)
        acc = contract(self.own[...], weight, 1, 0)
        if part == 0:
            acc = acc + self.vector(Q_BIAS)
        if part == 2:
            acc = acc + self.vector(V_BIAS)
        self.packed[:, cols] = acc.astype(bf16)

    def project_other(self, r, part):
        cols = slice(part * self.width, (part + 1) * self.width)
        from_cols = slice((part + 1) * self.width, (part + 2) * self.width)
        weight = self.w_input[:, :, :, :, from_cols].reshape(self.width, self.width)
        acc = contract(self.other[self.row(r), :], weight, 1, 0)
        if part == 1:
            acc = acc + self.vector(V_BIAS)
        self.pairs_other[self.row(r), cols] = acc.astype(bf16)

    def attend_pairs(self, r, together=4):
        most, span, wide = self.most, 4 * (self.width // HEADS), 2 * self.most
        spread = spread_heads(wide, span)
        key, query = iota((2 * wide, 4 * wide), 0), iota((2 * wide, 4 * wide), 1)
        key_frame, same = key % wide // most, key % wide // most == query % wide // most
        slot = key % most

        def two_pairs(pair):
            rows = pl.ds(pl.multiple_of(r * self.slots + pair * wide, wide), wide)
            counts = [self.lengths[r, half, 2 * pair + k] for half in (self.half, 1 - self.half) for k in range(2)]
            mine = jnp.where(key_frame == 0, counts[0], counts[1])
            theirs = jnp.where(key_frame == 0, counts[2], counts[3])
            allowed = same & (slot < jnp.where(key < wide, mine, theirs))
            for at in range(0, self.width, span):
                queries = self.packed[rows, at : at + span]
                keys = jnp.concatenate(
                    [
                        self.packed[rows, self.width + at : self.width + at + span],
                        self.pairs_other[rows, at : at + span],
                    ],
                    axis=0,
                )
                values = jnp.concatenate(
                    [
                        self.packed[rows, 2 * self.width + at : 2 * self.width + at + span],
                        self.pairs_other[rows, self.width + at : self.width + at + span],
                    ],
                    axis=0,
                )
                tiled = jnp.where(spread, jnp.concatenate([queries] * 4, axis=0), 0).astype(bf16)
                scores = jnp.where(allowed, contract(keys, tiled, 1, 1) * self.scale, MASKED)
                raw = jnp.exp(scores - jnp.max(scores, axis=0, keepdims=True))
                soft = raw * (1.0 / jnp.sum(raw, axis=0, keepdims=True))
                kept = [soft[k * most : (k + 1) * most] + soft[(k + 1) * most : (k + 2) * most] for k in (0, 2)]
                self.soft[rows, at : at + span] = jnp.concatenate(kept, axis=0).astype(bf16)
                mixed = contract(soft.astype(bf16), values, 0, 0)
                mixed = jnp.where(spread, mixed, 0.0)
                context = sum(mixed[h * wide : (h + 1) * wide, :] for h in range(4))
                self.context[rows, at : at + span] = context.astype(bf16)

        @pl.loop(0, self.pairs // (2 * together))
        def _(several):
            for k in range(together):
                two_pairs(several * together + k)

    def attend_padding(self, r, together=6):
        sizes = self.sizes_of(r, self.half)
        head = self.width // HEADS
        held_key = holds_token(iota((1, self.slots), 1), sizes, self.most)
        held_query = holds_token(iota((self.slots, 1), 0), sizes, self.most)
        pad_key = jnp.broadcast_to(held_key, (2 * self.slots, self.slots)) < 0.5
        pad_query = jnp.broadcast_to(held_query, (self.slots, 2 * head)) < 0.5
        left = iota((self.slots, 2 * head), 1) < head
        rows = self.row(r)

        def two_heads(pair):
            at = pl.multiple_of(pair * 2 * head, 2 * head)
            queries = self.packed[rows, pl.ds(at, 2 * head)] * self.scale
            keys = self.packed[rows, pl.ds(pl.multiple_of(self.width + at, 2 * head), 2 * head)]
            values = self.packed[rows, pl.ds(pl.multiple_of(2 * self.width + at, 2 * head), 2 * head)]
            both = jnp.concatenate([jnp.where(left, queries, 0), jnp.where(left, 0, queries)], axis=0)
            scores = jnp.where(pad_key, contract(both.astype(bf16), keys, 1, 1), MASKED)
            raw = jnp.exp(scores - jnp.max(scores, axis=1, keepdims=True))
            total = jnp.sum(raw, axis=1, keepdims=True)
            found = contract(raw.astype(bf16), values, 1, 0) * (1.0 / total)
            padded = jnp.where(left, found[: self.slots], found[self.slots :]).astype(bf16)
            cols = pl.ds(at, 2 * head)
            self.context[rows, cols] = jnp.where(pad_query, padded, self.context[rows, cols])

        @pl.loop(0, HEADS // 2 // together)
        def _(several):
            for k in range(together):
                two_heads(several * together + k)

    def first_norm(self, r):
        if r < self.rows:
            weight = self.w_output[...].reshape(self.width, self.width)
            self.sums[r % 2] = contract(self.context[self.row(r), :], weight, 1, 0)
        if r == 0:
            return
        bias, gain, shift = self.vector(O_BIAS), self.vector(GAIN_1), self.vector(SHIFT_1)
        size = 32
        for i in range(0, self.slots, size):
            there = pl.ds((r - 1) * self.slots + i, size)
            total = self.own[there, :].astype(f32) + self.sums[(r - 1) % 2, i : i + size, :] + bias
            centered = total - jnp.mean(total, axis=1, keepdims=True)
            inverse = lax.rsqrt(jnp.mean(centered * centered, axis=1, keepdims=True) + EPSILON)
            norm = centered * inverse
            self.norm[there, :] = norm
            self.inverse[there, :] = jnp.broadcast_to(inverse, (size, 128))
            self.low[there, :] = (norm * gain + shift).astype(bf16)

    def hidden_units(self, first, count, size=256):
        @pl.loop(first, first + count)
        def _(n):
            cols = pl.ds(pl.multiple_of(n * size, size), size)
            weight = self.w_inner[:, :, :, :, cols].reshape(self.width, size)
            bias = rounded(self.ff_bias[:, cols])
            for r in range(self.rows):
                inner = contract(self.low[self.row(r), :], weight, 1, 0) + bias
                share = 0.5 * (1.0 + lax.erf(inner * (0.5**0.5)))
                slope = share + inner * (jnp.exp(-0.5 * inner * inner) * ((2.0 * math.pi) ** -0.5))
                self.active[self.row(r), cols] = (inner * share).astype(bf16)
                self.slope[self.row(r), cols] = slope.astype(bf16)

    def second_norm(self, r):
        if r < self.rows:
            weight = self.w_outer[...].reshape(self.w_inner.shape[-1], self.width)
            self.sums[r % 2] = contract(self.active[self.row(r), :], weight, 1, 0)
        if r == 0:
            return
        gain_1, shift_1 = self.vector(GAIN_1), self.vector(SHIFT_1)
        bias, gain, shift = self.vector(OUT_BIAS), self.vector(GAIN_2), self.vector(SHIFT_2)
        size = 32
        sums = [self.gain_sum[...], self.shift_sum[...], self.low_sum[...]]
        for i in range(0, self.slots, size):
            there = pl.ds((r - 1) * self.slots + i, size)
            total = (self.norm[there, :] * gain_1 + shift_1) + self.sums[(r - 1) % 2, i : i + size, :] + bias
            centered = total - jnp.mean(total, axis=1, keepdims=True)
            inverse = lax.rsqrt(jnp.mean(centered * centered, axis=1, keepdims=True) + EPSILON)
            norm = centered * inverse
            self.framed[i : i + size, :] = (norm * gain + shift).astype(bf16)
            upstream = self.cot[there, :].astype(f32)
            incoming = upstream * gain
            plain = jnp.mean(incoming, axis=1, keepdims=True)
            along = jnp.mean(incoming * norm, axis=1, keepdims=True)
            grad = inverse * (incoming - plain - norm * along)
            low = grad.astype(bf16)
            self.grad[there, :] = grad
            self.soft[there, :] = low
            parts = (upstream * norm, upstream, low.astype(f32))
            sums = [total + folded(part) for total, part in zip(sums, parts, strict=True)]
        self.gain_sum[...], self.shift_sum[...], self.low_sum[...] = sums
        back = out_of_frames(self.sizes_of(r - 1, self.half), self.slots, self.most)
        self.hidden[self.row(r - 1), :] = contract(back, self.framed[...], 1, 0).astype(bf16)


FORWARD_VMEM = 127 * 2**19
ORDER = None


def forward_kernel(names, fast, sizes, routes, plan, *refs):
    refs = dict(zip(names, refs, strict=True))
    rows, slots, width, pairs = sizes
    place = Place(lax.axis_size("rows"))
    run = Forward(refs, place, sizes)
    sibling = place.device(C=1 - place.c)
    partner = place.device(X=1 - place.x)

    def local(src, dst, slot):
        return pltpu.make_async_copy(src, dst, run.local_sem.at[slot])

    load_hidden = local(run.hidden_in, run.hidden, 0)
    load_cot = local(run.cotangent, run.cot, 1)
    load_hidden.start()
    load_cot.start()

    if fast:
        greet(place, neighbours(place))
    else:
        greet(place, [partner])

    def hidden_copy(r):
        view = pl.ds(r * slots, slots)
        return pltpu.make_async_remote_copy(
            src_ref=run.own.at[view],
            dst_ref=run.other.at[view],
            send_sem=run.row_send.at[r],
            recv_sem=run.row_recv.at[r],
            device_id=partner,
            device_id_type=MESH,
        )

    weights = [Key.w_input, Key.w_output, Key.w_inner, Key.w_outer]
    masters = [Key.m_input, Key.m_output, Key.m_inner, Key.m_outer]
    gathers = {}
    drains = []
    if fast:
        totals = Totals(place, run.table, run.table_in, run.table_send, run.table_recv)
        for k, (weight, master) in enumerate(zip(weights, masters, strict=True)):
            buf = refs[weight]
            half = buf.shape[-1] // 2
            for j, (route, (row, count), (col, span)) in enumerate(routes.get(weight, ())):
                piece = Gather(
                    buf, place, run.piece_send.at[len(gathers)], run.piece_recv.at[len(gathers)],
                    route, pl.ds(row, count), col, span,
                )
                gathers[weight, j] = piece

        def swap(k):
            master = refs[masters[k]]
            half = master.shape[-1] // 2
            theirs = pl.ds(pl.multiple_of((1 - place.c) * half, 128), half)
            return pltpu.make_async_remote_copy(
                src_ref=master.at[:, theirs],
                dst_ref=refs[Key.from_sibling, k],
                send_sem=run.swap_send.at[k],
                recv_sem=run.swap_recv.at[k],
                device_id=sibling,
                device_id_type=MESH,
            )

        def lay(k):
            swap(k).wait_recv()
            master, buf = refs[masters[k]], refs[weights[k]]
            half = master.shape[-1] // 2
            cols = pl.ds(pl.multiple_of(place.c * half, 128), half)
            mine, theirs = master[:, cols], refs[Key.from_sibling, k][...]
            first = place.c == 0
            both = jnp.concatenate([jnp.where(first, mine, theirs), jnp.where(first, theirs, mine)], axis=0)
            buf[place.x, place.z, place.y, :, cols] = both.astype(bf16)

        for k in range(4):
            swap(k).start()
        run.table[0] = jnp.zeros((VECTORS, width), f32)
        for k in range(9):
            share = refs[Key.vector, k]
            run.table[0, k : k + 1, 0 : share.shape[1]] = share[...]
        piece = refs[Key.vector, 0].shape[1]
        wide = refs[Key.vector, 8].shape[1]
        per_row = width // wide
        upper = pltpu.roll(run.table[0, 0:8, :], place.index * piece, axis=1)
        lower = pltpu.roll(run.table[0, 8:16, :], (place.index % per_row) * wide, axis=1)
        lower = jnp.broadcast_to(lower[:1, :], (8, width))
        lower = jnp.where(iota((8, width), 0) == place.index // per_row, lower, 0.0)
        run.table[0, 0:8, :] = upper
        run.table[0, 8:16, :] = lower
        totals.start(0)

    def spread_vectors(table):
        run.vectors[...] = table
        for k in range(run.bias_rows):
            run.ff_bias[:, k * width : (k + 1) * width] = table[FF_ROW + k : FF_ROW + k + 1, :]

    if not fast:
        for k, weight in enumerate(weights):
            local(refs[masters[k]], refs[weight], 2 + k).start()
        spread_vectors(refs[Key.vector, 0][...])

    saved = [
        (Key.k_input, Key.w_input), (Key.k_output, Key.w_output), (Key.k_inner, Key.w_inner), (Key.k_outer, Key.w_outer),
        (Key.k_own, Key.own), (Key.k_other, Key.other), (Key.k_packed, Key.packed), (Key.k_pairs, Key.pairs_other),
        (Key.k_soft, Key.soft), (Key.k_context, Key.context), (Key.k_norm, Key.norm), (Key.k_inverse, Key.inverse),
        (Key.k_active, Key.active), (Key.k_slope, Key.slope), (Key.k_grad, Key.grad), (Key.k_vectors, Key.vectors), (Key.k_low, Key.soft),
        (Key.layer_out, Key.hidden),
    ]
    saves = {name: local(refs[src], refs[name], 6 + k) for k, (name, src) in enumerate(saved) if name in refs}
    started = []
    sent = []

    def save(name):
        if name in saves:
            saves[name].start()
            started.append(name)

    def step(what, *detail):
        if what == Key.event:
            if fast:
                gathers[detail[0], detail[1]].event(detail[2])
        elif what == Key.lay:
            if fast:
                lay(detail[0])
        elif what == Key.total:
            if fast:
                totals.advance(detail[0])
                if detail[0] + 1 == len(totals.steps):
                    spread_vectors(run.table[detail[0] + 1])
        elif what == Key.loaded:
            if not fast:
                k = weights.index(detail[0])
                local(refs[masters[k]], refs[detail[0]], 2 + k).wait()
        elif what == Key.frame:
            if detail[0] == 0:
                load_hidden.wait()
            run.frame_hidden(detail[0])
        elif what == Key.send:
            hidden_copy(detail[0]).start()
            sent.append(detail[0])
        elif what == Key.other:
            hidden_copy(detail[0]).wait_recv()
        elif what == Key.cot:
            if detail[0] == 0:
                load_cot.wait()
            run.frame_cotangent(detail[0])
        elif what == Key.save:
            save(detail[0])
        elif what == Key.saved:
            saves[detail[0]].wait()
            started.remove(detail[0])
        else:
            getattr(run, what.name)(*detail)

    run.gain_sum[...] = jnp.zeros_like(run.gain_sum)
    run.shift_sum[...] = jnp.zeros_like(run.shift_sum)
    run.low_sum[...] = jnp.zeros_like(run.low_sum)
    for entry in plan:
        step(*entry)
    run.k_sums[0:8, :] = run.gain_sum[...]
    run.k_sums[8:16, :] = run.shift_sum[...]
    run.k_sums[16:24, :] = run.low_sum[...]
    for r in sent:
        hidden_copy(r).wait_send()
    if fast:
        for gather in gathers.values():
            gather.drain()
        for k in range(4):
            swap(k).wait_send()
        totals.drain()
    for name in started:
        saves[name].wait()


def forward_plan(rows, units):
    plan = []
    for r in range(rows):
        plan += [(Key.frame, r), (Key.send, r)]
    for k in range(4):
        plan += [(Key.lay, k)]
    for n in range(5):
        plan += [(Key.total, n)]
    for r in range(rows):
        plan += [(Key.cot, r)]
    for w in (Key.w_input, Key.w_output, Key.w_inner, Key.w_outer):
        for e in range(5):
            plan += [(Key.event, w, 0, e)]
        plan += [(Key.loaded, w)]
    for part in range(3):
        plan += [(Key.project_own, part)]
    for r in range(rows):
        plan += [(Key.other, r), (Key.project_other, r, 0), (Key.project_other, r, 1)]
        plan += [(Key.attend_pairs, r), (Key.attend_padding, r), (Key.first_norm, r)]
    plan += [(Key.hidden_units, 0, units)]
    for r in range(rows):
        plan += [(Key.second_norm, r)]
    for name in (Key.layer_out, Key.k_input, Key.k_output, Key.k_inner, Key.k_outer, Key.k_own, Key.k_other, Key.k_packed, Key.k_pairs,
                 Key.k_soft, Key.k_context, Key.k_norm, Key.k_inverse, Key.k_active, Key.k_slope, Key.k_grad, Key.k_vectors):
        plan += [(Key.save, name)]
    return plan


def forward_call(mesh_rows, fast, hidden, cot, masters, small, lengths, routes, plan, with_saves=True):
    rows, slots, width = hidden.shape
    pairs = lengths.shape[2]
    tokens = rows * slots
    units = masters[2].shape[1]
    nz = mesh_rows // 4
    tall = [width, width, width, units]
    wide = [3 * width, width, units, width]
    if fast:
        shapes = [(2, nz, 2, tall[k] // (4 * nz), wide[k]) for k in range(4)]
    else:
        shapes = [(1, 1, 1, tall[k], wide[k]) for k in range(4)]
    weights = [Key.w_input, Key.w_output, Key.w_inner, Key.w_outer]
    ins = [Key.hidden_in, Key.cotangent, Key.m_input, Key.m_output, Key.m_inner, Key.m_outer]
    ins += [(Key.vector, k) for k in range(len(small))] + [Key.lengths]
    hbm, vmem, smem = (pl.BlockSpec(memory_space=s) for s in (pl.ANY, pltpu.VMEM, pltpu.SMEM))
    if fast:
        args = [hidden.reshape(tokens, width), cot.reshape(tokens, width), *masters, *small, lengths]
    else:
        args = [hidden.reshape(tokens, width), cot.reshape(tokens, width)]
        args += [m.reshape(s) for m, s in zip(masters, shapes, strict=True)] + [*small, lengths]
    in_specs = [hbm, hbm] + [vmem if fast else hbm] * 4 + [vmem] * len(small) + [smem]
    outs = {Key.layer_out: ((tokens, width), bf16), Key.k_sums: ((24, width), f32)}
    saved = {
        Key.k_input: (shapes[0], bf16), Key.k_output: (shapes[1], bf16), Key.k_inner: (shapes[2], bf16),
        Key.k_outer: (shapes[3], bf16), Key.k_own: ((tokens, width), bf16), Key.k_other: ((tokens, width), bf16),
        Key.k_packed: ((tokens, 3 * width), bf16), Key.k_pairs: ((tokens, 2 * width), bf16),
        Key.k_soft: ((tokens, width), bf16), Key.k_context: ((tokens, width), bf16),
        Key.k_norm: ((tokens, width), f32), Key.k_inverse: ((tokens, 128), f32),
        Key.k_active: ((tokens, units), bf16), Key.k_slope: ((tokens, units), bf16),
        Key.k_grad: ((tokens, width), f32), Key.k_low: ((tokens, width), bf16), Key.k_vectors: ((VECTORS, width), f32),
    }
    if with_saves:
        outs.update(saved)
    out_specs = [vmem if name == Key.k_sums else hbm for name in outs]
    scratch = {
        Key.w_input: pltpu.VMEM(shapes[0], bf16), Key.w_output: pltpu.VMEM(shapes[1], bf16),
        Key.w_inner: pltpu.VMEM(shapes[2], bf16), Key.w_outer: pltpu.VMEM(shapes[3], bf16),
        Key.hidden: pltpu.VMEM((tokens, width), bf16), Key.cot: pltpu.VMEM((tokens, width), bf16),
        Key.own: pltpu.VMEM((tokens, width), bf16), Key.other: pltpu.VMEM((tokens, width), bf16),
        Key.packed: pltpu.VMEM((tokens, 3 * width), bf16), Key.pairs_other: pltpu.VMEM((tokens, 2 * width), bf16),
        Key.context: pltpu.VMEM((tokens, width), bf16), Key.soft: pltpu.VMEM((tokens, width), bf16),
        Key.norm: pltpu.VMEM((tokens, width), f32), Key.inverse: pltpu.VMEM((tokens, 128), f32),
        Key.low: pltpu.VMEM((tokens, width), bf16), Key.active: pltpu.VMEM((tokens, units), bf16),
        Key.slope: pltpu.VMEM((tokens, units), bf16), Key.grad: pltpu.VMEM((tokens, width), f32),
        Key.sums: pltpu.VMEM((2, slots, width), f32), Key.framed: pltpu.VMEM((slots, width), bf16),
        Key.vectors: pltpu.VMEM((VECTORS, width), f32), Key.ff_bias: pltpu.VMEM((1, units), f32),
        Key.gain_sum: pltpu.VMEM((8, width), f32), Key.shift_sum: pltpu.VMEM((8, width), f32),
        Key.low_sum: pltpu.VMEM((8, width), f32),
        Key.local_sem: pltpu.SemaphoreType.DMA((6 + len(saved) + 1,)),
        Key.row_send: pltpu.SemaphoreType.DMA((rows,)), Key.row_recv: pltpu.SemaphoreType.DMA((rows,)),
    }
    if fast:
        steps, partners = 3, nz + 3
        pieces = sum(len(v) for v in routes.values())
        slots_each = nz + 1 + 1 + 2 * (nz - 1)
        scratch.update({
            Key.table: pltpu.VMEM((steps + 1, VECTORS, width), f32), Key.table_in: pltpu.VMEM((partners, VECTORS, width), f32),
            Key.table_send: pltpu.SemaphoreType.DMA((partners,)), Key.table_recv: pltpu.SemaphoreType.DMA((partners,)),
            Key.piece_send: pltpu.SemaphoreType.DMA((pieces, slots_each)),
            Key.piece_recv: pltpu.SemaphoreType.DMA((pieces, slots_each)),
            Key.swap_send: pltpu.SemaphoreType.DMA((4,)), Key.swap_recv: pltpu.SemaphoreType.DMA((4,)),
        })
        for k in range(4):
            scratch[Key.from_sibling, k] = pltpu.VMEM((masters[k].shape[0], wide[k] // 2), f32)
    names = ins + list(outs) + list(scratch)
    sizes = (rows, slots, width, pairs)
    body = functools.partial(forward_kernel, names, fast, sizes, routes, plan)
    found = pl.pallas_call(
        body,
        out_shape=[jax.ShapeDtypeStruct(*s) for s in outs.values()],
        in_specs=in_specs,
        out_specs=out_specs,
        scratch_shapes=list(scratch.values()),
        compiler_params=pltpu.CompilerParams(
            collective_id=0, has_side_effects=True, vmem_limit_bytes=FORWARD_VMEM
        ),
        name="forward",
    )(*args)
    return dict(zip(outs, found, strict=True))


class Scatter:
    def __init__(self, buf, place, swapped, landed, final, out, send, recv, routes, starts, width):
        self.buf, self.place, self.swapped, self.landed = buf, place, swapped, landed
        self.final, self.out, self.send, self.recv, self.routes = final, out, send, recv, routes
        self.starts, self.width = starts, width
        self.sizes = dict(zip("XZY", buf.shape[:3], strict=True))
        self.core_rows = buf.shape[3] // 2

    def cols(self, core):
        first, second = self.starts
        return pl.ds(pl.multiple_of(first + core * (second - first), 128), self.width)

    def remote(self, src, dst, slot, device):
        return pltpu.make_async_remote_copy(
            src_ref=src,
            dst_ref=dst,
            send_sem=self.send.at[slot],
            recv_sem=self.recv.at[slot],
            device_id=device,
            device_id_type=MESH,
        )

    def per_core(self, act):
        if self.routes[0] == self.routes[1]:
            act(self.routes[0])
            return
        for core in range(2):
            pl.when(self.place.c == core)(functools.partial(act, self.routes[core]))

    def lead(self, route, stage, at):
        own = {**self.place.own, **at}
        fixed = route[: stage + 1]
        return tuple(own[d] if d in fixed else ALL for d in "XZY")

    def swap(self):
        place = self.place
        src = self.buf.at[ALL, ALL, ALL, ALL, self.cols(1 - place.c)]
        return self.remote(src, self.swapped, 0, place.device(C=1 - place.c))

    def sends(self, route, stage):
        dim = route[stage]
        mine = self.landed.at[self.lead(route, stage, {})]
        found = []
        for k, peer in enumerate(self.place.peers(dim)):
            src = self.buf.at[self.lead(route, stage, {dim: peer}) + (ALL, self.cols(self.place.c))]
            found.append(self.remote(src, mine, 1 + self.place.first_slot(dim) + k, self.place.device(**{dim: peer})))
        return found

    def arrivals(self, route, stage):
        dim = route[stage]
        found = []
        for k, peer in enumerate(self.place.sources(dim)):
            view = self.landed.at[self.lead(route, stage, {dim: peer})]
            found.append(self.remote(view, view, 1 + self.place.first_slot(dim) + k, self.place.device()))
        return found

    def blocks(self, free, body):
        total = math.prod(self.sizes[d] for d in free)

        def visit(i):
            at = dict(self.place.own)
            for d in reversed(free):
                at[d] = i % self.sizes[d]
                i = i // self.sizes[d]
            body((at["X"], at["Z"], at["Y"]), at)

        if total == 1:
            visit(0)
        else:
            pl.loop(0, total)(visit)

    def start_swap(self):
        self.swap().start()

    def add_swapped(self):
        self.swap().wait_recv()
        cols = self.cols(self.place.c)

        def body(block, at):
            there = block + (ALL, cols)
            total = self.buf[there].astype(f32) + self.swapped[block].astype(f32)
            self.buf[there] = total.astype(bf16)

        self.blocks("XZY", body)

        def act(route):
            for copy in self.sends(route, 0):
                copy.start()

        self.per_core(act)

    def add_stage(self, stage):
        cols = self.cols(self.place.c)

        def act(route):
            dim = route[stage]
            for copy in self.arrivals(route, stage):
                copy.wait_recv()
            sources = self.place.sources(dim)

            def body(block, at):
                total = self.buf[block + (ALL, cols)].astype(f32)
                for peer in sources:
                    theirs = {**at, dim: peer}
                    total = total + self.landed[theirs["X"], theirs["Z"], theirs["Y"]].astype(f32)
                if stage < 2:
                    self.buf[block + (ALL, cols)] = total.astype(bf16)
                else:
                    self.final[...] = total

            self.blocks("".join(d for d in "XZY" if d not in route[: stage + 1]), body)
            if stage < 2:
                for copy in self.sends(route, stage + 1):
                    copy.start()

        self.per_core(act)
        if stage == 2:
            for copy in self.hand_over():
                copy.start()

    def hand_over(self):
        place, count = self.place, self.core_rows
        cols = self.cols(place.c)
        mine = self.final.at[pl.ds(pl.multiple_of(place.c * count, 8), count)]
        theirs = self.final.at[pl.ds(pl.multiple_of((1 - place.c) * count, 8), count)]
        there = self.remote(theirs, self.out.at[:, cols], 1 + place.slots(), place.device(C=1 - place.c))
        here = pltpu.make_async_copy(mine, self.out.at[:, cols], self.send.at[2 + place.slots()])
        return [there, here]

    def finish(self):
        there, here = self.hand_over()
        here.wait()
        there.wait_send()
        view = self.out.at[:, self.cols(1 - self.place.c)]
        self.remote(view, view, 1 + self.place.slots(), self.place.device()).wait_recv()

    def drain(self):
        self.swap().wait_send()

        def act(route):
            for stage in range(3):
                for copy in self.sends(route, stage):
                    copy.wait_send()

        self.per_core(act)

    def event(self, number):
        if number == 0:
            self.start_swap()
        elif number == 1:
            self.add_swapped()
        elif number < 5:
            self.add_stage(number - 2)
        else:
            self.finish()


class Backward:
    def __init__(self, refs, place, sizes):
        self.__dict__.update(attributes(refs))
        self.place = place
        self.rows, self.slots, self.width, self.pairs = sizes
        self.most = self.slots // self.pairs
        self.half = place.x
        self.scale = (self.width // HEADS) ** (-0.5)
        self.tokens = self.rows * self.slots
        self.units = self.active.shape[1]

    def sizes_of(self, row, half):
        return [self.lengths[row, half, p] for p in range(self.pairs)]

    def row(self, r):
        return pl.ds(r * self.slots, self.slots)

    def vector(self, at):
        return rounded(self.vectors[at : at + 1, :])

    def lower_norm(self):
        gain, shift = self.vector(GAIN_1), self.vector(SHIFT_1)

        @pl.loop(0, self.tokens // 64)
        def _(i):
            rows = block_rows(i, 64)
            self.low[rows, :] = (self.norm[rows, :] * gain + shift).astype(bf16)

    def grad_outer(self):
        nz = self.d_outer.shape[1]
        parts = self.d_outer.shape[0] * nz
        size = self.units // parts

        @pl.loop(0, parts)
        def _(i):
            found = contract(self.active[:, pl.ds(pl.multiple_of(i * size, 128), size)], self.grad_low[...], 0, 0)
            self.d_outer[i // nz, i % nz] = found.astype(bf16).reshape(self.d_outer.shape[2:])

    def grad_hidden(self, first, count, size=384):
        @pl.loop(first, first + count)
        def _(n):
            cols = pl.ds(pl.multiple_of(n * size, size), size)
            weight = self.w_outer[cols, :]
            total = jnp.zeros((8, size), f32)
            for r in range(self.rows):
                found = contract(self.grad_low[self.row(r), :], weight, 1, 1)
                low = (found * self.slope[self.row(r), cols].astype(f32)).astype(bf16)
                self.slope[self.row(r), cols] = low
                total = total + folded(low.astype(f32))
            self.ff_sums[:, cols] = total

    def grad_inner(self, core, part, size=768):
        half = self.units // 2
        cols = pl.ds(pl.multiple_of(core * half + part * size, 128), size)
        found = contract(self.low[...], self.slope[:, cols], 0, 0).astype(bf16)
        self.d_inner[:, :, :, :, cols] = found.reshape(self.d_inner.shape[:4] + (size,))

    def first_back(self, r):
        if r < self.rows:
            rows = self.row(r)
            weight = self.w_inner[...].reshape(self.width, self.units)
            self.grad[rows, :] = self.grad[rows, :] + contract(self.slope[rows, :], weight, 1, 1)
        if r == 0:
            for at in (GAIN_1, SHIFT_1, O_BIAS):
                self.col_sums[at] = jnp.zeros((8, self.width), f32)
            return
        gain = self.vector(GAIN_1)
        kinds = (GAIN_1, SHIFT_1, O_BIAS)
        sums = [self.col_sums[at] for at in kinds]
        for i in range(0, self.slots, 32):
            there = pl.ds((r - 1) * self.slots + i, 32)
            grad = self.grad[there, :]
            norm = self.norm[there, :]
            incoming = grad * gain
            plain = jnp.mean(incoming, axis=1, keepdims=True)
            along = jnp.mean(incoming * norm, axis=1, keepdims=True)
            attn = self.inverse[there, 0:1] * (incoming - plain - norm * along)
            self.grad[there, :] = attn
            low = attn.astype(bf16)
            self.grad_low[there, :] = low
            parts = (grad * norm, grad, low.astype(f32))
            sums = [total + folded(part) for total, part in zip(sums, parts, strict=True)]
        for at, total in zip(kinds, sums, strict=True):
            self.col_sums[at] = total

    def grad_output(self):
        context = self.w_outer[2 * self.tokens : 3 * self.tokens, :]
        found = contract(context, self.grad_low[...], 0, 0).astype(bf16)
        self.d_output[...] = found.reshape(self.d_output.shape)

    def grad_context(self, r):
        rows = self.row(r)
        weight = self.w_output[...].reshape(self.width, self.width)
        self.low[rows, :] = contract(self.grad_low[rows, :], weight, 1, 1).astype(bf16)

    def attend_back(self, r, together=4):
        most, span, width, wide = self.most, 4 * (self.width // HEADS), self.width, 2 * self.most
        spread = spread_heads(wide, span)
        first = iota((most, 4 * wide), 1) % wide < most

        def tiled(v):
            return jnp.where(spread, jnp.concatenate([v] * 4, axis=0), 0).astype(bf16)

        def two_pairs(pair):
            rows = pl.ds(pl.multiple_of(r * self.slots + pair * wide, wide), wide)
            for at in range(0, width, span):
                here = [slice(part * width + at, part * width + at + span) for part in range(4)]
                queries = tiled(self.active[rows, here[0]])
                keys = jnp.concatenate([self.active[rows, here[1]], self.slope[rows, here[0]]], axis=0)
                values = jnp.concatenate([self.active[rows, here[2]], self.slope[rows, here[1]]], axis=0)
                kept = self.active[rows, here[3]].astype(f32)
                mine, theirs = kept[:most], kept[most:]
                soft = jnp.concatenate(
                    [
                        jnp.where(first, mine, 0.0), jnp.where(first, 0.0, mine),
                        jnp.where(first, theirs, 0.0), jnp.where(first, 0.0, theirs),
                    ],
                    axis=0,
                )
                grad = tiled(self.low[rows, here[0]])
                grad_soft = contract(values, grad, 1, 1)
                delta = jnp.sum(soft * grad_soft, axis=0, keepdims=True)
                grad_scores = (soft * (grad_soft - delta)).astype(bf16)
                grad_values = contract(soft.astype(bf16), grad, 1, 0).astype(bf16)
                grad_keys = (contract(grad_scores, queries, 1, 0) * self.scale).astype(bf16)
                mixed = jnp.where(spread, contract(grad_scores, keys, 0, 0), 0.0)
                grad_queries = sum(mixed[h * wide : (h + 1) * wide, :] for h in range(4)) * self.scale
                self.active[rows, here[0]] = grad_queries.astype(bf16)
                self.active[rows, here[1]] = grad_keys[:wide]
                self.active[rows, here[2]] = grad_values[:wide]
                self.slope[rows, here[0]] = grad_keys[wide:]
                self.slope[rows, here[1]] = grad_values[wide:]

        @pl.loop(0, self.pairs // (2 * together))
        def _(several):
            for k in range(together):
                two_pairs(several * together + k)

    def input_weight(self, first, last):
        weight = self.w_inner[:, :, :, :, first:last] if self.fast else self.w_input[:, :, :, :, first:last]
        return weight.reshape(self.width, last - first)

    def return_other(self, r):
        rows = self.row(r)
        weight = self.input_weight(self.width, 3 * self.width)
        self.grad_low[rows, :] = contract(self.slope[rows, : 2 * self.width], weight, 1, 1).astype(bf16)

    def token_sums(self):
        width = self.width
        self.col_sums[Q_BIAS] = jnp.zeros((8, width), f32)
        self.col_sums[V_BIAS] = jnp.zeros((8, width), f32)

        @pl.loop(0, self.tokens // 64)
        def _(i):
            rows = block_rows(i, 64)
            self.col_sums[Q_BIAS] += folded(self.active[rows, :width].astype(f32))
            both = self.active[rows, 2 * width : 3 * width].astype(f32) + self.slope[rows, width : 2 * width].astype(f32)
            self.col_sums[V_BIAS] += folded(both)

        self.col_sums[GAIN_2] = self.k_sums[0:8, :]
        self.col_sums[SHIFT_2] = self.k_sums[8:16, :]
        self.col_sums[OUT_BIAS] = self.k_sums[16:24, :]
        rows = [jnp.sum(self.col_sums[at], axis=0, keepdims=True) for at in range(8)]
        units = jnp.sum(self.ff_sums[...], axis=0, keepdims=True)
        count = self.units // width
        rows += [units[:, k * width : (k + 1) * width] for k in range(count)]
        rows += [jnp.zeros((VECTORS - 8 - count, width), f32)]
        self.table[0] = jnp.concatenate(rows, axis=0)

    def grad_input_weight(self, part):
        width = self.width
        cols = pl.ds(pl.multiple_of(part * width, 128), width)
        target = self.d_inner

        def keep(found):
            target[:, :, :, :, cols] = found.astype(bf16).reshape(target.shape[:4] + (width,))

        if isinstance(part, int) and part == 0:
            keep(contract(self.w_outer[: self.tokens, :], self.active[:, :width], 0, 0))
            return
        there = pl.ds(pl.multiple_of((part - 1) * width, 128), width)
        found = contract(self.w_outer[: self.tokens, :], self.active[:, cols], 0, 0)
        keep(found + contract(self.w_outer[self.tokens : 2 * self.tokens, :], self.slope[:, there], 0, 0))

    def grad_hidden_in(self, r):
        rows = self.row(r)
        found = contract(self.active[rows, : 3 * self.width], self.input_weight(0, 3 * self.width), 1, 1)
        found = found + self.grad[rows, :] + self.back[rows, :].astype(f32)
        high = found.astype(bf16)
        rest = (found - high.astype(f32)).astype(bf16)
        back = out_of_frames(self.sizes_of(r, self.half), self.slots, self.most)
        self.norm[rows, :] = contract(back, high, 1, 0) + contract(back, rest, 1, 0)


BACKWARD_VMEM = 127 * 2**19


def backward_kernel(names, fast, sizes, routes, plan, *refs):
    refs = dict(zip(names, refs, strict=True))
    rows, slots, width, pairs = sizes
    tokens = rows * slots
    place = Place(lax.axis_size("rows"))
    run = Backward(refs, place, sizes)
    run.fast = fast
    partner = place.device(X=1 - place.x)
    in_outer = [run.w_outer.at[pl.ds(k * tokens, tokens)] for k in range(3)]
    loads = {
        Key.grad: (run.k_grad, run.grad), Key.low: (run.k_low, run.grad_low), Key.active: (run.k_active, run.active), Key.outer: (run.k_outer, run.w_outer),
        Key.slope: (run.k_slope, run.slope), Key.norm: (run.k_norm, run.norm), Key.inner: (run.k_inner, run.w_inner),
        Key.inverse: (run.k_inverse, run.inverse), Key.output: (run.k_output, run.w_output),
        Key.vectors: (run.k_vectors, run.vectors),
        Key.packed: (run.k_packed, run.active.at[:, pl.ds(0, 3 * width)]),
        Key.soft: (run.k_soft, run.active.at[:, pl.ds(3 * width, width)]),
        Key.pairs: (run.k_pairs, run.slope.at[:, pl.ds(0, 2 * width)]),
        Key.own: (run.k_own, in_outer[0]), Key.other: (run.k_other, in_outer[1]), Key.context: (run.k_context, in_outer[2]),
        Key.input: (run.k_input, run.w_inner.at[:, :, :, :, pl.ds(0, 3 * width)] if fast else run.w_input),
    }
    order = {name: k for k, name in enumerate(loads)}

    def load(name):
        return pltpu.make_async_copy(*loads[name], run.local_sem.at[order[name]])

    scatters = {}
    for name in (Key.low, Key.active):
        load(name).start()
    if fast:
        greet(place, neighbours(place))
        totals = Totals(place, run.table, run.table_in, run.table_send, run.table_recv)
        targets = {Key.outer: run.d_outer, Key.inner: run.d_inner, Key.output: run.d_output, Key.input: run.d_inner}
        for name, pieces in routes.items():
            for j, (route, starts, span) in enumerate(pieces):
                at = len(scatters)
                scatters[name, j] = Scatter(
                    targets[name], place, refs[Key.swapped, name, j], refs[Key.landed, name, j],
                    refs[Key.final, name, j], refs["g", name], run.piece_send.at[at], run.piece_recv.at[at],
                    route, starts, span,
                )
    else:
        greet(place, [partner])

    def returned(r):
        view = pl.ds(r * slots, slots)
        return pltpu.make_async_remote_copy(
            src_ref=run.grad_low.at[view],
            dst_ref=run.back.at[view],
            send_sem=run.row_send.at[r],
            recv_sem=run.row_recv.at[r],
            device_id=partner,
            device_id_type=MESH,
        )

    def put(r):
        view = pl.ds(r * slots, slots)
        return pltpu.make_async_copy(run.norm.at[view], run.grad_input.at[view], run.out_sem.at[r])

    whole = {Key.outer: Key.d_outer, Key.inner: Key.d_inner, Key.output: Key.d_output, Key.input: Key.d_inner}

    def keep(name):
        src = refs[whole[name]]
        if name == Key.input:
            src = src.at[:, :, :, :, pl.ds(0, 3 * width)]
        return pltpu.make_async_copy(src, refs["g", name], run.keep_sem.at[list(whole).index(name)])

    sent, written, summed = [], [], []

    def step(what, *detail):
        if what == Key.load:
            load(detail[0]).start()
        elif what == Key.loaded:
            load(detail[0]).wait()
        elif what == Key.event:
            if fast:
                scatters[detail[0], detail[1]].event(detail[2])
        elif what == Key.drain:
            if fast:
                for (name, _), scatter in scatters.items():
                    if name == detail[0]:
                        scatter.drain()
            else:
                keep(detail[0]).wait()
        elif what == Key.keep:
            if not fast:
                keep(detail[0]).start()
        elif what == Key.grad_inner:
            core = 1 - place.c if detail[0] == 0 else place.c
            run.grad_inner(core, *detail[1:])
        elif what == Key.grad_input_weight:
            run.grad_input_weight(detail[0])
        elif what == Key.send:
            returned(detail[0]).start()
            sent.append(detail[0])
        elif what == Key.back:
            returned(detail[0]).wait_recv()
        elif what == Key.total:
            if not fast:
                return
            if detail[0] < 0:
                totals.start(0)
                summed.append(True)
            else:
                totals.advance(detail[0])
        elif what == Key.put:
            put(detail[0]).start()
            written.append(detail[0])
        else:
            getattr(run, what.name)(*detail)

    for entry in plan:
        step(*entry)
    for r in sent:
        returned(r).wait_send()
    for r in written:
        put(r).wait()
    if fast:
        if summed: totals.drain()
        table = run.table[len(totals.steps)]
        devices = 2 * lax.axis_size("rows")
        piece = width // devices
        wide = piece * (run.units // width)
        per_row = width // wide
        upper = pltpu.roll(table[:8], (devices - place.index) * piece % width, axis=1)
        lower = jnp.where(iota((8, width), 0) == place.index // per_row, table[8:], 0.0)
        lower = jnp.sum(lower, axis=0, keepdims=True)
        lower = pltpu.roll(jnp.broadcast_to(lower, (8, width)), (per_row - place.index % per_row) * wide % width, axis=1)
        run.g_small[...] = jnp.concatenate([upper[:, :128], lower[:, :128]], axis=0)
    else:
        run.g_small[...] = run.table[0]


def backward_call(mesh_rows, fast, kept, lengths, routes, plan, sizes, units):
    rows, slots, width, pairs = sizes
    tokens = rows * slots
    nz = mesh_rows // 4
    hbm, vmem, smem = (pl.BlockSpec(memory_space=s) for s in (pl.ANY, pltpu.VMEM, pltpu.SMEM))
    ins = [
        Key.k_input, Key.k_output, Key.k_inner, Key.k_outer, Key.k_own, Key.k_other, Key.k_packed, Key.k_pairs, Key.k_soft, Key.k_context,
        Key.k_norm, Key.k_inverse, Key.k_active, Key.k_slope, Key.k_grad, Key.k_vectors, Key.k_low,
    ]
    kept = dict(kept)
    kept[Key.k_outer] = kept[Key.k_outer].reshape(units, width)
    args = [kept[name] for name in ins] + [kept[Key.k_sums], lengths]
    in_specs = [hbm] * len(ins) + [vmem, smem]
    tall = {Key.outer: units, Key.inner: width, Key.output: width, Key.input: width}
    wide = {Key.outer: width, Key.inner: units, Key.output: width, Key.input: 3 * width}
    lead = (2, nz, 2) if fast else (1, 1, 1)
    blocks = math.prod(lead)
    outs = {Key.grad_input: ((tokens, width), f32)}
    for name in tall:
        if fast:
            outs["g", name] = ((tall[name] // (2 * blocks), wide[name]), f32)
        else:
            outs["g", name] = (lead + (tall[name], wide[name]), bf16)
    outs[Key.g_small] = ((VECTORS, 128 if fast else width), f32)
    out_specs = [vmem if name == Key.g_small else hbm for name in outs]
    steps, partners = (3, nz + 3) if fast else (0, 0)
    scratch = {
        Key.w_outer: pltpu.VMEM((units, width), bf16), Key.w_inner: pltpu.VMEM(lead + (width // blocks, units), bf16),
        Key.w_output: pltpu.VMEM(lead + (width // blocks, width), bf16),
        Key.active: pltpu.VMEM((tokens, units), bf16), Key.slope: pltpu.VMEM((tokens, units), bf16),
        Key.grad: pltpu.VMEM((tokens, width), f32), Key.norm: pltpu.VMEM((tokens, width), f32),
        Key.inverse: pltpu.VMEM((tokens, 128), f32), Key.vectors: pltpu.VMEM((VECTORS, width), f32),
        Key.grad_low: pltpu.VMEM((tokens, width), bf16), Key.low: pltpu.VMEM((tokens, width), bf16),
        Key.back: pltpu.VMEM((tokens, width), bf16),
        Key.col_sums: pltpu.VMEM((8, 8, width), f32),
        Key.ff_sums: pltpu.VMEM((8, units), f32),
        Key.d_outer: pltpu.VMEM(lead + (units // blocks, width), bf16),
        Key.d_inner: pltpu.VMEM(lead + (width // blocks, units), bf16),
        Key.d_output: pltpu.VMEM(lead + (width // blocks, width), bf16),
        Key.table: pltpu.VMEM((steps + 1, VECTORS, width), f32),
        Key.local_sem: pltpu.SemaphoreType.DMA((17,)), Key.out_sem: pltpu.SemaphoreType.DMA((rows,)),
        Key.row_send: pltpu.SemaphoreType.DMA((rows,)), Key.row_recv: pltpu.SemaphoreType.DMA((rows,)),
    }
    if fast:
        pieces = sum(len(v) for v in routes.values())
        scratch.update({
            Key.table_in: pltpu.VMEM((partners, VECTORS, width), f32),
            Key.table_send: pltpu.SemaphoreType.DMA((partners,)), Key.table_recv: pltpu.SemaphoreType.DMA((partners,)),
            Key.piece_send: pltpu.SemaphoreType.DMA((pieces, nz + 4)),
            Key.piece_recv: pltpu.SemaphoreType.DMA((pieces, nz + 4)),
        })
        for name, found in routes.items():
            height = tall[name] // blocks
            for j, (_, _, span) in enumerate(found):
                scratch[Key.swapped, name, j] = pltpu.VMEM(lead + (height, span), bf16)
                scratch[Key.landed, name, j] = pltpu.VMEM(lead + (height, span), bf16)
                scratch[Key.final, name, j] = pltpu.VMEM((height, span), f32)
    else:
        scratch[Key.w_input] = pltpu.VMEM(lead + (width, 3 * width), bf16)
        scratch[Key.keep_sem] = pltpu.SemaphoreType.DMA((4,))
    names = ins + [Key.k_sums, Key.lengths] + list(outs) + list(scratch)
    found = pl.pallas_call(
        functools.partial(backward_kernel, names, fast, sizes, routes, plan),
        out_shape=[jax.ShapeDtypeStruct(*s) for s in outs.values()],
        in_specs=in_specs,
        out_specs=out_specs,
        scratch_shapes=list(scratch.values()),
        compiler_params=pltpu.CompilerParams(
            collective_id=1, has_side_effects=True, vmem_limit_bytes=BACKWARD_VMEM
        ),
        name="backward",
    )(*args)
    return dict(zip(outs, found, strict=True))


def plain_forward(rows, units):
    plan = []
    for r in range(rows):
        plan += [(Key.frame, r), (Key.send, r), (Key.cot, r)]
    plan += [(Key.loaded, Key.w_input), (Key.save, Key.k_vectors)]
    plan += [(Key.project_own, part) for part in range(3)] + [(Key.loaded, Key.w_output)]
    for r in range(rows):
        plan += [(Key.other, r), (Key.project_other, r, 0), (Key.project_other, r, 1)]
        plan += [(Key.attend_pairs, r), (Key.attend_padding, r)]
    plan += [(Key.first_norm, r) for r in range(rows + 1)]
    plan += [(Key.loaded, Key.w_inner), (Key.hidden_units, 0, units // 256), (Key.loaded, Key.w_outer)]
    plan += [(Key.save, Key.k_soft), (Key.saved, Key.k_soft)] + [(Key.second_norm, r) for r in range(rows + 1)]
    saved = (Key.layer_out, Key.k_input, Key.k_output, Key.k_inner, Key.k_outer, Key.k_own, Key.k_other, Key.k_packed, Key.k_pairs)
    saved += (Key.k_context, Key.k_norm, Key.k_inverse, Key.k_active, Key.k_slope, Key.k_grad, Key.k_low)
    return plan + [(Key.save, name) for name in saved]


def plain_backward(rows, units):
    first = (Key.vectors, Key.grad, Key.outer, Key.slope, Key.norm, Key.inner, Key.inverse, Key.output)
    plan = [(Key.load, name) for name in first] + [(Key.loaded, name) for name in first + (Key.low, Key.active)]
    plan += [(Key.lower_norm,), (Key.grad_outer,)]
    plan += [(Key.grad_hidden, 0, units // 384), (Key.keep, Key.outer)]
    plan += [(Key.grad_inner, core, part) for core in range(2) for part in range(units // 1536)] + [(Key.keep, Key.inner)]
    plan += [(Key.load, name) for name in (Key.own, Key.other, Key.context, Key.packed, Key.soft)]
    plan += [(Key.first_back, r) for r in range(rows + 1)]
    plan += [(Key.load, Key.pairs), (Key.load, Key.input)]
    plan += [(Key.loaded, name) for name in (Key.own, Key.other, Key.context, Key.packed, Key.soft, Key.pairs, Key.input)]
    plan += [(Key.grad_output,), (Key.keep, Key.output)]
    plan += [(Key.grad_context, r) for r in range(rows)] + [(Key.drain, Key.inner)]
    for r in range(rows):
        plan += [(Key.attend_back, r), (Key.return_other, r), (Key.send, r)]
    plan += [(Key.token_sums,)] + [(Key.grad_input_weight, part) for part in range(3)]
    plan += [(Key.keep, Key.input)]
    for r in range(rows):
        plan += [(Key.back, r), (Key.grad_hidden_in, r), (Key.put, r)]
    return plan + [(Key.drain, Key.outer), (Key.drain, Key.output), (Key.drain, Key.input)]


GATHER = {
    Key.w_input: (
        (("ZYX", "ZXY"), 0, 640, 0, 48),
        (("XZY", "XZY"), 640, 512, 0, 48),
    ),
    Key.w_output: (
        (("ZXY", "ZXY"), 0, 384, 0, 48),
    ),
    Key.w_inner: (
        (("ZYX", "XZY"), 0, 768, 0, 48),
        (("ZYX", "XZY"), 768, 768, 0, 48),
    ),
    Key.w_outer: (
        (("XZY", "ZYX"), 0, 384, 0, 96),
        (("XZY", "XYZ"), 0, 384, 96, 96),
    ),
}
SCATTER = {
    Key.outer: (
        (("XYZ", "ZYX"), (0, 512), 256),
        (("YXZ", "XYZ"), (256, 384), 128),
    ),
    Key.inner: (
        (("XYZ", "YZX"), (0, 1536), 768),
        (("XZY", "YXZ"), (768, 2304), 768),
    ),
    Key.output: (
        (("YXZ", "YZX"), (0, 384), 384),
    ),
    Key.input: (
        (("YXZ", "ZYX"), (0, 1536), 768),
        (("YXZ", "YXZ"), (768, 1152), 384),
    ),
}
FORWARD_PLAN = (
    (Key.lay, 0), (Key.event, Key.w_input, 0, 0), (Key.event, Key.w_input, 1, 0), (Key.frame, 0), (Key.frame, 1),
    (Key.frame, 2), (Key.frame, 3), (Key.lay, 1), (Key.lay, 2), (Key.lay, 3), (Key.cot, 0), (Key.cot, 1), (Key.total, 0),
    (Key.cot, 2), (Key.event, Key.w_output, 0, 0), (Key.event, Key.w_inner, 0, 0), (Key.cot, 3), (Key.send, 2),
    (Key.event, Key.w_input, 1, 1), (Key.event, Key.w_input, 0, 1), (Key.total, 1), (Key.event, Key.w_inner, 1, 0),
    (Key.event, Key.w_output, 0, 1), (Key.send, 0), (Key.event, Key.w_inner, 0, 1), (Key.event, Key.w_input, 0, 2),
    (Key.event, Key.w_outer, 1, 0), (Key.send, 3), (Key.event, Key.w_outer, 0, 0), (Key.event, Key.w_output, 0, 2),
    (Key.send, 1), (Key.event, Key.w_input, 1, 2), (Key.total, 2), (Key.event, Key.w_inner, 1, 1),
    (Key.event, Key.w_output, 0, 3), (Key.event, Key.w_input, 0, 3), (Key.event, Key.w_output, 0, 4),
    (Key.save, Key.k_output), (Key.event, Key.w_outer, 1, 1), (Key.event, Key.w_input, 0, 4), (Key.event, Key.w_inner, 0, 2),
    (Key.event, Key.w_input, 1, 3), (Key.event, Key.w_input, 1, 4), (Key.save, Key.k_input), (Key.save, Key.k_own),
    (Key.project_own, 0), (Key.project_own, 1), (Key.event, Key.w_outer, 0, 1), (Key.project_own, 2),
    (Key.save, Key.k_packed), (Key.save, Key.k_vectors), (Key.other, 0), (Key.project_other, 0, 0),
    (Key.project_other, 0, 1), (Key.attend_pairs, 0), (Key.event, Key.w_inner, 1, 2), (Key.attend_padding, 0),
    (Key.other, 1), (Key.project_other, 1, 0), (Key.project_other, 1, 1), (Key.attend_pairs, 1),
    (Key.attend_padding, 1), (Key.event, Key.w_outer, 1, 2), (Key.other, 2), (Key.project_other, 2, 0),
    (Key.project_other, 2, 1), (Key.attend_pairs, 2), (Key.attend_padding, 2), (Key.event, Key.w_inner, 0, 3),
    (Key.other, 3), (Key.project_other, 3, 0), (Key.project_other, 3, 1), (Key.save, Key.k_pairs), (Key.save, Key.k_other),
    (Key.attend_pairs, 3), (Key.save, Key.k_soft), (Key.event, Key.w_outer, 0, 2), (Key.event, Key.w_inner, 0, 4),
    (Key.attend_padding, 3), (Key.save, Key.k_context), (Key.first_norm, 0), (Key.first_norm, 1),
    (Key.event, Key.w_inner, 1, 3), (Key.first_norm, 2), (Key.first_norm, 3), (Key.first_norm, 4), (Key.save, Key.k_norm),
    (Key.save, Key.k_inverse), (Key.event, Key.w_inner, 1, 4), (Key.save, Key.k_inner), (Key.hidden_units, 0, 2),
    (Key.hidden_units, 2, 2), (Key.hidden_units, 4, 2), (Key.hidden_units, 6, 2), (Key.event, Key.w_outer, 0, 3),
    (Key.hidden_units, 8, 2), (Key.event, Key.w_outer, 1, 3), (Key.event, Key.w_outer, 0, 4), (Key.hidden_units, 10, 2),
    (Key.save, Key.k_active), (Key.save, Key.k_slope), (Key.event, Key.w_outer, 1, 4), (Key.save, Key.k_outer),
    (Key.saved, Key.k_soft), (Key.second_norm, 0), (Key.second_norm, 1), (Key.second_norm, 2), (Key.second_norm, 3),
    (Key.second_norm, 4), (Key.save, Key.layer_out), (Key.save, Key.k_grad), (Key.save, Key.k_low),
)
BACKWARD_PLAN = (
    (Key.loaded, Key.low), (Key.loaded, Key.active), (Key.load, Key.outer), (Key.load, Key.slope), (Key.load, Key.vectors),
    (Key.load, Key.norm), (Key.load, Key.inner), (Key.load, Key.grad), (Key.load, Key.inverse), (Key.load, Key.output),
    (Key.grad_outer,), (Key.event, Key.outer, 0, 0), (Key.loaded, Key.outer), (Key.loaded, Key.slope),
    (Key.loaded, Key.vectors), (Key.load, Key.packed), (Key.load, Key.soft), (Key.grad_hidden, 0, 2),
    (Key.grad_hidden, 2, 2), (Key.grad_hidden, 4, 2), (Key.event, Key.outer, 0, 1), (Key.grad_hidden, 6, 2),
    (Key.load, Key.own), (Key.load, Key.other), (Key.load, Key.context), (Key.loaded, Key.norm), (Key.lower_norm,),
    (Key.grad_inner, 0, 0), (Key.event, Key.inner, 0, 0), (Key.grad_inner, 1, 0), (Key.grad_inner, 0, 1),
    (Key.event, Key.inner, 1, 0), (Key.event, Key.inner, 0, 1), (Key.grad_inner, 1, 1), (Key.loaded, Key.inner),
    (Key.loaded, Key.inverse), (Key.loaded, Key.grad), (Key.first_back, 0), (Key.event, Key.inner, 1, 1),
    (Key.first_back, 1), (Key.first_back, 2), (Key.event, Key.outer, 1, 0), (Key.first_back, 3), (Key.first_back, 4),
    (Key.load, Key.pairs), (Key.load, Key.input), (Key.loaded, Key.context), (Key.loaded, Key.output), (Key.grad_output,),
    (Key.event, Key.inner, 0, 2), (Key.event, Key.outer, 1, 1), (Key.event, Key.output, 0, 0), (Key.grad_context, 0),
    (Key.grad_context, 1), (Key.grad_context, 2), (Key.grad_context, 3), (Key.loaded, Key.packed), (Key.loaded, Key.soft),
    (Key.loaded, Key.pairs), (Key.loaded, Key.input), (Key.attend_back, 0), (Key.event, Key.inner, 1, 2),
    (Key.event, Key.output, 0, 1), (Key.event, Key.outer, 0, 2), (Key.return_other, 0), (Key.send, 0),
    (Key.attend_back, 1), (Key.event, Key.outer, 1, 2), (Key.event, Key.inner, 0, 3), (Key.return_other, 1), (Key.send, 1),
    (Key.attend_back, 2), (Key.return_other, 2), (Key.send, 2), (Key.attend_back, 3), (Key.event, Key.inner, 1, 3),
    (Key.event, Key.output, 0, 2), (Key.return_other, 3), (Key.send, 3), (Key.token_sums,), (Key.total, -1),
    (Key.loaded, Key.own), (Key.loaded, Key.other), (Key.event, Key.inner, 0, 4), (Key.event, Key.outer, 0, 3),
    (Key.event, Key.outer, 1, 3), (Key.total, 0), (Key.event, Key.inner, 0, 5), (Key.event, Key.inner, 1, 4),
    (Key.drain, Key.inner), (Key.grad_input_weight, 0), (Key.grad_input_weight, 2), (Key.event, Key.input, 0, 0),
    (Key.event, Key.inner, 1, 5), (Key.grad_input_weight, 1), (Key.event, Key.input, 0, 1), (Key.event, Key.input, 1, 0),
    (Key.back, 0), (Key.grad_hidden_in, 0), (Key.put, 0), (Key.back, 1), (Key.grad_hidden_in, 1), (Key.put, 1),
    (Key.event, Key.outer, 1, 4), (Key.event, Key.output, 0, 3), (Key.event, Key.input, 1, 1), (Key.back, 2),
    (Key.grad_hidden_in, 2), (Key.put, 2), (Key.event, Key.outer, 1, 5), (Key.back, 3), (Key.grad_hidden_in, 3),
    (Key.put, 3), (Key.event, Key.outer, 0, 4), (Key.event, Key.input, 1, 2), (Key.event, Key.outer, 0, 5), (Key.total, 1),
    (Key.event, Key.input, 0, 2), (Key.event, Key.output, 0, 4), (Key.event, Key.input, 1, 3), (Key.event, Key.output, 0, 5),
    (Key.event, Key.input, 0, 3), (Key.total, 2), (Key.event, Key.input, 1, 4), (Key.event, Key.input, 1, 5),
    (Key.event, Key.input, 0, 4), (Key.event, Key.input, 0, 5), (Key.drain, Key.outer), (Key.drain, Key.output),
    (Key.drain, Key.input),
)


def gather_routes(masters):
    return {
        name: [(route, (row, count), (col, span)) for route, col, span, row, count in found]
        for name, found in GATHER.items()
    }


def scatter_routes(width, units):
    return SCATTER


def forward_steps(rows, nz, units):
    return FORWARD_PLAN


def backward_steps(rows, nz):
    return BACKWARD_PLAN


def spread(masters, vectors):
    gathered = [lax.all_gather(v.astype(bf16), ("pair", "rows"), axis=0, tiled=True) for v in masters]
    rows = [lax.all_gather(v, ("pair", "rows"), axis=0, tiled=True) for v in vectors]
    width = rows[0].shape[0]
    table = jnp.concatenate(rows).reshape(-1, width)
    return gathered, [jnp.pad(table, ((0, VECTORS - table.shape[0]), (0, 0)))]


def gather_sums(found, units):
    def summed(v):
        return lax.psum_scatter(v.astype(f32), ("pair", "rows"), scatter_dimension=0, tiled=True)

    weights = {name: summed(found[name].reshape(found[name].shape[3:])) for name in found if name != Key.g_small}
    table = found[Key.g_small]
    width = table.shape[1]
    small = [summed(table[k]) for k in range(8)] + [summed(table[8 : 8 + units // width].reshape(units))]
    return weights, small


def settle(arrays):
    def kernel(*refs):
        count = len(refs) // 2
        copies = [
            pltpu.make_async_copy(refs[k], refs[count + k], refs[-1].at[k]) for k in range(count)
        ]
        for copy in copies:
            copy.start()
        for copy in copies:
            copy.wait()

    return pl.pallas_call(
        kernel,
        out_shape=[jax.ShapeDtypeStruct(v.shape, v.dtype) for v in arrays],
        in_specs=[pl.BlockSpec(memory_space=pl.ANY)] * len(arrays),
        out_specs=[pl.BlockSpec(memory_space=pl.ANY)] * len(arrays),
        scratch_shapes=[pltpu.SemaphoreType.DMA((len(arrays),))],
        compiler_params=pltpu.CompilerParams(vmem_limit_bytes=BACKWARD_VMEM),
        name="k_settle",
    )(*arrays)


def shards(rows_axis, *args):
    (
        hidden_in, input_proj, query_bias, value_bias, output_proj, output_bias, first_gain, first_shift,
        inner_proj, inner_bias, outer_proj, outer_bias, second_gain, second_shift, cotangent, pair_lengths,
    ) = args
    row_count, _, slots, width = hidden_in.shape
    units = inner_proj.shape[1]
    share = input_proj.shape[0]
    fast = rows_axis % 4 == 0 and share % 8 == 0
    masters = (input_proj, output_proj, inner_proj, outer_proj)
    vectors = (
        query_bias, value_bias, output_bias, first_gain, first_shift, outer_bias, second_gain, second_shift,
        inner_bias,
    )
    if fast:
        routes_f, plan_f = gather_routes(masters), forward_steps(row_count, rows_axis // 4, units)
        routes_b, plan_b = scatter_routes(width, units), backward_steps(row_count, rows_axis // 4)
        small = [v.reshape(1, -1) for v in vectors]
    else:
        routes_f, routes_b = {}, {}
        plan_f, plan_b = plain_forward(row_count, units), plain_backward(row_count, units)
        masters, small = spread(masters, vectors)
    sizes = (row_count, slots, width, pair_lengths.shape[2])
    kept = forward_call(
        rows_axis, fast, hidden_in[:, 0], cotangent[:, 0], masters, small, pair_lengths, routes_f, plan_f
    )
    found = backward_call(rows_axis, fast, kept, pair_lengths, routes_b, plan_b, sizes, units)
    layer_out, grad_input = kept[Key.layer_out], found.pop(Key.grad_input)
    if fast:
        weights = (Key.input, Key.output, Key.inner, Key.outer)
        results = settle([layer_out, grad_input] + [found["g", name] for name in weights])
        layer_out, grad_input = results[:2]
        found.update(zip([("g", name) for name in weights], results[2:], strict=True))
        table = found[Key.g_small]
        sums = [table[k, :share] for k in range(8)] + [table[8, : inner_bias.shape[0]]]
    else:
        found, sums = gather_sums(found, units)
    return (
        layer_out.reshape(hidden_in.shape), grad_input.reshape(hidden_in.shape), found["g", Key.input], sums[Q_BIAS], sums[V_BIAS], found["g", Key.output], sums[O_BIAS],
        sums[GAIN_1], sums[SHIFT_1], found["g", Key.inner], sums[FF_ROW], found["g", Key.outer], sums[OUT_BIAS],
        sums[GAIN_2], sums[SHIFT_2],
    )


def solution(mesh):
    tokens = P("rows", "pair", None, None)
    matrix = P(("pair", "rows"), None)
    vector = P(("pair", "rows"))
    weights = (
        matrix, vector, vector, matrix, vector, vector, vector, matrix, vector, matrix, vector, vector, vector
    )
    return jax.shard_map(
        functools.partial(shards, mesh.shape["rows"]),
        mesh=mesh,
        in_specs=(tokens, *weights, tokens, P("rows", None, None)),
        out_specs=(tokens, tokens, *weights),
        check_vma=False,
    )
```

```python
import enum
import functools
import math

import jax
import jax.numpy as jnp
from jax import lax
from jax.experimental import pallas as pl
from jax.experimental.pallas import tpu as pltpu
from jax.sharding import PartitionSpec as P

HEADS = 12
EPSILON = 1e-12
MESH = pl.DeviceIdType.MESH
bf16 = jnp.bfloat16
f32 = jnp.float32
ALL = slice(None)
MASKED = -1e30
VECTORS = 16
Q_BIAS, V_BIAS, O_BIAS, GAIN_1, SHIFT_1, OUT_BIAS, GAIN_2, SHIFT_2, FF_ROW = range(9)


def contract(left, right, left_dim, right_dim):
    return lax.dot_general(
        left, right, (((left_dim,), (right_dim,)), ((), ())), preferred_element_type=f32
    )


def iota(shape, dim):
    return lax.broadcasted_iota(jnp.int32, shape, dim)


def rounded(v):
    return v.astype(bf16).astype(f32)


class Key(enum.Enum):
    active = 0
    attend_back = 1
    attend_padding = 2
    attend_pairs = 3
    back = 4
    col_sums = 5
    context = 6
    cot = 7
    cotangent = 8
    d_inner = 9
    d_outer = 10
    d_output = 11
    drain = 12
    event = 13
    ff_bias = 14
    ff_sums = 15
    final = 16
    first_back = 17
    first_norm = 18
    frame = 19
    framed = 20
    from_sibling = 21
    g_small = 22
    gain_sum = 23
    grad = 24
    grad_context = 25
    grad_hidden = 26
    grad_hidden_in = 27
    grad_inner = 28
    grad_input = 29
    grad_input_weight = 30
    grad_low = 31
    grad_outer = 32
    grad_output = 33
    hidden = 34
    hidden_in = 35
    hidden_units = 36
    inner = 37
    input = 38
    inverse = 39
    k_active = 40
    k_context = 41
    k_grad = 42
    k_inner = 43
    k_input = 44
    k_inverse = 45
    k_low = 46
    k_norm = 47
    k_other = 48
    k_outer = 49
    k_output = 50
    k_own = 51
    k_packed = 52
    k_pairs = 53
    k_slope = 54
    k_soft = 55
    k_sums = 56
    k_vectors = 57
    keep = 58
    keep_sem = 59
    landed = 60
    lay = 61
    layer_out = 62
    lengths = 63
    load = 64
    loaded = 65
    local_sem = 66
    low = 67
    low_sum = 68
    lower_norm = 69
    m_inner = 70
    m_input = 71
    m_outer = 72
    m_output = 73
    norm = 74
    other = 75
    out_sem = 76
    outer = 77
    output = 78
    own = 79
    packed = 80
    pairs = 81
    pairs_other = 82
    piece_recv = 83
    piece_send = 84
    project_other = 85
    project_own = 86
    put = 87
    return_other = 88
    row_recv = 89
    row_send = 90
    save = 91
    saved = 92
    second_norm = 93
    send = 94
    shift_sum = 95
    slope = 96
    soft = 97
    sums = 98
    swap_recv = 99
    swap_send = 100
    swapped = 101
    table = 102
    table_in = 103
    table_recv = 104
    table_send = 105
    token_sums = 106
    total = 107
    vector = 108
    vectors = 109
    w_inner = 110
    w_input = 111
    w_outer = 112
    w_output = 113


def attributes(refs):
    return {key.name: ref for key, ref in refs.items() if isinstance(key, Key)}


class Place:
    def __init__(self, rows):
        self.nz = rows // 4
        r = lax.axis_index("rows")
        self.x = lax.axis_index("pair")
        self.z = r // 4
        self.y = (r // 2) % 2
        self.c = r % 2
        self.index = self.x * rows + r
        self.own = {"X": self.x, "Z": self.z, "Y": self.y}

    def device(self, **other):
        at = {"X": self.x, "Z": self.z, "Y": self.y, "C": self.c, **other}
        return {"pair": at["X"], "rows": (at["Z"] * 2 + at["Y"]) * 2 + at["C"]}

    def peers(self, dim):
        if dim == "Z":
            return [(self.z + k) % self.nz for k in range(1, self.nz)]
        return [1 - self.own[dim]]

    def sources(self, dim):
        if dim == "Z":
            return [(self.z + self.nz - k) % self.nz for k in range(1, self.nz)]
        return [1 - self.own[dim]]

    def first_slot(self, dim):
        return {"X": 0, "Y": 1, "Z": 2}[dim]

    def slots(self):
        return self.nz + 1


def slab(buf, place, gathered, at, rows, cols):
    own = {**place.own, **at}
    lead = tuple(ALL if d in gathered else own[d] for d in "XZY")
    return buf.at[lead + (rows, cols)]


class Gather:
    def __init__(self, buf, place, send, recv, routes, rows, col, width):
        self.buf, self.place, self.send, self.recv, self.routes = buf, place, send, recv, routes
        self.rows, self.col, self.width = rows, col, width
        self.half = buf.shape[-1] // 2

    def cols(self, core):
        return pl.ds(pl.multiple_of(core * self.half + self.col, 128), self.width)

    def per_core(self, act):
        if self.routes[0] == self.routes[1]:
            act(self.routes[0])
            return
        for core in range(2):
            pl.when(self.place.c == core)(functools.partial(act, self.routes[core]))

    def copy(self, view, slot, device):
        return pltpu.make_async_remote_copy(
            src_ref=view,
            dst_ref=view,
            send_sem=self.send.at[slot],
            recv_sem=self.recv.at[slot],
            device_id=device,
            device_id_type=MESH,
        )

    def sends(self, route, stage):
        dim, gathered = route[stage], route[:stage]
        view = slab(self.buf, self.place, gathered, {}, self.rows, self.cols(self.place.c))
        first = self.place.first_slot(dim)
        return [
            self.copy(view, first + k, self.place.device(**{dim: peer}))
            for k, peer in enumerate(self.place.peers(dim))
        ]

    def arrivals(self, route, stage, core):
        dim, gathered = route[stage], route[:stage]
        return [
            slab(self.buf, self.place, gathered, {dim: peer}, self.rows, self.cols(core))
            for peer in self.place.sources(dim)
        ]

    def hand_ons(self, route, stage, core):
        device = self.place.device(C=1 - self.place.c)
        base = self.place.slots()
        if stage == 0:
            view = slab(self.buf, self.place, route[:1], {}, self.rows, self.cols(core))
            return [self.copy(view, base, device)]
        first = base + 1 + (stage - 1) * (self.place.nz - 1)
        return [
            self.copy(view, first + k, device)
            for k, view in enumerate(self.arrivals(route, stage, core))
        ]

    def start(self, stage):
        def act(route):
            for copy in self.sends(route, stage):
                copy.start()

        self.per_core(act)

    def arrived(self, stage):
        def act(route):
            dim = route[stage]
            first = self.place.first_slot(dim)
            device = self.place.device()
            for k, view in enumerate(self.arrivals(route, stage, self.place.c)):
                self.copy(view, first + k, device).wait_recv()
            if stage < 2:
                for copy in self.sends(route, stage + 1):
                    copy.start()
            for copy in self.hand_ons(route, stage, self.place.c):
                copy.start()

        self.per_core(act)

    def event(self, number):
        if number == 0:
            self.start(0)
        elif number < 4:
            self.arrived(number - 1)
        else:
            self.complete()

    def complete(self):
        def other(route):
            for stage in range(3):
                for copy in self.hand_ons(route, stage, 1 - self.place.c):
                    copy.wait_recv()

        if self.routes[0] == self.routes[1]:
            other(self.routes[0])
        else:
            for core in range(2):
                pl.when(self.place.c == 1 - core)(functools.partial(other, self.routes[core]))

    def drain(self):
        def act(route):
            for stage in range(3):
                for copy in self.sends(route, stage) + self.hand_ons(route, stage, self.place.c):
                    copy.wait_send()

        self.per_core(act)


def greet(place, devices):
    barrier = pltpu.get_barrier_semaphore()
    for device in devices:
        pl.semaphore_signal(barrier, inc=1, device_id=device, device_id_type=MESH)
    pl.semaphore_wait(barrier, len(devices))


class Totals:
    def __init__(self, place, table, landed, send, recv):
        self.place, self.table, self.landed, self.send, self.recv = place, table, landed, send, recv
        x, y = 1 - place.x, 1 - place.y
        self.steps = [
            [place.device(C=1 - place.c)],
            [place.device(X=x), place.device(Y=y), place.device(X=x, Y=y)],
            [place.device(Z=peer) for peer in place.peers("Z")],
        ]

    def copies(self, step):
        first = sum(len(found) for found in self.steps[:step])
        return [
            pltpu.make_async_remote_copy(
                src_ref=self.table.at[step],
                dst_ref=self.landed.at[first + k],
                send_sem=self.send.at[first + k],
                recv_sem=self.recv.at[first + k],
                device_id=device,
                device_id_type=MESH,
            )
            for k, device in enumerate(self.steps[step])
        ]

    def start(self, step):
        for copy in self.copies(step):
            copy.start()

    def advance(self, step):
        first = sum(len(found) for found in self.steps[:step])
        total = self.table[step]
        for k, copy in enumerate(self.copies(step)):
            copy.wait_recv()
            total = total + self.landed[first + k]
        self.table[step + 1] = total
        if step + 1 < len(self.steps):
            self.start(step + 1)

    def drain(self):
        for step in range(len(self.steps)):
            for copy in self.copies(step):
                copy.wait_send()


def neighbours(place):
    x, y = 1 - place.x, 1 - place.y
    found = [place.device(C=1 - place.c), place.device(X=x), place.device(Y=y), place.device(X=x, Y=y)]
    return found + [place.device(Z=peer) for peer in place.peers("Z")]


def source_slots(slots, sizes, most):
    frame, offset = slots // most, slots % most
    total = sum(sizes[1:], sizes[0])
    found, start = slots, jnp.int32(0)
    for p, size in enumerate(sizes):
        mine = jnp.where(offset < size, start + offset, total + slots - (start + size))
        found = jnp.where(frame == p, mine, found)
        start = start + size
    return found


def holds_token(slots, sizes, most):
    frame, offset = slots // most, slots % most
    held = jnp.zeros(slots.shape, f32)
    for p, size in enumerate(sizes):
        held = jnp.where((frame == p) & (offset < size), 1.0, held)
    return held


def into_frames(sizes, slots, most):
    source = source_slots(iota((slots, 1), 0), sizes, most)
    return (iota((slots, slots), 1) == source).astype(f32).astype(bf16)


def out_of_frames(sizes, slots, most):
    source = source_slots(iota((1, slots), 1), sizes, most)
    return (iota((slots, slots), 0) == source).astype(f32).astype(bf16)


def folded(v):
    return jnp.sum(v.reshape(v.shape[0] // 8, 8, v.shape[1]), axis=0)


def spread_heads(tokens, span):
    shape = (4 * tokens, span)
    return iota(shape, 0) // tokens == iota(shape, 1) // (span // 4)


def block_rows(i, size):
    return pl.ds(pl.multiple_of(i * size, size), size)


class Forward:
    def __init__(self, refs, place, sizes):
        self.__dict__.update(attributes(refs))
        self.place = place
        self.rows, self.slots, self.width, self.pairs = sizes
        self.most = self.slots // self.pairs
        self.half = place.x
        self.bias_rows = self.ff_bias.shape[1] // self.width
        self.scale = (self.width // HEADS) ** (-0.5)

    def sizes_of(self, row, half):
        return [self.lengths[row, half, p] for p in range(self.pairs)]

    def row(self, r):
        return pl.ds(r * self.slots, self.slots)

    def vector(self, at, count=1):
        found = rounded(self.vectors[at : at + count, :])
        return found if count == 1 else found.reshape(1, count * self.width)

    def frame_hidden(self, r):
        frames = into_frames(self.sizes_of(r, self.half), self.slots, self.most)
        self.own[self.row(r), :] = contract(frames, self.hidden[self.row(r), :], 1, 0).astype(bf16)

    def frame_cotangent(self, r):
        sizes = self.sizes_of(r, self.half)
        frames = into_frames(sizes, self.slots, self.most)
        held = holds_token(iota((self.slots, 1), 0), sizes, self.most)
        moved = contract(frames, self.cot[self.row(r), :], 1, 0) * held
        self.cot[self.row(r), :] = moved.astype(bf16)

    def project_own(self, part):
        cols = slice(part * self.width, (part + 1) * self.width)
        weight = self.w_input[:, :, :, :, cols].reshape(self.width, self.width)
        acc = contract(self.own[...], weight, 1, 0)
        if part == 0:
            acc = acc + self.vector(Q_BIAS)
        if part == 2:
            acc = acc + self.vector(V_BIAS)
        self.packed[:, cols] = acc.astype(bf16)

    def project_other(self, r, part):
        cols = slice(part * self.width, (part + 1) * self.width)
        from_cols = slice((part + 1) * self.width, (part + 2) * self.width)
        weight = self.w_input[:, :, :, :, from_cols].reshape(self.width, self.width)
        acc = contract(self.other[self.row(r), :], weight, 1, 0)
        if part == 1:
            acc = acc + self.vector(V_BIAS)
        self.pairs_other[self.row(r), cols] = acc.astype(bf16)

    def attend_pairs(self, r, together=4):
        most, span, wide = self.most, 4 * (self.width // HEADS), 2 * self.most
        spread = spread_heads(wide, span)
        key, query = iota((2 * wide, 4 * wide), 0), iota((2 * wide, 4 * wide), 1)
        key_frame, same = key % wide // most, key % wide // most == query % wide // most
        slot = key % most

        def two_pairs(pair):
            rows = pl.ds(pl.multiple_of(r * self.slots + pair * wide, wide), wide)
            counts = [self.lengths[r, half, 2 * pair + k] for half in (self.half, 1 - self.half) for k in range(2)]
            mine = jnp.where(key_frame == 0, counts[0], counts[1])
            theirs = jnp.where(key_frame == 0, counts[2], counts[3])
            allowed = same & (slot < jnp.where(key < wide, mine, theirs))
            for at in range(0, self.width, span):
                queries = self.packed[rows, at : at + span]
                keys = jnp.concatenate(
                    [
                        self.packed[rows, self.width + at : self.width + at + span],
                        self.pairs_other[rows, at : at + span],
                    ],
                    axis=0,
                )
                values = jnp.concatenate(
                    [
                        self.packed[rows, 2 * self.width + at : 2 * self.width + at + span],
                        self.pairs_other[rows, self.width + at : self.width + at + span],
                    ],
                    axis=0,
                )
                tiled = jnp.where(spread, jnp.concatenate([queries] * 4, axis=0), 0).astype(bf16)
                scores = jnp.where(allowed, contract(keys, tiled, 1, 1) * self.scale, MASKED)
                raw = jnp.exp(scores - jnp.max(scores, axis=0, keepdims=True))
                soft = raw * (1.0 / jnp.sum(raw, axis=0, keepdims=True))
                kept = [soft[k * most : (k + 1) * most] + soft[(k + 1) * most : (k + 2) * most] for k in (0, 2)]
                self.soft[rows, at : at + span] = jnp.concatenate(kept, axis=0).astype(bf16)
                mixed = contract(soft.astype(bf16), values, 0, 0)
                mixed = jnp.where(spread, mixed, 0.0)
                context = sum(mixed[h * wide : (h + 1) * wide, :] for h in range(4))
                self.context[rows, at : at + span] = context.astype(bf16)

        @pl.loop(0, self.pairs // (2 * together))
        def _(several):
            for k in range(together):
                two_pairs(several * together + k)

    def attend_padding(self, r, together=6):
        sizes = self.sizes_of(r, self.half)
        head = self.width // HEADS
        held_key = holds_token(iota((1, self.slots), 1), sizes, self.most)
        held_query = holds_token(iota((self.slots, 1), 0), sizes, self.most)
        pad_key = jnp.broadcast_to(held_key, (2 * self.slots, self.slots)) < 0.5
        pad_query = jnp.broadcast_to(held_query, (self.slots, 2 * head)) < 0.5
        left = iota((self.slots, 2 * head), 1) < head
        rows = self.row(r)

        def two_heads(pair):
            at = pl.multiple_of(pair * 2 * head, 2 * head)
            queries = self.packed[rows, pl.ds(at, 2 * head)] * self.scale
            keys = self.packed[rows, pl.ds(pl.multiple_of(self.width + at, 2 * head), 2 * head)]
            values = self.packed[rows, pl.ds(pl.multiple_of(2 * self.width + at, 2 * head), 2 * head)]
            both = jnp.concatenate([jnp.where(left, queries, 0), jnp.where(left, 0, queries)], axis=0)
            scores = jnp.where(pad_key, contract(both.astype(bf16), keys, 1, 1), MASKED)
            raw = jnp.exp(scores - jnp.max(scores, axis=1, keepdims=True))
            total = jnp.sum(raw, axis=1, keepdims=True)
            found = contract(raw.astype(bf16), values, 1, 0) * (1.0 / total)
            padded = jnp.where(left, found[: self.slots], found[self.slots :]).astype(bf16)
            cols = pl.ds(at, 2 * head)
            self.context[rows, cols] = jnp.where(pad_query, padded, self.context[rows, cols])

        @pl.loop(0, HEADS // 2 // together)
        def _(several):
            for k in range(together):
                two_heads(several * together + k)

    def first_norm(self, r):
        if r < self.rows:
            weight = self.w_output[...].reshape(self.width, self.width)
            self.sums[r % 2] = contract(self.context[self.row(r), :], weight, 1, 0)
        if r == 0:
            return
        bias, gain, shift = self.vector(O_BIAS), self.vector(GAIN_1), self.vector(SHIFT_1)
        size = 32
        for i in range(0, self.slots, size):
            there = pl.ds((r - 1) * self.slots + i, size)
            total = self.own[there, :].astype(f32) + self.sums[(r - 1) % 2, i : i + size, :] + bias
            centered = total - jnp.mean(total, axis=1, keepdims=True)
            inverse = lax.rsqrt(jnp.mean(centered * centered, axis=1, keepdims=True) + EPSILON)
            norm = centered * inverse
            self.norm[there, :] = norm
            self.inverse[there, :] = jnp.broadcast_to(inverse, (size, 128))
            self.low[there, :] = (norm * gain + shift).astype(bf16)

    def hidden_units(self, first, count, size=256):
        @pl.loop(first, first + count)
        def _(n):
            cols = pl.ds(pl.multiple_of(n * size, size), size)
            weight = self.w_inner[:, :, :, :, cols].reshape(self.width, size)
            bias = rounded(self.ff_bias[:, cols])
            for r in range(self.rows):
                inner = contract(self.low[self.row(r), :], weight, 1, 0) + bias
                share = 0.5 * (1.0 + lax.erf(inner * (0.5**0.5)))
                slope = share + inner * (jnp.exp(-0.5 * inner * inner) * ((2.0 * math.pi) ** -0.5))
                self.active[self.row(r), cols] = (inner * share).astype(bf16)
                self.slope[self.row(r), cols] = slope.astype(bf16)

    def second_norm(self, r):
        if r < self.rows:
            weight = self.w_outer[...].reshape(self.w_inner.shape[-1], self.width)
            self.sums[r % 2] = contract(self.active[self.row(r), :], weight, 1, 0)
        if r == 0:
            return
        gain_1, shift_1 = self.vector(GAIN_1), self.vector(SHIFT_1)
        bias, gain, shift = self.vector(OUT_BIAS), self.vector(GAIN_2), self.vector(SHIFT_2)
        size = 32
        sums = [self.gain_sum[...], self.shift_sum[...], self.low_sum[...]]
        for i in range(0, self.slots, size):
            there = pl.ds((r - 1) * self.slots + i, size)
            total = (self.norm[there, :] * gain_1 + shift_1) + self.sums[(r - 1) % 2, i : i + size, :] + bias
            centered = total - jnp.mean(total, axis=1, keepdims=True)
            inverse = lax.rsqrt(jnp.mean(centered * centered, axis=1, keepdims=True) + EPSILON)
            norm = centered * inverse
            self.framed[i : i + size, :] = (norm * gain + shift).astype(bf16)
            upstream = self.cot[there, :].astype(f32)
            incoming = upstream * gain
            plain = jnp.mean(incoming, axis=1, keepdims=True)
            along = jnp.mean(incoming * norm, axis=1, keepdims=True)
            grad = inverse * (incoming - plain - norm * along)
            low = grad.astype(bf16)
            self.grad[there, :] = grad
            self.soft[there, :] = low
            parts = (upstream * norm, upstream, low.astype(f32))
            sums = [total + folded(part) for total, part in zip(sums, parts, strict=True)]
        self.gain_sum[...], self.shift_sum[...], self.low_sum[...] = sums
        back = out_of_frames(self.sizes_of(r - 1, self.half), self.slots, self.most)
        self.hidden[self.row(r - 1), :] = contract(back, self.framed[...], 1, 0).astype(bf16)


FORWARD_VMEM = 127 * 2**19
ORDER = None


def forward_kernel(names, fast, sizes, routes, plan, *refs):
    refs = dict(zip(names, refs, strict=True))
    rows, slots, width, pairs = sizes
    place = Place(lax.axis_size("rows"))
    run = Forward(refs, place, sizes)
    sibling = place.device(C=1 - place.c)
    partner = place.device(X=1 - place.x)

    def local(src, dst, slot):
        return pltpu.make_async_copy(src, dst, run.local_sem.at[slot])

    load_hidden = local(run.hidden_in, run.hidden, 0)
    load_cot = local(run.cotangent, run.cot, 1)
    load_hidden.start()
    load_cot.start()

    if fast:
        greet(place, neighbours(place))
    else:
        greet(place, [partner])

    def hidden_copy(r):
        view = pl.ds(r * slots, slots)
        return pltpu.make_async_remote_copy(
            src_ref=run.own.at[view],
            dst_ref=run.other.at[view],
            send_sem=run.row_send.at[r],
            recv_sem=run.row_recv.at[r],
            device_id=partner,
            device_id_type=MESH,
        )

    weights = [Key.w_input, Key.w_output, Key.w_inner, Key.w_outer]
    masters = [Key.m_input, Key.m_output, Key.m_inner, Key.m_outer]
    gathers = {}
    drains = []
    if fast:
        totals = Totals(place, run.table, run.table_in, run.table_send, run.table_recv)
        for k, (weight, master) in enumerate(zip(weights, masters, strict=True)):
            buf = refs[weight]
            half = buf.shape[-1] // 2
            for j, (route, (row, count), (col, span)) in enumerate(routes.get(weight, ())):
                piece = Gather(
                    buf, place, run.piece_send.at[len(gathers)], run.piece_recv.at[len(gathers)],
                    route, pl.ds(row, count), col, span,
                )
                gathers[weight, j] = piece

        def swap(k):
            master = refs[masters[k]]
            half = master.shape[-1] // 2
            theirs = pl.ds(pl.multiple_of((1 - place.c) * half, 128), half)
            return pltpu.make_async_remote_copy(
                src_ref=master.at[:, theirs],
                dst_ref=refs[Key.from_sibling, k],
                send_sem=run.swap_send.at[k],
                recv_sem=run.swap_recv.at[k],
                device_id=sibling,
                device_id_type=MESH,
            )

        def lay(k):
            swap(k).wait_recv()
            master, buf = refs[masters[k]], refs[weights[k]]
            half = master.shape[-1] // 2
            cols = pl.ds(pl.multiple_of(place.c * half, 128), half)
            mine, theirs = master[:, cols], refs[Key.from_sibling, k][...]
            first = place.c == 0
            both = jnp.concatenate([jnp.where(first, mine, theirs), jnp.where(first, theirs, mine)], axis=0)
            buf[place.x, place.z, place.y, :, cols] = both.astype(bf16)

        for k in range(4):
            swap(k).start()
        run.table[0] = jnp.zeros((VECTORS, width), f32)
        for k in range(9):
            share = refs[Key.vector, k]
            run.table[0, k : k + 1, 0 : share.shape[1]] = share[...]
        piece = refs[Key.vector, 0].shape[1]
        wide = refs[Key.vector, 8].shape[1]
        per_row = width // wide
        upper = pltpu.roll(run.table[0, 0:8, :], place.index * piece, axis=1)
        lower = pltpu.roll(run.table[0, 8:16, :], (place.index % per_row) * wide, axis=1)
        lower = jnp.broadcast_to(lower[:1, :], (8, width))
        lower = jnp.where(iota((8, width), 0) == place.index // per_row, lower, 0.0)
        run.table[0, 0:8, :] = upper
        run.table[0, 8:16, :] = lower
        totals.start(0)

    def spread_vectors(table):
        run.vectors[...] = table
        for k in range(run.bias_rows):
            run.ff_bias[:, k * width : (k + 1) * width] = table[FF_ROW + k : FF_ROW + k + 1, :]

    if not fast:
        for k, weight in enumerate(weights):
            local(refs[masters[k]], refs[weight], 2 + k).start()
        spread_vectors(refs[Key.vector, 0][...])

    saved = [
        (Key.k_input, Key.w_input), (Key.k_output, Key.w_output), (Key.k_inner, Key.w_inner), (Key.k_outer, Key.w_outer),
        (Key.k_own, Key.own), (Key.k_other, Key.other), (Key.k_packed, Key.packed), (Key.k_pairs, Key.pairs_other),
        (Key.k_soft, Key.soft), (Key.k_context, Key.context), (Key.k_norm, Key.norm), (Key.k_inverse, Key.inverse),
        (Key.k_active, Key.active), (Key.k_slope, Key.slope), (Key.k_grad, Key.grad), (Key.k_vectors, Key.vectors), (Key.k_low, Key.soft),
        (Key.layer_out, Key.hidden),
    ]
    saves = {name: local(refs[src], refs[name], 6 + k) for k, (name, src) in enumerate(saved) if name in refs}
    started = []
    sent = []

    def save(name):
        if name in saves:
            saves[name].start()
            started.append(name)

    def step(what, *detail):
        if what == Key.event:
            if fast:
                gathers[detail[0], detail[1]].event(detail[2])
        elif what == Key.lay:
            if fast:
                lay(detail[0])
        elif what == Key.total:
            if fast:
                totals.advance(detail[0])
                if detail[0] + 1 == len(totals.steps):
                    spread_vectors(run.table[detail[0] + 1])
        elif what == Key.loaded:
            if not fast:
                k = weights.index(detail[0])
                local(refs[masters[k]], refs[detail[0]], 2 + k).wait()
        elif what == Key.frame:
            if detail[0] == 0:
                load_hidden.wait()
            run.frame_hidden(detail[0])
        elif what == Key.send:
            hidden_copy(detail[0]).start()
            sent.append(detail[0])
        elif what == Key.other:
            hidden_copy(detail[0]).wait_recv()
        elif what == Key.cot:
            if detail[0] == 0:
                load_cot.wait()
            run.frame_cotangent(detail[0])
        elif what == Key.save:
            save(detail[0])
        elif what == Key.saved:
            saves[detail[0]].wait()
            started.remove(detail[0])
        else:
            getattr(run, what.name)(*detail)

    run.gain_sum[...] = jnp.zeros_like(run.gain_sum)
    run.shift_sum[...] = jnp.zeros_like(run.shift_sum)
    run.low_sum[...] = jnp.zeros_like(run.low_sum)
    for entry in plan:
        step(*entry)
    run.k_sums[0:8, :] = run.gain_sum[...]
    run.k_sums[8:16, :] = run.shift_sum[...]
    run.k_sums[16:24, :] = run.low_sum[...]
    for r in sent:
        hidden_copy(r).wait_send()
    if fast:
        for gather in gathers.values():
            gather.drain()
        for k in range(4):
            swap(k).wait_send()
        totals.drain()
    for name in started:
        saves[name].wait()


def forward_plan(rows, units):
    plan = []
    for r in range(rows):
        plan += [(Key.frame, r), (Key.send, r)]
    for k in range(4):
        plan += [(Key.lay, k)]
    for n in range(5):
        plan += [(Key.total, n)]
    for r in range(rows):
        plan += [(Key.cot, r)]
    for w in (Key.w_input, Key.w_output, Key.w_inner, Key.w_outer):
        for e in range(5):
            plan += [(Key.event, w, 0, e)]
        plan += [(Key.loaded, w)]
    for part in range(3):
        plan += [(Key.project_own, part)]
    for r in range(rows):
        plan += [(Key.other, r), (Key.project_other, r, 0), (Key.project_other, r, 1)]
        plan += [(Key.attend_pairs, r), (Key.attend_padding, r), (Key.first_norm, r)]
    plan += [(Key.hidden_units, 0, units)]
    for r in range(rows):
        plan += [(Key.second_norm, r)]
    for name in (Key.layer_out, Key.k_input, Key.k_output, Key.k_inner, Key.k_outer, Key.k_own, Key.k_other, Key.k_packed, Key.k_pairs,
                 Key.k_soft, Key.k_context, Key.k_norm, Key.k_inverse, Key.k_active, Key.k_slope, Key.k_grad, Key.k_vectors):
        plan += [(Key.save, name)]
    return plan


def forward_call(mesh_rows, fast, hidden, cot, masters, small, lengths, routes, plan, with_saves=True):
    rows, slots, width = hidden.shape
    pairs = lengths.shape[2]
    tokens = rows * slots
    units = masters[2].shape[1]
    nz = mesh_rows // 4
    tall = [width, width, width, units]
    wide = [3 * width, width, units, width]
    if fast:
        shapes = [(2, nz, 2, tall[k] // (4 * nz), wide[k]) for k in range(4)]
    else:
        shapes = [(1, 1, 1, tall[k], wide[k]) for k in range(4)]
    weights = [Key.w_input, Key.w_output, Key.w_inner, Key.w_outer]
    ins = [Key.hidden_in, Key.cotangent, Key.m_input, Key.m_output, Key.m_inner, Key.m_outer]
    ins += [(Key.vector, k) for k in range(len(small))] + [Key.lengths]
    hbm, vmem, smem = (pl.BlockSpec(memory_space=s) for s in (pl.ANY, pltpu.VMEM, pltpu.SMEM))
    if fast:
        args = [hidden.reshape(tokens, width), cot.reshape(tokens, width), *masters, *small, lengths]
    else:
        args = [hidden.reshape(tokens, width), cot.reshape(tokens, width)]
        args += [m.reshape(s) for m, s in zip(masters, shapes, strict=True)] + [*small, lengths]
    in_specs = [hbm, hbm] + [vmem if fast else hbm] * 4 + [vmem] * len(small) + [smem]
    outs = {Key.layer_out: ((tokens, width), bf16), Key.k_sums: ((24, width), f32)}
    saved = {
        Key.k_input: (shapes[0], bf16), Key.k_output: (shapes[1], bf16), Key.k_inner: (shapes[2], bf16),
        Key.k_outer: (shapes[3], bf16), Key.k_own: ((tokens, width), bf16), Key.k_other: ((tokens, width), bf16),
        Key.k_packed: ((tokens, 3 * width), bf16), Key.k_pairs: ((tokens, 2 * width), bf16),
        Key.k_soft: ((tokens, width), bf16), Key.k_context: ((tokens, width), bf16),
        Key.k_norm: ((tokens, width), f32), Key.k_inverse: ((tokens, 128), f32),
        Key.k_active: ((tokens, units), bf16), Key.k_slope: ((tokens, units), bf16),
        Key.k_grad: ((tokens, width), f32), Key.k_low: ((tokens, width), bf16), Key.k_vectors: ((VECTORS, width), f32),
    }
    if with_saves:
        outs.update(saved)
    out_specs = [vmem if name == Key.k_sums else hbm for name in outs]
    scratch = {
        Key.w_input: pltpu.VMEM(shapes[0], bf16), Key.w_output: pltpu.VMEM(shapes[1], bf16),
        Key.w_inner: pltpu.VMEM(shapes[2], bf16), Key.w_outer: pltpu.VMEM(shapes[3], bf16),
        Key.hidden: pltpu.VMEM((tokens, width), bf16), Key.cot: pltpu.VMEM((tokens, width), bf16),
        Key.own: pltpu.VMEM((tokens, width), bf16), Key.other: pltpu.VMEM((tokens, width), bf16),
        Key.packed: pltpu.VMEM((tokens, 3 * width), bf16), Key.pairs_other: pltpu.VMEM((tokens, 2 * width), bf16),
        Key.context: pltpu.VMEM((tokens, width), bf16), Key.soft: pltpu.VMEM((tokens, width), bf16),
        Key.norm: pltpu.VMEM((tokens, width), f32), Key.inverse: pltpu.VMEM((tokens, 128), f32),
        Key.low: pltpu.VMEM((tokens, width), bf16), Key.active: pltpu.VMEM((tokens, units), bf16),
        Key.slope: pltpu.VMEM((tokens, units), bf16), Key.grad: pltpu.VMEM((tokens, width), f32),
        Key.sums: pltpu.VMEM((2, slots, width), f32), Key.framed: pltpu.VMEM((slots, width), bf16),
        Key.vectors: pltpu.VMEM((VECTORS, width), f32), Key.ff_bias: pltpu.VMEM((1, units), f32),
        Key.gain_sum: pltpu.VMEM((8, width), f32), Key.shift_sum: pltpu.VMEM((8, width), f32),
        Key.low_sum: pltpu.VMEM((8, width), f32),
        Key.local_sem: pltpu.SemaphoreType.DMA((6 + len(saved) + 1,)),
        Key.row_send: pltpu.SemaphoreType.DMA((rows,)), Key.row_recv: pltpu.SemaphoreType.DMA((rows,)),
    }
    if fast:
        steps, partners = 3, nz + 3
        pieces = sum(len(v) for v in routes.values())
        slots_each = nz + 1 + 1 + 2 * (nz - 1)
        scratch.update({
            Key.table: pltpu.VMEM((steps + 1, VECTORS, width), f32), Key.table_in: pltpu.VMEM((partners, VECTORS, width), f32),
            Key.table_send: pltpu.SemaphoreType.DMA((partners,)), Key.table_recv: pltpu.SemaphoreType.DMA((partners,)),
            Key.piece_send: pltpu.SemaphoreType.DMA((pieces, slots_each)),
            Key.piece_recv: pltpu.SemaphoreType.DMA((pieces, slots_each)),
            Key.swap_send: pltpu.SemaphoreType.DMA((4,)), Key.swap_recv: pltpu.SemaphoreType.DMA((4,)),
        })
        for k in range(4):
            scratch[Key.from_sibling, k] = pltpu.VMEM((masters[k].shape[0], wide[k] // 2), f32)
    names = ins + list(outs) + list(scratch)
    sizes = (rows, slots, width, pairs)
    body = functools.partial(forward_kernel, names, fast, sizes, routes, plan)
    found = pl.pallas_call(
        body,
        out_shape=[jax.ShapeDtypeStruct(*s) for s in outs.values()],
        in_specs=in_specs,
        out_specs=out_specs,
        scratch_shapes=list(scratch.values()),
        compiler_params=pltpu.CompilerParams(
            collective_id=0, has_side_effects=True, vmem_limit_bytes=FORWARD_VMEM
        ),
        name="forward",
    )(*args)
    return dict(zip(outs, found, strict=True))


class Scatter:
    def __init__(self, buf, place, swapped, landed, final, out, send, recv, routes, starts, width):
        self.buf, self.place, self.swapped, self.landed = buf, place, swapped, landed
        self.final, self.out, self.send, self.recv, self.routes = final, out, send, recv, routes
        self.starts, self.width = starts, width
        self.sizes = dict(zip("XZY", buf.shape[:3], strict=True))
        self.core_rows = buf.shape[3] // 2

    def cols(self, core):
        first, second = self.starts
        return pl.ds(pl.multiple_of(first + core * (second - first), 128), self.width)

    def remote(self, src, dst, slot, device):
        return pltpu.make_async_remote_copy(
            src_ref=src,
            dst_ref=dst,
            send_sem=self.send.at[slot],
            recv_sem=self.recv.at[slot],
            device_id=device,
            device_id_type=MESH,
        )

    def per_core(self, act):
        if self.routes[0] == self.routes[1]:
            act(self.routes[0])
            return
        for core in range(2):
            pl.when(self.place.c == core)(functools.partial(act, self.routes[core]))

    def lead(self, route, stage, at):
        own = {**self.place.own, **at}
        fixed = route[: stage + 1]
        return tuple(own[d] if d in fixed else ALL for d in "XZY")

    def swap(self):
        place = self.place
        src = self.buf.at[ALL, ALL, ALL, ALL, self.cols(1 - place.c)]
        return self.remote(src, self.swapped, 0, place.device(C=1 - place.c))

    def sends(self, route, stage):
        dim = route[stage]
        mine = self.landed.at[self.lead(route, stage, {})]
        found = []
        for k, peer in enumerate(self.place.peers(dim)):
            src = self.buf.at[self.lead(route, stage, {dim: peer}) + (ALL, self.cols(self.place.c))]
            found.append(self.remote(src, mine, 1 + self.place.first_slot(dim) + k, self.place.device(**{dim: peer})))
        return found

    def arrivals(self, route, stage):
        dim = route[stage]
        found = []
        for k, peer in enumerate(self.place.sources(dim)):
            view = self.landed.at[self.lead(route, stage, {dim: peer})]
            found.append(self.remote(view, view, 1 + self.place.first_slot(dim) + k, self.place.device()))
        return found

    def blocks(self, free, body):
        total = math.prod(self.sizes[d] for d in free)

        def visit(i):
            at = dict(self.place.own)
            for d in reversed(free):
                at[d] = i % self.sizes[d]
                i = i // self.sizes[d]
            body((at["X"], at["Z"], at["Y"]), at)

        if total == 1:
            visit(0)
        else:
            pl.loop(0, total)(visit)

    def start_swap(self):
        self.swap().start()

    def add_swapped(self):
        self.swap().wait_recv()
        cols = self.cols(self.place.c)

        def body(block, at):
            there = block + (ALL, cols)
            total = self.buf[there].astype(f32) + self.swapped[block].astype(f32)
            self.buf[there] = total.astype(bf16)

        self.blocks("XZY", body)

        def act(route):
            for copy in self.sends(route, 0):
                copy.start()

        self.per_core(act)

    def add_stage(self, stage):
        cols = self.cols(self.place.c)

        def act(route):
            dim = route[stage]
            for copy in self.arrivals(route, stage):
                copy.wait_recv()
            sources = self.place.sources(dim)

            def body(block, at):
                total = self.buf[block + (ALL, cols)].astype(f32)
                for peer in sources:
                    theirs = {**at, dim: peer}
                    total = total + self.landed[theirs["X"], theirs["Z"], theirs["Y"]].astype(f32)
                if stage < 2:
                    self.buf[block + (ALL, cols)] = total.astype(bf16)
                else:
                    self.final[...] = total

            self.blocks("".join(d for d in "XZY" if d not in route[: stage + 1]), body)
            if stage < 2:
                for copy in self.sends(route, stage + 1):
                    copy.start()

        self.per_core(act)
        if stage == 2:
            for copy in self.hand_over():
                copy.start()

    def hand_over(self):
        place, count = self.place, self.core_rows
        cols = self.cols(place.c)
        mine = self.final.at[pl.ds(pl.multiple_of(place.c * count, 8), count)]
        theirs = self.final.at[pl.ds(pl.multiple_of((1 - place.c) * count, 8), count)]
        there = self.remote(theirs, self.out.at[:, cols], 1 + place.slots(), place.device(C=1 - place.c))
        here = pltpu.make_async_copy(mine, self.out.at[:, cols], self.send.at[2 + place.slots()])
        return [there, here]

    def finish(self):
        there, here = self.hand_over()
        here.wait()
        there.wait_send()
        view = self.out.at[:, self.cols(1 - self.place.c)]
        self.remote(view, view, 1 + self.place.slots(), self.place.device()).wait_recv()

    def drain(self):
        self.swap().wait_send()

        def act(route):
            for stage in range(3):
                for copy in self.sends(route, stage):
                    copy.wait_send()

        self.per_core(act)

    def event(self, number):
        if number == 0:
            self.start_swap()
        elif number == 1:
            self.add_swapped()
        elif number < 5:
            self.add_stage(number - 2)
        else:
            self.finish()


class Backward:
    def __init__(self, refs, place, sizes):
        self.__dict__.update(attributes(refs))
        self.place = place
        self.rows, self.slots, self.width, self.pairs = sizes
        self.most = self.slots // self.pairs
        self.half = place.x
        self.scale = (self.width // HEADS) ** (-0.5)
        self.tokens = self.rows * self.slots
        self.units = self.active.shape[1]

    def sizes_of(self, row, half):
        return [self.lengths[row, half, p] for p in range(self.pairs)]

    def row(self, r):
        return pl.ds(r * self.slots, self.slots)

    def vector(self, at):
        return rounded(self.vectors[at : at + 1, :])

    def lower_norm(self):
        gain, shift = self.vector(GAIN_1), self.vector(SHIFT_1)

        @pl.loop(0, self.tokens // 64)
        def _(i):
            rows = block_rows(i, 64)
            self.low[rows, :] = (self.norm[rows, :] * gain + shift).astype(bf16)

    def grad_outer(self):
        nz = self.d_outer.shape[1]
        parts = self.d_outer.shape[0] * nz
        size = self.units // parts

        @pl.loop(0, parts)
        def _(i):
            found = contract(self.active[:, pl.ds(pl.multiple_of(i * size, 128), size)], self.grad_low[...], 0, 0)
            self.d_outer[i // nz, i % nz] = found.astype(bf16).reshape(self.d_outer.shape[2:])

    def grad_hidden(self, first, count, size=384):
        @pl.loop(first, first + count)
        def _(n):
            cols = pl.ds(pl.multiple_of(n * size, size), size)
            weight = self.w_outer[cols, :]
            total = jnp.zeros((8, size), f32)
            for r in range(self.rows):
                found = contract(self.grad_low[self.row(r), :], weight, 1, 1)
                low = (found * self.slope[self.row(r), cols].astype(f32)).astype(bf16)
                self.slope[self.row(r), cols] = low
                total = total + folded(low.astype(f32))
            self.ff_sums[:, cols] = total

    def grad_inner(self, core, part, size=768):
        half = self.units // 2
        cols = pl.ds(pl.multiple_of(core * half + part * size, 128), size)
        found = contract(self.low[...], self.slope[:, cols], 0, 0).astype(bf16)
        self.d_inner[:, :, :, :, cols] = found.reshape(self.d_inner.shape[:4] + (size,))

    def first_back(self, r):
        if r < self.rows:
            rows = self.row(r)
            weight = self.w_inner[...].reshape(self.width, self.units)
            self.grad[rows, :] = self.grad[rows, :] + contract(self.slope[rows, :], weight, 1, 1)
        if r == 0:
            for at in (GAIN_1, SHIFT_1, O_BIAS):
                self.col_sums[at] = jnp.zeros((8, self.width), f32)
            return
        gain = self.vector(GAIN_1)
        kinds = (GAIN_1, SHIFT_1, O_BIAS)
        sums = [self.col_sums[at] for at in kinds]
        for i in range(0, self.slots, 32):
            there = pl.ds((r - 1) * self.slots + i, 32)
            grad = self.grad[there, :]
            norm = self.norm[there, :]
            incoming = grad * gain
            plain = jnp.mean(incoming, axis=1, keepdims=True)
            along = jnp.mean(incoming * norm, axis=1, keepdims=True)
            attn = self.inverse[there, 0:1] * (incoming - plain - norm * along)
            self.grad[there, :] = attn
            low = attn.astype(bf16)
            self.grad_low[there, :] = low
            parts = (grad * norm, grad, low.astype(f32))
            sums = [total + folded(part) for total, part in zip(sums, parts, strict=True)]
        for at, total in zip(kinds, sums, strict=True):
            self.col_sums[at] = total

    def grad_output(self):
        context = self.w_outer[2 * self.tokens : 3 * self.tokens, :]
        found = contract(context, self.grad_low[...], 0, 0).astype(bf16)
        self.d_output[...] = found.reshape(self.d_output.shape)

    def grad_context(self, r):
        rows = self.row(r)
        weight = self.w_output[...].reshape(self.width, self.width)
        self.low[rows, :] = contract(self.grad_low[rows, :], weight, 1, 1).astype(bf16)

    def attend_back(self, r, together=4):
        most, span, width, wide = self.most, 4 * (self.width // HEADS), self.width, 2 * self.most
        spread = spread_heads(wide, span)
        first = iota((most, 4 * wide), 1) % wide < most

        def tiled(v):
            return jnp.where(spread, jnp.concatenate([v] * 4, axis=0), 0).astype(bf16)

        def two_pairs(pair):
            rows = pl.ds(pl.multiple_of(r * self.slots + pair * wide, wide), wide)
            for at in range(0, width, span):
                here = [slice(part * width + at, part * width + at + span) for part in range(4)]
                queries = tiled(self.active[rows, here[0]])
                keys = jnp.concatenate([self.active[rows, here[1]], self.slope[rows, here[0]]], axis=0)
                values = jnp.concatenate([self.active[rows, here[2]], self.slope[rows, here[1]]], axis=0)
                kept = self.active[rows, here[3]].astype(f32)
                mine, theirs = kept[:most], kept[most:]
                soft = jnp.concatenate(
                    [
                        jnp.where(first, mine, 0.0), jnp.where(first, 0.0, mine),
                        jnp.where(first, theirs, 0.0), jnp.where(first, 0.0, theirs),
                    ],
                    axis=0,
                )
                grad = tiled(self.low[rows, here[0]])
                grad_soft = contract(values, grad, 1, 1)
                delta = jnp.sum(soft * grad_soft, axis=0, keepdims=True)
                grad_scores = (soft * (grad_soft - delta)).astype(bf16)
                grad_values = contract(soft.astype(bf16), grad, 1, 0).astype(bf16)
                grad_keys = (contract(grad_scores, queries, 1, 0) * self.scale).astype(bf16)
                mixed = jnp.where(spread, contract(grad_scores, keys, 0, 0), 0.0)
                grad_queries = sum(mixed[h * wide : (h + 1) * wide, :] for h in range(4)) * self.scale
                self.active[rows, here[0]] = grad_queries.astype(bf16)
                self.active[rows, here[1]] = grad_keys[:wide]
                self.active[rows, here[2]] = grad_values[:wide]
                self.slope[rows, here[0]] = grad_keys[wide:]
                self.slope[rows, here[1]] = grad_values[wide:]

        @pl.loop(0, self.pairs // (2 * together))
        def _(several):
            for k in range(together):
                two_pairs(several * together + k)

    def input_weight(self, first, last):
        weight = self.w_inner[:, :, :, :, first:last] if self.fast else self.w_input[:, :, :, :, first:last]
        return weight.reshape(self.width, last - first)

    def return_other(self, r):
        rows = self.row(r)
        weight = self.input_weight(self.width, 3 * self.width)
        self.grad_low[rows, :] = contract(self.slope[rows, : 2 * self.width], weight, 1, 1).astype(bf16)

    def token_sums(self):
        width = self.width
        self.col_sums[Q_BIAS] = jnp.zeros((8, width), f32)
        self.col_sums[V_BIAS] = jnp.zeros((8, width), f32)

        @pl.loop(0, self.tokens // 64)
        def _(i):
            rows = block_rows(i, 64)
            self.col_sums[Q_BIAS] += folded(self.active[rows, :width].astype(f32))
            both = self.active[rows, 2 * width : 3 * width].astype(f32) + self.slope[rows, width : 2 * width].astype(f32)
            self.col_sums[V_BIAS] += folded(both)

        self.col_sums[GAIN_2] = self.k_sums[0:8, :]
        self.col_sums[SHIFT_2] = self.k_sums[8:16, :]
        self.col_sums[OUT_BIAS] = self.k_sums[16:24, :]
        rows = [jnp.sum(self.col_sums[at], axis=0, keepdims=True) for at in range(8)]
        units = jnp.sum(self.ff_sums[...], axis=0, keepdims=True)
        count = self.units // width
        rows += [units[:, k * width : (k + 1) * width] for k in range(count)]
        rows += [jnp.zeros((VECTORS - 8 - count, width), f32)]
        self.table[0] = jnp.concatenate(rows, axis=0)

    def grad_input_weight(self, part):
        width = self.width
        cols = pl.ds(pl.multiple_of(part * width, 128), width)
        target = self.d_inner

        def keep(found):
            target[:, :, :, :, cols] = found.astype(bf16).reshape(target.shape[:4] + (width,))

        if isinstance(part, int) and part == 0:
            keep(contract(self.w_outer[: self.tokens, :], self.active[:, :width], 0, 0))
            return
        there = pl.ds(pl.multiple_of((part - 1) * width, 128), width)
        found = contract(self.w_outer[: self.tokens, :], self.active[:, cols], 0, 0)
        keep(found + contract(self.w_outer[self.tokens : 2 * self.tokens, :], self.slope[:, there], 0, 0))

    def grad_hidden_in(self, r):
        rows = self.row(r)
        found = contract(self.active[rows, : 3 * self.width], self.input_weight(0, 3 * self.width), 1, 1)
        found = found + self.grad[rows, :] + self.back[rows, :].astype(f32)
        high = found.astype(bf16)
        rest = (found - high.astype(f32)).astype(bf16)
        back = out_of_frames(self.sizes_of(r, self.half), self.slots, self.most)
        self.norm[rows, :] = contract(back, high, 1, 0) + contract(back, rest, 1, 0)


BACKWARD_VMEM = 127 * 2**19


def backward_kernel(names, fast, sizes, routes, plan, *refs):
    refs = dict(zip(names, refs, strict=True))
    rows, slots, width, pairs = sizes
    tokens = rows * slots
    place = Place(lax.axis_size("rows"))
    run = Backward(refs, place, sizes)
    run.fast = fast
    partner = place.device(X=1 - place.x)
    in_outer = [run.w_outer.at[pl.ds(k * tokens, tokens)] for k in range(3)]
    loads = {
        Key.grad: (run.k_grad, run.grad), Key.low: (run.k_low, run.grad_low), Key.active: (run.k_active, run.active), Key.outer: (run.k_outer, run.w_outer),
        Key.slope: (run.k_slope, run.slope), Key.norm: (run.k_norm, run.norm), Key.inner: (run.k_inner, run.w_inner),
        Key.inverse: (run.k_inverse, run.inverse), Key.output: (run.k_output, run.w_output),
        Key.vectors: (run.k_vectors, run.vectors),
        Key.packed: (run.k_packed, run.active.at[:, pl.ds(0, 3 * width)]),
        Key.soft: (run.k_soft, run.active.at[:, pl.ds(3 * width, width)]),
        Key.pairs: (run.k_pairs, run.slope.at[:, pl.ds(0, 2 * width)]),
        Key.own: (run.k_own, in_outer[0]), Key.other: (run.k_other, in_outer[1]), Key.context: (run.k_context, in_outer[2]),
        Key.input: (run.k_input, run.w_inner.at[:, :, :, :, pl.ds(0, 3 * width)] if fast else run.w_input),
    }
    order = {name: k for k, name in enumerate(loads)}

    def load(name):
        return pltpu.make_async_copy(*loads[name], run.local_sem.at[order[name]])

    scatters = {}
    for name in (Key.low, Key.active):
        load(name).start()
    if fast:
        greet(place, neighbours(place))
        totals = Totals(place, run.table, run.table_in, run.table_send, run.table_recv)
        targets = {Key.outer: run.d_outer, Key.inner: run.d_inner, Key.output: run.d_output, Key.input: run.d_inner}
        for name, pieces in routes.items():
            for j, (route, starts, span) in enumerate(pieces):
                at = len(scatters)
                scatters[name, j] = Scatter(
                    targets[name], place, refs[Key.swapped, name, j], refs[Key.landed, name, j],
                    refs[Key.final, name, j], refs["g", name], run.piece_send.at[at], run.piece_recv.at[at],
                    route, starts, span,
                )
    else:
        greet(place, [partner])

    def returned(r):
        view = pl.ds(r * slots, slots)
        return pltpu.make_async_remote_copy(
            src_ref=run.grad_low.at[view],
            dst_ref=run.back.at[view],
            send_sem=run.row_send.at[r],
            recv_sem=run.row_recv.at[r],
            device_id=partner,
            device_id_type=MESH,
        )

    def put(r):
        view = pl.ds(r * slots, slots)
        return pltpu.make_async_copy(run.norm.at[view], run.grad_input.at[view], run.out_sem.at[r])

    whole = {Key.outer: Key.d_outer, Key.inner: Key.d_inner, Key.output: Key.d_output, Key.input: Key.d_inner}

    def keep(name):
        src = refs[whole[name]]
        if name == Key.input:
            src = src.at[:, :, :, :, pl.ds(0, 3 * width)]
        return pltpu.make_async_copy(src, refs["g", name], run.keep_sem.at[list(whole).index(name)])

    sent, written, summed = [], [], []

    def step(what, *detail):
        if what == Key.load:
            load(detail[0]).start()
        elif what == Key.loaded:
            load(detail[0]).wait()
        elif what == Key.event:
            if fast:
                scatters[detail[0], detail[1]].event(detail[2])
        elif what == Key.drain:
            if fast:
                for (name, _), scatter in scatters.items():
                    if name == detail[0]:
                        scatter.drain()
            else:
                keep(detail[0]).wait()
        elif what == Key.keep:
            if not fast:
                keep(detail[0]).start()
        elif what == Key.grad_inner:
            core = 1 - place.c if detail[0] == 0 else place.c
            run.grad_inner(core, *detail[1:])
        elif what == Key.grad_input_weight:
            run.grad_input_weight(detail[0])
        elif what == Key.send:
            returned(detail[0]).start()
            sent.append(detail[0])
        elif what == Key.back:
            returned(detail[0]).wait_recv()
        elif what == Key.total:
            if not fast:
                return
            if detail[0] < 0:
                totals.start(0)
                summed.append(True)
            else:
                totals.advance(detail[0])
        elif what == Key.put:
            put(detail[0]).start()
            written.append(detail[0])
        else:
            getattr(run, what.name)(*detail)

    for entry in plan:
        step(*entry)
    for r in sent:
        returned(r).wait_send()
    for r in written:
        put(r).wait()
    if fast:
        if summed: totals.drain()
        table = run.table[len(totals.steps)]
        devices = 2 * lax.axis_size("rows")
        piece = width // devices
        wide = piece * (run.units // width)
        per_row = width // wide
        upper = pltpu.roll(table[:8], (devices - place.index) * piece % width, axis=1)
        lower = jnp.where(iota((8, width), 0) == place.index // per_row, table[8:], 0.0)
        lower = jnp.sum(lower, axis=0, keepdims=True)
        lower = pltpu.roll(jnp.broadcast_to(lower, (8, width)), (per_row - place.index % per_row) * wide % width, axis=1)
        run.g_small[...] = jnp.concatenate([upper[:, :128], lower[:, :128]], axis=0)
    else:
        run.g_small[...] = run.table[0]


def backward_call(mesh_rows, fast, kept, lengths, routes, plan, sizes, units):
    rows, slots, width, pairs = sizes
    tokens = rows * slots
    nz = mesh_rows // 4
    hbm, vmem, smem = (pl.BlockSpec(memory_space=s) for s in (pl.ANY, pltpu.VMEM, pltpu.SMEM))
    ins = [
        Key.k_input, Key.k_output, Key.k_inner, Key.k_outer, Key.k_own, Key.k_other, Key.k_packed, Key.k_pairs, Key.k_soft, Key.k_context,
        Key.k_norm, Key.k_inverse, Key.k_active, Key.k_slope, Key.k_grad, Key.k_vectors, Key.k_low,
    ]
    kept = dict(kept)
    kept[Key.k_outer] = kept[Key.k_outer].reshape(units, width)
    args = [kept[name] for name in ins] + [kept[Key.k_sums], lengths]
    in_specs = [hbm] * len(ins) + [vmem, smem]
    tall = {Key.outer: units, Key.inner: width, Key.output: width, Key.input: width}
    wide = {Key.outer: width, Key.inner: units, Key.output: width, Key.input: 3 * width}
    lead = (2, nz, 2) if fast else (1, 1, 1)
    blocks = math.prod(lead)
    outs = {Key.grad_input: ((tokens, width), f32)}
    for name in tall:
        if fast:
            outs["g", name] = ((tall[name] // (2 * blocks), wide[name]), f32)
        else:
            outs["g", name] = (lead + (tall[name], wide[name]), bf16)
    outs[Key.g_small] = ((VECTORS, 128 if fast else width), f32)
    out_specs = [vmem if name == Key.g_small else hbm for name in outs]
    steps, partners = (3, nz + 3) if fast else (0, 0)
    scratch = {
        Key.w_outer: pltpu.VMEM((units, width), bf16), Key.w_inner: pltpu.VMEM(lead + (width // blocks, units), bf16),
        Key.w_output: pltpu.VMEM(lead + (width // blocks, width), bf16),
        Key.active: pltpu.VMEM((tokens, units), bf16), Key.slope: pltpu.VMEM((tokens, units), bf16),
        Key.grad: pltpu.VMEM((tokens, width), f32), Key.norm: pltpu.VMEM((tokens, width), f32),
        Key.inverse: pltpu.VMEM((tokens, 128), f32), Key.vectors: pltpu.VMEM((VECTORS, width), f32),
        Key.grad_low: pltpu.VMEM((tokens, width), bf16), Key.low: pltpu.VMEM((tokens, width), bf16),
        Key.back: pltpu.VMEM((tokens, width), bf16),
        Key.col_sums: pltpu.VMEM((8, 8, width), f32),
        Key.ff_sums: pltpu.VMEM((8, units), f32),
        Key.d_outer: pltpu.VMEM(lead + (units // blocks, width), bf16),
        Key.d_inner: pltpu.VMEM(lead + (width // blocks, units), bf16),
        Key.d_output: pltpu.VMEM(lead + (width // blocks, width), bf16),
        Key.table: pltpu.VMEM((steps + 1, VECTORS, width), f32),
        Key.local_sem: pltpu.SemaphoreType.DMA((17,)), Key.out_sem: pltpu.SemaphoreType.DMA((rows,)),
        Key.row_send: pltpu.SemaphoreType.DMA((rows,)), Key.row_recv: pltpu.SemaphoreType.DMA((rows,)),
    }
    if fast:
        pieces = sum(len(v) for v in routes.values())
        scratch.update({
            Key.table_in: pltpu.VMEM((partners, VECTORS, width), f32),
            Key.table_send: pltpu.SemaphoreType.DMA((partners,)), Key.table_recv: pltpu.SemaphoreType.DMA((partners,)),
            Key.piece_send: pltpu.SemaphoreType.DMA((pieces, nz + 4)),
            Key.piece_recv: pltpu.SemaphoreType.DMA((pieces, nz + 4)),
        })
        for name, found in routes.items():
            height = tall[name] // blocks
            for j, (_, _, span) in enumerate(found):
                scratch[Key.swapped, name, j] = pltpu.VMEM(lead + (height, span), bf16)
                scratch[Key.landed, name, j] = pltpu.VMEM(lead + (height, span), bf16)
                scratch[Key.final, name, j] = pltpu.VMEM((height, span), f32)
    else:
        scratch[Key.w_input] = pltpu.VMEM(lead + (width, 3 * width), bf16)
        scratch[Key.keep_sem] = pltpu.SemaphoreType.DMA((4,))
    names = ins + [Key.k_sums, Key.lengths] + list(outs) + list(scratch)
    found = pl.pallas_call(
        functools.partial(backward_kernel, names, fast, sizes, routes, plan),
        out_shape=[jax.ShapeDtypeStruct(*s) for s in outs.values()],
        in_specs=in_specs,
        out_specs=out_specs,
        scratch_shapes=list(scratch.values()),
        compiler_params=pltpu.CompilerParams(
            collective_id=1, has_side_effects=True, vmem_limit_bytes=BACKWARD_VMEM
        ),
        name="backward",
    )(*args)
    return dict(zip(outs, found, strict=True))


def plain_forward(rows, units):
    plan = []
    for r in range(rows):
        plan += [(Key.frame, r), (Key.send, r), (Key.cot, r)]
    plan += [(Key.loaded, Key.w_input), (Key.save, Key.k_vectors)]
    plan += [(Key.project_own, part) for part in range(3)] + [(Key.loaded, Key.w_output)]
    for r in range(rows):
        plan += [(Key.other, r), (Key.project_other, r, 0), (Key.project_other, r, 1)]
        plan += [(Key.attend_pairs, r), (Key.attend_padding, r)]
    plan += [(Key.first_norm, r) for r in range(rows + 1)]
    plan += [(Key.loaded, Key.w_inner), (Key.hidden_units, 0, units // 256), (Key.loaded, Key.w_outer)]
    plan += [(Key.save, Key.k_soft), (Key.saved, Key.k_soft)] + [(Key.second_norm, r) for r in range(rows + 1)]
    saved = (Key.layer_out, Key.k_input, Key.k_output, Key.k_inner, Key.k_outer, Key.k_own, Key.k_other, Key.k_packed, Key.k_pairs)
    saved += (Key.k_context, Key.k_norm, Key.k_inverse, Key.k_active, Key.k_slope, Key.k_grad, Key.k_low)
    return plan + [(Key.save, name) for name in saved]


def plain_backward(rows, units):
    first = (Key.vectors, Key.grad, Key.outer, Key.slope, Key.norm, Key.inner, Key.inverse, Key.output)
    plan = [(Key.load, name) for name in first] + [(Key.loaded, name) for name in first + (Key.low, Key.active)]
    plan += [(Key.lower_norm,), (Key.grad_outer,)]
    plan += [(Key.grad_hidden, 0, units // 384), (Key.keep, Key.outer)]
    plan += [(Key.grad_inner, core, part) for core in range(2) for part in range(units // 1536)] + [(Key.keep, Key.inner)]
    plan += [(Key.load, name) for name in (Key.own, Key.other, Key.context, Key.packed, Key.soft)]
    plan += [(Key.first_back, r) for r in range(rows + 1)]
    plan += [(Key.load, Key.pairs), (Key.load, Key.input)]
    plan += [(Key.loaded, name) for name in (Key.own, Key.other, Key.context, Key.packed, Key.soft, Key.pairs, Key.input)]
    plan += [(Key.grad_output,), (Key.keep, Key.output)]
    plan += [(Key.grad_context, r) for r in range(rows)] + [(Key.drain, Key.inner)]
    for r in range(rows):
        plan += [(Key.attend_back, r), (Key.return_other, r), (Key.send, r)]
    plan += [(Key.token_sums,)] + [(Key.grad_input_weight, part) for part in range(3)]
    plan += [(Key.keep, Key.input)]
    for r in range(rows):
        plan += [(Key.back, r), (Key.grad_hidden_in, r), (Key.put, r)]
    return plan + [(Key.drain, Key.outer), (Key.drain, Key.output), (Key.drain, Key.input)]


GATHER = {
    Key.w_input: (
        (("ZYX", "ZXY"), 0, 640, 0, 48),
        (("XZY", "XZY"), 640, 512, 0, 48),
    ),
    Key.w_output: (
        (("ZXY", "ZXY"), 0, 384, 0, 48),
    ),
    Key.w_inner: (
        (("ZYX", "XZY"), 0, 768, 0, 48),
        (("ZYX", "XZY"), 768, 768, 0, 48),
    ),
    Key.w_outer: (
        (("XZY", "ZYX"), 0, 384, 0, 96),
        (("XZY", "XYZ"), 0, 384, 96, 96),
    ),
}
SCATTER = {
    Key.outer: (
        (("XYZ", "ZXY"), (0, 512), 256),
        (("YXZ", "YZX"), (256, 384), 128),
    ),
    Key.inner: (
        (("YZX", "XYZ"), (0, 1536), 768),
        (("XZY", "YXZ"), (768, 2304), 768),
    ),
    Key.output: (
        (("XZY", "YZX"), (0, 384), 384),
    ),
    Key.input: (
        (("ZYX", "YXZ"), (0, 1536), 768),
        (("YZX", "YXZ"), (768, 1152), 384),
    ),
}
FORWARD_PLAN = (
    (Key.lay, 0), (Key.event, Key.w_input, 0, 0), (Key.event, Key.w_input, 1, 0), (Key.frame, 0), (Key.frame, 1),
    (Key.frame, 2), (Key.frame, 3), (Key.lay, 1), (Key.lay, 2), (Key.lay, 3), (Key.cot, 0), (Key.cot, 1), (Key.total, 0),
    (Key.cot, 2), (Key.event, Key.w_output, 0, 0), (Key.event, Key.w_inner, 0, 0), (Key.cot, 3), (Key.send, 2),
    (Key.event, Key.w_input, 1, 1), (Key.event, Key.w_input, 0, 1), (Key.total, 1), (Key.event, Key.w_inner, 1, 0),
    (Key.event, Key.w_output, 0, 1), (Key.send, 0), (Key.event, Key.w_inner, 0, 1), (Key.event, Key.w_input, 0, 2),
    (Key.event, Key.w_outer, 1, 0), (Key.send, 3), (Key.event, Key.w_outer, 0, 0), (Key.event, Key.w_output, 0, 2),
    (Key.send, 1), (Key.event, Key.w_input, 1, 2), (Key.total, 2), (Key.event, Key.w_inner, 1, 1),
    (Key.event, Key.w_output, 0, 3), (Key.event, Key.w_input, 0, 3), (Key.event, Key.w_output, 0, 4),
    (Key.save, Key.k_output), (Key.event, Key.w_outer, 1, 1), (Key.event, Key.w_input, 0, 4), (Key.event, Key.w_inner, 0, 2),
    (Key.event, Key.w_input, 1, 3), (Key.event, Key.w_input, 1, 4), (Key.save, Key.k_input), (Key.save, Key.k_own),
    (Key.project_own, 0), (Key.project_own, 1), (Key.event, Key.w_outer, 0, 1), (Key.project_own, 2),
    (Key.save, Key.k_packed), (Key.save, Key.k_vectors), (Key.other, 0), (Key.project_other, 0, 0),
    (Key.project_other, 0, 1), (Key.attend_pairs, 0), (Key.event, Key.w_inner, 1, 2), (Key.attend_padding, 0),
    (Key.other, 1), (Key.project_other, 1, 0), (Key.project_other, 1, 1), (Key.attend_pairs, 1),
    (Key.attend_padding, 1), (Key.event, Key.w_outer, 1, 2), (Key.other, 2), (Key.project_other, 2, 0),
    (Key.project_other, 2, 1), (Key.attend_pairs, 2), (Key.attend_padding, 2), (Key.event, Key.w_inner, 0, 3),
    (Key.other, 3), (Key.project_other, 3, 0), (Key.project_other, 3, 1), (Key.save, Key.k_pairs), (Key.save, Key.k_other),
    (Key.attend_pairs, 3), (Key.save, Key.k_soft), (Key.event, Key.w_outer, 0, 2), (Key.event, Key.w_inner, 0, 4),
    (Key.attend_padding, 3), (Key.save, Key.k_context), (Key.first_norm, 0), (Key.first_norm, 1),
    (Key.event, Key.w_inner, 1, 3), (Key.first_norm, 2), (Key.first_norm, 3), (Key.first_norm, 4), (Key.save, Key.k_norm),
    (Key.save, Key.k_inverse), (Key.event, Key.w_inner, 1, 4), (Key.save, Key.k_inner), (Key.hidden_units, 0, 2),
    (Key.hidden_units, 2, 2), (Key.hidden_units, 4, 2), (Key.hidden_units, 6, 2), (Key.event, Key.w_outer, 0, 3),
    (Key.hidden_units, 8, 2), (Key.event, Key.w_outer, 1, 3), (Key.event, Key.w_outer, 0, 4), (Key.hidden_units, 10, 2),
    (Key.save, Key.k_active), (Key.save, Key.k_slope), (Key.event, Key.w_outer, 1, 4), (Key.save, Key.k_outer),
    (Key.saved, Key.k_soft), (Key.second_norm, 0), (Key.second_norm, 1), (Key.second_norm, 2), (Key.second_norm, 3),
    (Key.second_norm, 4), (Key.save, Key.layer_out), (Key.save, Key.k_grad), (Key.save, Key.k_low),
)
BACKWARD_PLAN = (
    (Key.loaded, Key.low), (Key.loaded, Key.active), (Key.load, Key.outer), (Key.load, Key.slope), (Key.load, Key.vectors),
    (Key.load, Key.norm), (Key.load, Key.inner), (Key.load, Key.grad), (Key.load, Key.inverse), (Key.load, Key.output),
    (Key.grad_outer,), (Key.event, Key.outer, 0, 0), (Key.loaded, Key.outer), (Key.loaded, Key.slope),
    (Key.loaded, Key.vectors), (Key.load, Key.packed), (Key.load, Key.soft), (Key.grad_hidden, 0, 2),
    (Key.grad_hidden, 2, 2), (Key.grad_hidden, 4, 2), (Key.event, Key.outer, 0, 1), (Key.grad_hidden, 6, 2),
    (Key.load, Key.own), (Key.load, Key.other), (Key.load, Key.context), (Key.loaded, Key.norm), (Key.lower_norm,),
    (Key.grad_inner, 0, 0), (Key.event, Key.inner, 0, 0), (Key.grad_inner, 1, 0), (Key.grad_inner, 0, 1),
    (Key.event, Key.inner, 1, 0), (Key.event, Key.inner, 0, 1), (Key.grad_inner, 1, 1), (Key.loaded, Key.inner),
    (Key.loaded, Key.inverse), (Key.loaded, Key.grad), (Key.first_back, 0), (Key.event, Key.inner, 1, 1),
    (Key.first_back, 1), (Key.first_back, 2), (Key.event, Key.outer, 1, 0), (Key.first_back, 3), (Key.first_back, 4),
    (Key.load, Key.pairs), (Key.load, Key.input), (Key.loaded, Key.context), (Key.loaded, Key.output), (Key.grad_output,),
    (Key.event, Key.output, 0, 0), (Key.event, Key.inner, 0, 2), (Key.event, Key.outer, 1, 1), (Key.event, Key.outer, 0, 2),
    (Key.event, Key.output, 0, 1), (Key.grad_context, 0), (Key.grad_context, 1), (Key.grad_context, 2),
    (Key.grad_context, 3), (Key.loaded, Key.packed), (Key.loaded, Key.soft), (Key.loaded, Key.pairs), (Key.loaded, Key.input),
    (Key.attend_back, 0), (Key.event, Key.inner, 1, 2), (Key.return_other, 0), (Key.send, 0), (Key.attend_back, 1),
    (Key.event, Key.inner, 0, 3), (Key.return_other, 1), (Key.send, 1), (Key.attend_back, 2), (Key.return_other, 2),
    (Key.send, 2), (Key.attend_back, 3), (Key.event, Key.inner, 1, 3), (Key.event, Key.outer, 1, 2), (Key.return_other, 3),
    (Key.send, 3), (Key.token_sums,), (Key.total, -1), (Key.loaded, Key.own), (Key.loaded, Key.other),
    (Key.event, Key.outer, 0, 3), (Key.event, Key.inner, 0, 4), (Key.event, Key.output, 0, 2), (Key.total, 0),
    (Key.event, Key.inner, 1, 4), (Key.event, Key.inner, 0, 5), (Key.drain, Key.inner), (Key.grad_input_weight, 0),
    (Key.event, Key.inner, 1, 5), (Key.grad_input_weight, 2), (Key.event, Key.input, 0, 0), (Key.grad_input_weight, 1),
    (Key.event, Key.input, 1, 0), (Key.event, Key.input, 0, 1), (Key.event, Key.outer, 0, 4), (Key.event, Key.input, 1, 1),
    (Key.back, 0), (Key.grad_hidden_in, 0), (Key.put, 0), (Key.event, Key.outer, 0, 5), (Key.back, 1),
    (Key.grad_hidden_in, 1), (Key.put, 1), (Key.event, Key.output, 0, 3), (Key.event, Key.outer, 1, 3), (Key.back, 2),
    (Key.grad_hidden_in, 2), (Key.put, 2), (Key.back, 3), (Key.grad_hidden_in, 3), (Key.put, 3),
    (Key.event, Key.input, 1, 2), (Key.event, Key.input, 0, 2), (Key.event, Key.output, 0, 4), (Key.total, 1),
    (Key.event, Key.outer, 1, 4), (Key.event, Key.output, 0, 5), (Key.event, Key.outer, 1, 5), (Key.event, Key.input, 1, 3),
    (Key.event, Key.input, 0, 3), (Key.event, Key.input, 1, 4), (Key.total, 2), (Key.event, Key.input, 1, 5),
    (Key.event, Key.input, 0, 4), (Key.event, Key.input, 0, 5), (Key.drain, Key.outer), (Key.drain, Key.output),
    (Key.drain, Key.input),
)


def gather_routes(masters):
    return {
        name: [(route, (row, count), (col, span)) for route, col, span, row, count in found]
        for name, found in GATHER.items()
    }


def scatter_routes(width, units):
    return SCATTER


def forward_steps(rows, nz, units):
    return FORWARD_PLAN


def backward_steps(rows, nz):
    return BACKWARD_PLAN


def spread(masters, vectors):
    gathered = [lax.all_gather(v.astype(bf16), ("pair", "rows"), axis=0, tiled=True) for v in masters]
    rows = [lax.all_gather(v, ("pair", "rows"), axis=0, tiled=True) for v in vectors]
    width = rows[0].shape[0]
    table = jnp.concatenate(rows).reshape(-1, width)
    return gathered, [jnp.pad(table, ((0, VECTORS - table.shape[0]), (0, 0)))]


def gather_sums(found, units):
    def summed(v):
        return lax.psum_scatter(v.astype(f32), ("pair", "rows"), scatter_dimension=0, tiled=True)

    weights = {name: summed(found[name].reshape(found[name].shape[3:])) for name in found if name != Key.g_small}
    table = found[Key.g_small]
    width = table.shape[1]
    small = [summed(table[k]) for k in range(8)] + [summed(table[8 : 8 + units // width].reshape(units))]
    return weights, small


def settle(arrays):
    parts = []
    for k, v in enumerate(arrays):
        count = 4 if v.shape[0] % 64 == 0 else 1
        size = v.shape[0] // count
        parts += [(k, pl.ds(i * size, size)) for i in range(count)]

    def kernel(*refs):
        count = len(arrays)
        ins, outs, held, sems = refs[:count], refs[count : 2 * count], refs[2 * count : 3 * count], refs[-1]
        loads = [pltpu.make_async_copy(ins[k].at[at], held[k].at[at], sems.at[0, n]) for n, (k, at) in enumerate(parts)]
        stores = [pltpu.make_async_copy(held[k].at[at], outs[k].at[at], sems.at[1, n]) for n, (k, at) in enumerate(parts)]
        for load in loads:
            load.start()
        for load, store in zip(loads, stores, strict=True):
            load.wait()
            store.start()
        for store in stores:
            store.wait()

    return pl.pallas_call(
        kernel,
        out_shape=[jax.ShapeDtypeStruct(v.shape, v.dtype) for v in arrays],
        in_specs=[pl.BlockSpec(memory_space=pl.ANY)] * len(arrays),
        out_specs=[pl.BlockSpec(memory_space=pl.ANY)] * len(arrays),
        scratch_shapes=[pltpu.VMEM(v.shape, v.dtype) for v in arrays] + [pltpu.SemaphoreType.DMA((2, len(parts)))],
        compiler_params=pltpu.CompilerParams(vmem_limit_bytes=BACKWARD_VMEM),
        name="k_settle",
    )(*arrays)


def shards(rows_axis, *args):
    (
        hidden_in, input_proj, query_bias, value_bias, output_proj, output_bias, first_gain, first_shift,
        inner_proj, inner_bias, outer_proj, outer_bias, second_gain, second_shift, cotangent, pair_lengths,
    ) = args
    row_count, _, slots, width = hidden_in.shape
    units = inner_proj.shape[1]
    share = input_proj.shape[0]
    fast = rows_axis % 4 == 0 and share % 8 == 0
    masters = (input_proj, output_proj, inner_proj, outer_proj)
    vectors = (
        query_bias, value_bias, output_bias, first_gain, first_shift, outer_bias, second_gain, second_shift,
        inner_bias,
    )
    if fast:
        routes_f, plan_f = gather_routes(masters), forward_steps(row_count, rows_axis // 4, units)
        routes_b, plan_b = scatter_routes(width, units), backward_steps(row_count, rows_axis // 4)
        small = [v.reshape(1, -1) for v in vectors]
    else:
        routes_f, routes_b = {}, {}
        plan_f, plan_b = plain_forward(row_count, units), plain_backward(row_count, units)
        masters, small = spread(masters, vectors)
    sizes = (row_count, slots, width, pair_lengths.shape[2])
    kept = forward_call(
        rows_axis, fast, hidden_in[:, 0], cotangent[:, 0], masters, small, pair_lengths, routes_f, plan_f
    )
    found = backward_call(rows_axis, fast, kept, pair_lengths, routes_b, plan_b, sizes, units)
    layer_out, grad_input = kept[Key.layer_out], found.pop(Key.grad_input)
    if fast:
        weights = (Key.input, Key.output, Key.inner, Key.outer)
        results = settle([layer_out, grad_input] + [found["g", name] for name in weights])
        layer_out, grad_input = results[:2]
        found.update(zip([("g", name) for name in weights], results[2:], strict=True))
        table = found[Key.g_small]
        sums = [table[k, :share] for k in range(8)] + [table[8, : inner_bias.shape[0]]]
    else:
        found, sums = gather_sums(found, units)
    return (
        layer_out.reshape(hidden_in.shape), grad_input.reshape(hidden_in.shape), found["g", Key.input], sums[Q_BIAS], sums[V_BIAS], found["g", Key.output], sums[O_BIAS],
        sums[GAIN_1], sums[SHIFT_1], found["g", Key.inner], sums[FF_ROW], found["g", Key.outer], sums[OUT_BIAS],
        sums[GAIN_2], sums[SHIFT_2],
    )


def solution(mesh):
    tokens = P("rows", "pair", None, None)
    matrix = P(("pair", "rows"), None)
    vector = P(("pair", "rows"))
    weights = (
        matrix, vector, vector, matrix, vector, vector, vector, matrix, vector, matrix, vector, vector, vector
    )
    return jax.shard_map(
        functools.partial(shards, mesh.shape["rows"]),
        mesh=mesh,
        in_specs=(tokens, *weights, tokens, P("rows", None, None)),
        out_specs=(tokens, tokens, *weights),
        check_vma=False,
    )
```

```python
import enum
import functools
import math

import jax
import jax.numpy as jnp
from jax import lax
from jax.experimental import pallas as pl
from jax.experimental.pallas import tpu as pltpu
from jax.sharding import PartitionSpec as P

HEADS = 12
EPSILON = 1e-12
MESH = pl.DeviceIdType.MESH
bf16 = jnp.bfloat16
f32 = jnp.float32
ALL = slice(None)
MASKED = -1e30
VECTORS = 16
Q_BIAS, V_BIAS, O_BIAS, GAIN_1, SHIFT_1, OUT_BIAS, GAIN_2, SHIFT_2, FF_ROW = range(9)


def contract(left, right, left_dim, right_dim):
    return lax.dot_general(
        left, right, (((left_dim,), (right_dim,)), ((), ())), preferred_element_type=f32
    )


def iota(shape, dim):
    return lax.broadcasted_iota(jnp.int32, shape, dim)


def rounded(v):
    return v.astype(bf16).astype(f32)


class Key(enum.Enum):
    active = 0
    attend_back = 1
    attend_padding = 2
    attend_pairs = 3
    back = 4
    col_sums = 5
    context = 6
    cot = 7
    cotangent = 8
    d_inner = 9
    d_outer = 10
    d_output = 11
    drain = 12
    event = 13
    ff_bias = 14
    ff_sums = 15
    final = 16
    first_back = 17
    first_norm = 18
    frame = 19
    framed = 20
    from_sibling = 21
    g_small = 22
    gain_sum = 23
    grad = 24
    grad_context = 25
    grad_hidden = 26
    grad_hidden_in = 27
    grad_inner = 28
    grad_input = 29
    grad_input_weight = 30
    grad_low = 31
    grad_outer = 32
    grad_output = 33
    hidden = 34
    hidden_in = 35
    hidden_units = 36
    inner = 37
    input = 38
    inverse = 39
    k_active = 40
    k_context = 41
    k_grad = 42
    k_inner = 43
    k_input = 44
    k_inverse = 45
    k_low = 46
    k_norm = 47
    k_other = 48
    k_outer = 49
    k_output = 50
    k_own = 51
    k_packed = 52
    k_pairs = 53
    k_slope = 54
    k_soft = 55
    k_sums = 56
    k_vectors = 57
    keep = 58
    keep_sem = 59
    landed = 60
    lay = 61
    layer_out = 62
    lengths = 63
    load = 64
    loaded = 65
    local_sem = 66
    low = 67
    low_sum = 68
    lower_norm = 69
    m_inner = 70
    m_input = 71
    m_outer = 72
    m_output = 73
    norm = 74
    other = 75
    out_sem = 76
    outer = 77
    output = 78
    own = 79
    packed = 80
    pairs = 81
    pairs_other = 82
    piece_recv = 83
    piece_send = 84
    project_other = 85
    project_own = 86
    put = 87
    return_other = 88
    row_recv = 89
    row_send = 90
    save = 91
    saved = 92
    second_norm = 93
    send = 94
    shift_sum = 95
    slope = 96
    soft = 97
    sums = 98
    swap_recv = 99
    swap_send = 100
    swapped = 101
    table = 102
    table_in = 103
    table_recv = 104
    table_send = 105
    token_sums = 106
    total = 107
    vector = 108
    vectors = 109
    w_inner = 110
    w_input = 111
    w_outer = 112
    w_output = 113


def attributes(refs):
    return {key.name: ref for key, ref in refs.items() if isinstance(key, Key)}


class Place:
    def __init__(self, rows):
        self.nz = rows // 4
        r = lax.axis_index("rows")
        self.x = lax.axis_index("pair")
        self.z = r // 4
        self.y = (r // 2) % 2
        self.c = r % 2
        self.index = self.x * rows + r
        self.own = {"X": self.x, "Z": self.z, "Y": self.y}

    def device(self, **other):
        at = {"X": self.x, "Z": self.z, "Y": self.y, "C": self.c, **other}
        return {"pair": at["X"], "rows": (at["Z"] * 2 + at["Y"]) * 2 + at["C"]}

    def peers(self, dim):
        if dim == "Z":
            return [(self.z + k) % self.nz for k in range(1, self.nz)]
        return [1 - self.own[dim]]

    def sources(self, dim):
        if dim == "Z":
            return [(self.z + self.nz - k) % self.nz for k in range(1, self.nz)]
        return [1 - self.own[dim]]

    def first_slot(self, dim):
        return {"X": 0, "Y": 1, "Z": 2}[dim]

    def slots(self):
        return self.nz + 1


def slab(buf, place, gathered, at, rows, cols):
    own = {**place.own, **at}
    lead = tuple(ALL if d in gathered else own[d] for d in "XZY")
    return buf.at[lead + (rows, cols)]


class Gather:
    def __init__(self, buf, place, send, recv, routes, rows, col, width):
        self.buf, self.place, self.send, self.recv, self.routes = buf, place, send, recv, routes
        self.rows, self.col, self.width = rows, col, width
        self.half = buf.shape[-1] // 2

    def cols(self, core):
        return pl.ds(pl.multiple_of(core * self.half + self.col, 128), self.width)

    def per_core(self, act):
        if self.routes[0] == self.routes[1]:
            act(self.routes[0])
            return
        for core in range(2):
            pl.when(self.place.c == core)(functools.partial(act, self.routes[core]))

    def copy(self, view, slot, device):
        return pltpu.make_async_remote_copy(
            src_ref=view,
            dst_ref=view,
            send_sem=self.send.at[slot],
            recv_sem=self.recv.at[slot],
            device_id=device,
            device_id_type=MESH,
        )

    def sends(self, route, stage):
        dim, gathered = route[stage], route[:stage]
        view = slab(self.buf, self.place, gathered, {}, self.rows, self.cols(self.place.c))
        first = self.place.first_slot(dim)
        return [
            self.copy(view, first + k, self.place.device(**{dim: peer}))
            for k, peer in enumerate(self.place.peers(dim))
        ]

    def arrivals(self, route, stage, core):
        dim, gathered = route[stage], route[:stage]
        return [
            slab(self.buf, self.place, gathered, {dim: peer}, self.rows, self.cols(core))
            for peer in self.place.sources(dim)
        ]

    def hand_ons(self, route, stage, core):
        device = self.place.device(C=1 - self.place.c)
        base = self.place.slots()
        if stage == 0:
            view = slab(self.buf, self.place, route[:1], {}, self.rows, self.cols(core))
            return [self.copy(view, base, device)]
        first = base + 1 + (stage - 1) * (self.place.nz - 1)
        return [
            self.copy(view, first + k, device)
            for k, view in enumerate(self.arrivals(route, stage, core))
        ]

    def start(self, stage):
        def act(route):
            for copy in self.sends(route, stage):
                copy.start()

        self.per_core(act)

    def arrived(self, stage):
        def act(route):
            dim = route[stage]
            first = self.place.first_slot(dim)
            device = self.place.device()
            for k, view in enumerate(self.arrivals(route, stage, self.place.c)):
                self.copy(view, first + k, device).wait_recv()
            if stage < 2:
                for copy in self.sends(route, stage + 1):
                    copy.start()
            for copy in self.hand_ons(route, stage, self.place.c):
                copy.start()

        self.per_core(act)

    def event(self, number):
        if number == 0:
            self.start(0)
        elif number < 4:
            self.arrived(number - 1)
        else:
            self.complete()

    def complete(self):
        def other(route):
            for stage in range(3):
                for copy in self.hand_ons(route, stage, 1 - self.place.c):
                    copy.wait_recv()

        if self.routes[0] == self.routes[1]:
            other(self.routes[0])
        else:
            for core in range(2):
                pl.when(self.place.c == 1 - core)(functools.partial(other, self.routes[core]))

    def drain(self):
        def act(route):
            for stage in range(3):
                for copy in self.sends(route, stage) + self.hand_ons(route, stage, self.place.c):
                    copy.wait_send()

        self.per_core(act)


def greet(place, devices):
    barrier = pltpu.get_barrier_semaphore()
    for device in devices:
        pl.semaphore_signal(barrier, inc=1, device_id=device, device_id_type=MESH)
    pl.semaphore_wait(barrier, len(devices))


class Totals:
    def __init__(self, place, table, landed, send, recv):
        self.place, self.table, self.landed, self.send, self.recv = place, table, landed, send, recv
        x, y = 1 - place.x, 1 - place.y
        self.steps = [
            [place.device(C=1 - place.c)],
            [place.device(X=x), place.device(Y=y), place.device(X=x, Y=y)],
            [place.device(Z=peer) for peer in place.peers("Z")],
        ]

    def copies(self, step):
        first = sum(len(found) for found in self.steps[:step])
        return [
            pltpu.make_async_remote_copy(
                src_ref=self.table.at[step],
                dst_ref=self.landed.at[first + k],
                send_sem=self.send.at[first + k],
                recv_sem=self.recv.at[first + k],
                device_id=device,
                device_id_type=MESH,
            )
            for k, device in enumerate(self.steps[step])
        ]

    def start(self, step):
        for copy in self.copies(step):
            copy.start()

    def advance(self, step):
        first = sum(len(found) for found in self.steps[:step])
        total = self.table[step]
        for k, copy in enumerate(self.copies(step)):
            copy.wait_recv()
            total = total + self.landed[first + k]
        self.table[step + 1] = total
        if step + 1 < len(self.steps):
            self.start(step + 1)

    def drain(self):
        for step in range(len(self.steps)):
            for copy in self.copies(step):
                copy.wait_send()


def neighbours(place):
    x, y = 1 - place.x, 1 - place.y
    found = [place.device(C=1 - place.c), place.device(X=x), place.device(Y=y), place.device(X=x, Y=y)]
    return found + [place.device(Z=peer) for peer in place.peers("Z")]


def source_slots(slots, sizes, most):
    frame, offset = slots // most, slots % most
    total = sum(sizes[1:], sizes[0])
    found, start = slots, jnp.int32(0)
    for p, size in enumerate(sizes):
        mine = jnp.where(offset < size, start + offset, total + slots - (start + size))
        found = jnp.where(frame == p, mine, found)
        start = start + size
    return found


def holds_token(slots, sizes, most):
    frame, offset = slots // most, slots % most
    held = jnp.zeros(slots.shape, f32)
    for p, size in enumerate(sizes):
        held = jnp.where((frame == p) & (offset < size), 1.0, held)
    return held


def into_frames(sizes, slots, most):
    source = source_slots(iota((slots, 1), 0), sizes, most)
    return (iota((slots, slots), 1) == source).astype(f32).astype(bf16)


def out_of_frames(sizes, slots, most):
    source = source_slots(iota((1, slots), 1), sizes, most)
    return (iota((slots, slots), 0) == source).astype(f32).astype(bf16)


def folded(v):
    return jnp.sum(v.reshape(v.shape[0] // 8, 8, v.shape[1]), axis=0)


def spread_heads(tokens, span):
    shape = (4 * tokens, span)
    return iota(shape, 0) // tokens == iota(shape, 1) // (span // 4)


def block_rows(i, size):
    return pl.ds(pl.multiple_of(i * size, size), size)


class Forward:
    def __init__(self, refs, place, sizes):
        self.__dict__.update(attributes(refs))
        self.place = place
        self.rows, self.slots, self.width, self.pairs = sizes
        self.most = self.slots // self.pairs
        self.half = place.x
        self.bias_rows = self.ff_bias.shape[1] // self.width
        self.scale = (self.width // HEADS) ** (-0.5)

    def sizes_of(self, row, half):
        return [self.lengths[row, half, p] for p in range(self.pairs)]

    def row(self, r):
        return pl.ds(r * self.slots, self.slots)

    def vector(self, at, count=1):
        found = rounded(self.vectors[at : at + count, :])
        return found if count == 1 else found.reshape(1, count * self.width)

    def frame_hidden(self, r):
        frames = into_frames(self.sizes_of(r, self.half), self.slots, self.most)
        self.own[self.row(r), :] = contract(frames, self.hidden[self.row(r), :], 1, 0).astype(bf16)

    def frame_cotangent(self, r):
        sizes = self.sizes_of(r, self.half)
        frames = into_frames(sizes, self.slots, self.most)
        held = holds_token(iota((self.slots, 1), 0), sizes, self.most)
        moved = contract(frames, self.cot[self.row(r), :], 1, 0) * held
        self.cot[self.row(r), :] = moved.astype(bf16)

    def project_own(self, part):
        cols = slice(part * self.width, (part + 1) * self.width)
        weight = self.w_input[:, :, :, :, cols].reshape(self.width, self.width)
        acc = contract(self.own[...], weight, 1, 0)
        if part == 0:
            acc = acc + self.vector(Q_BIAS)
        if part == 2:
            acc = acc + self.vector(V_BIAS)
        self.packed[:, cols] = acc.astype(bf16)

    def project_other(self, r, part):
        cols = slice(part * self.width, (part + 1) * self.width)
        from_cols = slice((part + 1) * self.width, (part + 2) * self.width)
        weight = self.w_input[:, :, :, :, from_cols].reshape(self.width, self.width)
        acc = contract(self.other[self.row(r), :], weight, 1, 0)
        if part == 1:
            acc = acc + self.vector(V_BIAS)
        self.pairs_other[self.row(r), cols] = acc.astype(bf16)

    def attend_pairs(self, r, together=4):
        most, span, wide = self.most, 4 * (self.width // HEADS), 2 * self.most
        spread = spread_heads(wide, span)
        key, query = iota((2 * wide, 4 * wide), 0), iota((2 * wide, 4 * wide), 1)
        key_frame, same = key % wide // most, key % wide // most == query % wide // most
        slot = key % most

        def two_pairs(pair):
            rows = pl.ds(pl.multiple_of(r * self.slots + pair * wide, wide), wide)
            counts = [self.lengths[r, half, 2 * pair + k] for half in (self.half, 1 - self.half) for k in range(2)]
            mine = jnp.where(key_frame == 0, counts[0], counts[1])
            theirs = jnp.where(key_frame == 0, counts[2], counts[3])
            allowed = same & (slot < jnp.where(key < wide, mine, theirs))
            for at in range(0, self.width, span):
                queries = self.packed[rows, at : at + span]
                keys = jnp.concatenate(
                    [
                        self.packed[rows, self.width + at : self.width + at + span],
                        self.pairs_other[rows, at : at + span],
                    ],
                    axis=0,
                )
                values = jnp.concatenate(
                    [
                        self.packed[rows, 2 * self.width + at : 2 * self.width + at + span],
                        self.pairs_other[rows, self.width + at : self.width + at + span],
                    ],
                    axis=0,
                )
                tiled = jnp.where(spread, jnp.concatenate([queries] * 4, axis=0), 0).astype(bf16)
                scores = jnp.where(allowed, contract(keys, tiled, 1, 1) * self.scale, MASKED)
                raw = jnp.exp(scores - jnp.max(scores, axis=0, keepdims=True))
                soft = raw * (1.0 / jnp.sum(raw, axis=0, keepdims=True))
                kept = [soft[k * most : (k + 1) * most] + soft[(k + 1) * most : (k + 2) * most] for k in (0, 2)]
                self.soft[rows, at : at + span] = jnp.concatenate(kept, axis=0).astype(bf16)
                mixed = contract(soft.astype(bf16), values, 0, 0)
                mixed = jnp.where(spread, mixed, 0.0)
                context = sum(mixed[h * wide : (h + 1) * wide, :] for h in range(4))
                self.context[rows, at : at + span] = context.astype(bf16)

        @pl.loop(0, self.pairs // (2 * together))
        def _(several):
            for k in range(together):
                two_pairs(several * together + k)

    def attend_padding(self, r, together=6):
        sizes = self.sizes_of(r, self.half)
        head = self.width // HEADS
        held_key = holds_token(iota((1, self.slots), 1), sizes, self.most)
        held_query = holds_token(iota((self.slots, 1), 0), sizes, self.most)
        pad_key = jnp.broadcast_to(held_key, (2 * self.slots, self.slots)) < 0.5
        pad_query = jnp.broadcast_to(held_query, (self.slots, 2 * head)) < 0.5
        left = iota((self.slots, 2 * head), 1) < head
        rows = self.row(r)

        def two_heads(pair):
            at = pl.multiple_of(pair * 2 * head, 2 * head)
            queries = self.packed[rows, pl.ds(at, 2 * head)] * self.scale
            keys = self.packed[rows, pl.ds(pl.multiple_of(self.width + at, 2 * head), 2 * head)]
            values = self.packed[rows, pl.ds(pl.multiple_of(2 * self.width + at, 2 * head), 2 * head)]
            both = jnp.concatenate([jnp.where(left, queries, 0), jnp.where(left, 0, queries)], axis=0)
            scores = jnp.where(pad_key, contract(both.astype(bf16), keys, 1, 1), MASKED)
            raw = jnp.exp(scores - jnp.max(scores, axis=1, keepdims=True))
            total = jnp.sum(raw, axis=1, keepdims=True)
            found = contract(raw.astype(bf16), values, 1, 0) * (1.0 / total)
            padded = jnp.where(left, found[: self.slots], found[self.slots :]).astype(bf16)
            cols = pl.ds(at, 2 * head)
            self.context[rows, cols] = jnp.where(pad_query, padded, self.context[rows, cols])

        @pl.loop(0, HEADS // 2 // together)
        def _(several):
            for k in range(together):
                two_heads(several * together + k)

    def first_norm(self, r):
        if r < self.rows:
            weight = self.w_output[...].reshape(self.width, self.width)
            self.sums[r % 2] = contract(self.context[self.row(r), :], weight, 1, 0)
        if r == 0:
            return
        bias, gain, shift = self.vector(O_BIAS), self.vector(GAIN_1), self.vector(SHIFT_1)
        size = 32
        for i in range(0, self.slots, size):
            there = pl.ds((r - 1) * self.slots + i, size)
            total = self.own[there, :].astype(f32) + self.sums[(r - 1) % 2, i : i + size, :] + bias
            centered = total - jnp.mean(total, axis=1, keepdims=True)
            inverse = lax.rsqrt(jnp.mean(centered * centered, axis=1, keepdims=True) + EPSILON)
            norm = centered * inverse
            self.norm[there, :] = norm
            self.inverse[there, :] = jnp.broadcast_to(inverse, (size, 128))
            self.low[there, :] = (norm * gain + shift).astype(bf16)

    def hidden_units(self, first, count, size=256):
        @pl.loop(first, first + count, unroll=2)
        def _(n):
            cols = pl.ds(pl.multiple_of(n * size, size), size)
            weight = self.w_inner[:, :, :, :, cols].reshape(self.width, size)
            bias = rounded(self.ff_bias[:, cols])
            for r in range(self.rows):
                inner = contract(self.low[self.row(r), :], weight, 1, 0) + bias
                share = 0.5 * (1.0 + lax.erf(inner * (0.5**0.5)))
                slope = share + inner * (jnp.exp(-0.5 * inner * inner) * ((2.0 * math.pi) ** -0.5))
                self.active[self.row(r), cols] = (inner * share).astype(bf16)
                self.slope[self.row(r), cols] = slope.astype(bf16)

    def second_norm(self, r):
        if r < self.rows:
            weight = self.w_outer[...].reshape(self.w_inner.shape[-1], self.width)
            self.sums[r % 2] = contract(self.active[self.row(r), :], weight, 1, 0)
        if r == 0:
            return
        gain_1, shift_1 = self.vector(GAIN_1), self.vector(SHIFT_1)
        bias, gain, shift = self.vector(OUT_BIAS), self.vector(GAIN_2), self.vector(SHIFT_2)
        size = 32
        sums = [self.gain_sum[...], self.shift_sum[...], self.low_sum[...]]
        for i in range(0, self.slots, size):
            there = pl.ds((r - 1) * self.slots + i, size)
            total = (self.norm[there, :] * gain_1 + shift_1) + self.sums[(r - 1) % 2, i : i + size, :] + bias
            centered = total - jnp.mean(total, axis=1, keepdims=True)
            inverse = lax.rsqrt(jnp.mean(centered * centered, axis=1, keepdims=True) + EPSILON)
            norm = centered * inverse
            self.framed[i : i + size, :] = (norm * gain + shift).astype(bf16)
            upstream = self.cot[there, :].astype(f32)
            incoming = upstream * gain
            plain = jnp.mean(incoming, axis=1, keepdims=True)
            along = jnp.mean(incoming * norm, axis=1, keepdims=True)
            grad = inverse * (incoming - plain - norm * along)
            low = grad.astype(bf16)
            self.grad[there, :] = grad
            self.soft[there, :] = low
            parts = (upstream * norm, upstream, low.astype(f32))
            sums = [total + folded(part) for total, part in zip(sums, parts, strict=True)]
        self.gain_sum[...], self.shift_sum[...], self.low_sum[...] = sums
        back = out_of_frames(self.sizes_of(r - 1, self.half), self.slots, self.most)
        self.hidden[self.row(r - 1), :] = contract(back, self.framed[...], 1, 0).astype(bf16)


FORWARD_VMEM = 127 * 2**19
ORDER = None


def forward_kernel(names, fast, sizes, routes, plan, *refs):
    refs = dict(zip(names, refs, strict=True))
    rows, slots, width, pairs = sizes
    place = Place(lax.axis_size("rows"))
    run = Forward(refs, place, sizes)
    sibling = place.device(C=1 - place.c)
    partner = place.device(X=1 - place.x)

    def local(src, dst, slot):
        return pltpu.make_async_copy(src, dst, run.local_sem.at[slot])

    load_hidden = local(run.hidden_in, run.hidden, 0)
    load_cot = local(run.cotangent, run.cot, 1)
    load_hidden.start()
    load_cot.start()

    if fast:
        greet(place, neighbours(place))
    else:
        greet(place, [partner])

    def hidden_copy(r):
        view = pl.ds(r * slots, slots)
        return pltpu.make_async_remote_copy(
            src_ref=run.own.at[view],
            dst_ref=run.other.at[view],
            send_sem=run.row_send.at[r],
            recv_sem=run.row_recv.at[r],
            device_id=partner,
            device_id_type=MESH,
        )

    weights = [Key.w_input, Key.w_output, Key.w_inner, Key.w_outer]
    masters = [Key.m_input, Key.m_output, Key.m_inner, Key.m_outer]
    gathers = {}
    drains = []
    if fast:
        totals = Totals(place, run.table, run.table_in, run.table_send, run.table_recv)
        for k, (weight, master) in enumerate(zip(weights, masters, strict=True)):
            buf = refs[weight]
            half = buf.shape[-1] // 2
            for j, (route, (row, count), (col, span)) in enumerate(routes.get(weight, ())):
                piece = Gather(
                    buf, place, run.piece_send.at[len(gathers)], run.piece_recv.at[len(gathers)],
                    route, pl.ds(row, count), col, span,
                )
                gathers[weight, j] = piece

        def swap(k):
            master = refs[masters[k]]
            half = master.shape[-1] // 2
            theirs = pl.ds(pl.multiple_of((1 - place.c) * half, 128), half)
            return pltpu.make_async_remote_copy(
                src_ref=master.at[:, theirs],
                dst_ref=refs[Key.from_sibling, k],
                send_sem=run.swap_send.at[k],
                recv_sem=run.swap_recv.at[k],
                device_id=sibling,
                device_id_type=MESH,
            )

        def lay(k):
            swap(k).wait_recv()
            master, buf = refs[masters[k]], refs[weights[k]]
            half = master.shape[-1] // 2
            cols = pl.ds(pl.multiple_of(place.c * half, 128), half)
            mine, theirs = master[:, cols], refs[Key.from_sibling, k][...]
            first = place.c == 0
            both = jnp.concatenate([jnp.where(first, mine, theirs), jnp.where(first, theirs, mine)], axis=0)
            buf[place.x, place.z, place.y, :, cols] = both.astype(bf16)

        for k in range(4):
            swap(k).start()
        run.table[0] = jnp.zeros((VECTORS, width), f32)
        for k in range(9):
            share = refs[Key.vector, k]
            run.table[0, k : k + 1, 0 : share.shape[1]] = share[...]
        piece = refs[Key.vector, 0].shape[1]
        wide = refs[Key.vector, 8].shape[1]
        per_row = width // wide
        upper = pltpu.roll(run.table[0, 0:8, :], place.index * piece, axis=1)
        lower = pltpu.roll(run.table[0, 8:16, :], (place.index % per_row) * wide, axis=1)
        lower = jnp.broadcast_to(lower[:1, :], (8, width))
        lower = jnp.where(iota((8, width), 0) == place.index // per_row, lower, 0.0)
        run.table[0, 0:8, :] = upper
        run.table[0, 8:16, :] = lower
        totals.start(0)

    def spread_vectors(table):
        run.vectors[...] = table
        for k in range(run.bias_rows):
            run.ff_bias[:, k * width : (k + 1) * width] = table[FF_ROW + k : FF_ROW + k + 1, :]

    if not fast:
        for k, weight in enumerate(weights):
            local(refs[masters[k]], refs[weight], 2 + k).start()
        spread_vectors(refs[Key.vector, 0][...])

    saved = [
        (Key.k_input, Key.w_input), (Key.k_output, Key.w_output), (Key.k_inner, Key.w_inner), (Key.k_outer, Key.w_outer),
        (Key.k_own, Key.own), (Key.k_other, Key.other), (Key.k_packed, Key.packed), (Key.k_pairs, Key.pairs_other),
        (Key.k_soft, Key.soft), (Key.k_context, Key.context), (Key.k_norm, Key.norm), (Key.k_inverse, Key.inverse),
        (Key.k_active, Key.active), (Key.k_slope, Key.slope), (Key.k_grad, Key.grad), (Key.k_vectors, Key.vectors), (Key.k_low, Key.soft),
        (Key.layer_out, Key.hidden),
    ]
    saves = {name: local(refs[src], refs[name], 6 + k) for k, (name, src) in enumerate(saved) if name in refs}
    started = []
    sent = []

    def save(name):
        if name in saves:
            saves[name].start()
            started.append(name)

    def step(what, *detail):
        if what == Key.event:
            if fast:
                gathers[detail[0], detail[1]].event(detail[2])
        elif what == Key.lay:
            if fast:
                lay(detail[0])
        elif what == Key.total:
            if fast:
                totals.advance(detail[0])
                if detail[0] + 1 == len(totals.steps):
                    spread_vectors(run.table[detail[0] + 1])
        elif what == Key.loaded:
            if not fast:
                k = weights.index(detail[0])
                local(refs[masters[k]], refs[detail[0]], 2 + k).wait()
        elif what == Key.frame:
            if detail[0] == 0:
                load_hidden.wait()
            run.frame_hidden(detail[0])
        elif what == Key.send:
            hidden_copy(detail[0]).start()
            sent.append(detail[0])
        elif what == Key.other:
            hidden_copy(detail[0]).wait_recv()
        elif what == Key.cot:
            if detail[0] == 0:
                load_cot.wait()
            run.frame_cotangent(detail[0])
        elif what == Key.save:
            save(detail[0])
        elif what == Key.saved:
            saves[detail[0]].wait()
            started.remove(detail[0])
        else:
            getattr(run, what.name)(*detail)

    run.gain_sum[...] = jnp.zeros_like(run.gain_sum)
    run.shift_sum[...] = jnp.zeros_like(run.shift_sum)
    run.low_sum[...] = jnp.zeros_like(run.low_sum)
    for entry in plan:
        step(*entry)
    run.k_sums[0:8, :] = run.gain_sum[...]
    run.k_sums[8:16, :] = run.shift_sum[...]
    run.k_sums[16:24, :] = run.low_sum[...]
    for r in sent:
        hidden_copy(r).wait_send()
    if fast:
        for gather in gathers.values():
            gather.drain()
        for k in range(4):
            swap(k).wait_send()
        totals.drain()
    for name in started:
        saves[name].wait()


def forward_plan(rows, units):
    plan = []
    for r in range(rows):
        plan += [(Key.frame, r), (Key.send, r)]
    for k in range(4):
        plan += [(Key.lay, k)]
    for n in range(5):
        plan += [(Key.total, n)]
    for r in range(rows):
        plan += [(Key.cot, r)]
    for w in (Key.w_input, Key.w_output, Key.w_inner, Key.w_outer):
        for e in range(5):
            plan += [(Key.event, w, 0, e)]
        plan += [(Key.loaded, w)]
    for part in range(3):
        plan += [(Key.project_own, part)]
    for r in range(rows):
        plan += [(Key.other, r), (Key.project_other, r, 0), (Key.project_other, r, 1)]
        plan += [(Key.attend_pairs, r), (Key.attend_padding, r), (Key.first_norm, r)]
    plan += [(Key.hidden_units, 0, units)]
    for r in range(rows):
        plan += [(Key.second_norm, r)]
    for name in (Key.layer_out, Key.k_input, Key.k_output, Key.k_inner, Key.k_outer, Key.k_own, Key.k_other, Key.k_packed, Key.k_pairs,
                 Key.k_soft, Key.k_context, Key.k_norm, Key.k_inverse, Key.k_active, Key.k_slope, Key.k_grad, Key.k_vectors):
        plan += [(Key.save, name)]
    return plan


def forward_call(mesh_rows, fast, hidden, cot, masters, small, lengths, routes, plan, with_saves=True):
    rows, slots, width = hidden.shape
    pairs = lengths.shape[2]
    tokens = rows * slots
    units = masters[2].shape[1]
    nz = mesh_rows // 4
    tall = [width, width, width, units]
    wide = [3 * width, width, units, width]
    if fast:
        shapes = [(2, nz, 2, tall[k] // (4 * nz), wide[k]) for k in range(4)]
    else:
        shapes = [(1, 1, 1, tall[k], wide[k]) for k in range(4)]
    weights = [Key.w_input, Key.w_output, Key.w_inner, Key.w_outer]
    ins = [Key.hidden_in, Key.cotangent, Key.m_input, Key.m_output, Key.m_inner, Key.m_outer]
    ins += [(Key.vector, k) for k in range(len(small))] + [Key.lengths]
    hbm, vmem, smem = (pl.BlockSpec(memory_space=s) for s in (pl.ANY, pltpu.VMEM, pltpu.SMEM))
    if fast:
        args = [hidden.reshape(tokens, width), cot.reshape(tokens, width), *masters, *small, lengths]
    else:
        args = [hidden.reshape(tokens, width), cot.reshape(tokens, width)]
        args += [m.reshape(s) for m, s in zip(masters, shapes, strict=True)] + [*small, lengths]
    in_specs = [hbm, hbm] + [vmem if fast else hbm] * 4 + [vmem] * len(small) + [smem]
    outs = {Key.layer_out: ((tokens, width), bf16), Key.k_sums: ((24, width), f32)}
    saved = {
        Key.k_input: (shapes[0], bf16), Key.k_output: (shapes[1], bf16), Key.k_inner: (shapes[2], bf16),
        Key.k_outer: (shapes[3], bf16), Key.k_own: ((tokens, width), bf16), Key.k_other: ((tokens, width), bf16),
        Key.k_packed: ((tokens, 3 * width), bf16), Key.k_pairs: ((tokens, 2 * width), bf16),
        Key.k_soft: ((tokens, width), bf16), Key.k_context: ((tokens, width), bf16),
        Key.k_norm: ((tokens, width), f32), Key.k_inverse: ((tokens, 128), f32),
        Key.k_active: ((tokens, units), bf16), Key.k_slope: ((tokens, units), bf16),
        Key.k_grad: ((tokens, width), f32), Key.k_low: ((tokens, width), bf16), Key.k_vectors: ((VECTORS, width), f32),
    }
    if with_saves:
        outs.update(saved)
    out_specs = [vmem if name == Key.k_sums else hbm for name in outs]
    scratch = {
        Key.w_input: pltpu.VMEM(shapes[0], bf16), Key.w_output: pltpu.VMEM(shapes[1], bf16),
        Key.w_inner: pltpu.VMEM(shapes[2], bf16), Key.w_outer: pltpu.VMEM(shapes[3], bf16),
        Key.hidden: pltpu.VMEM((tokens, width), bf16), Key.cot: pltpu.VMEM((tokens, width), bf16),
        Key.own: pltpu.VMEM((tokens, width), bf16), Key.other: pltpu.VMEM((tokens, width), bf16),
        Key.packed: pltpu.VMEM((tokens, 3 * width), bf16), Key.pairs_other: pltpu.VMEM((tokens, 2 * width), bf16),
        Key.context: pltpu.VMEM((tokens, width), bf16), Key.soft: pltpu.VMEM((tokens, width), bf16),
        Key.norm: pltpu.VMEM((tokens, width), f32), Key.inverse: pltpu.VMEM((tokens, 128), f32),
        Key.low: pltpu.VMEM((tokens, width), bf16), Key.active: pltpu.VMEM((tokens, units), bf16),
        Key.slope: pltpu.VMEM((tokens, units), bf16), Key.grad: pltpu.VMEM((tokens, width), f32),
        Key.sums: pltpu.VMEM((2, slots, width), f32), Key.framed: pltpu.VMEM((slots, width), bf16),
        Key.vectors: pltpu.VMEM((VECTORS, width), f32), Key.ff_bias: pltpu.VMEM((1, units), f32),
        Key.gain_sum: pltpu.VMEM((8, width), f32), Key.shift_sum: pltpu.VMEM((8, width), f32),
        Key.low_sum: pltpu.VMEM((8, width), f32),
        Key.local_sem: pltpu.SemaphoreType.DMA((6 + len(saved) + 1,)),
        Key.row_send: pltpu.SemaphoreType.DMA((rows,)), Key.row_recv: pltpu.SemaphoreType.DMA((rows,)),
    }
    if fast:
        steps, partners = 3, nz + 3
        pieces = sum(len(v) for v in routes.values())
        slots_each = nz + 1 + 1 + 2 * (nz - 1)
        scratch.update({
            Key.table: pltpu.VMEM((steps + 1, VECTORS, width), f32), Key.table_in: pltpu.VMEM((partners, VECTORS, width), f32),
            Key.table_send: pltpu.SemaphoreType.DMA((partners,)), Key.table_recv: pltpu.SemaphoreType.DMA((partners,)),
            Key.piece_send: pltpu.SemaphoreType.DMA((pieces, slots_each)),
            Key.piece_recv: pltpu.SemaphoreType.DMA((pieces, slots_each)),
            Key.swap_send: pltpu.SemaphoreType.DMA((4,)), Key.swap_recv: pltpu.SemaphoreType.DMA((4,)),
        })
        for k in range(4):
            scratch[Key.from_sibling, k] = pltpu.VMEM((masters[k].shape[0], wide[k] // 2), f32)
    names = ins + list(outs) + list(scratch)
    sizes = (rows, slots, width, pairs)
    body = functools.partial(forward_kernel, names, fast, sizes, routes, plan)
    found = pl.pallas_call(
        body,
        out_shape=[jax.ShapeDtypeStruct(*s) for s in outs.values()],
        in_specs=in_specs,
        out_specs=out_specs,
        scratch_shapes=list(scratch.values()),
        compiler_params=pltpu.CompilerParams(
            collective_id=0, has_side_effects=True, vmem_limit_bytes=FORWARD_VMEM
        ),
        name="forward",
    )(*args)
    return dict(zip(outs, found, strict=True))


class Scatter:
    def __init__(self, buf, place, swapped, landed, final, out, send, recv, routes, starts, width):
        self.buf, self.place, self.swapped, self.landed = buf, place, swapped, landed
        self.final, self.out, self.send, self.recv, self.routes = final, out, send, recv, routes
        self.starts, self.width = starts, width
        self.sizes = dict(zip("XZY", buf.shape[:3], strict=True))
        self.core_rows = buf.shape[3] // 2

    def cols(self, core):
        first, second = self.starts
        return pl.ds(pl.multiple_of(first + core * (second - first), 128), self.width)

    def remote(self, src, dst, slot, device):
        return pltpu.make_async_remote_copy(
            src_ref=src,
            dst_ref=dst,
            send_sem=self.send.at[slot],
            recv_sem=self.recv.at[slot],
            device_id=device,
            device_id_type=MESH,
        )

    def per_core(self, act):
        if self.routes[0] == self.routes[1]:
            act(self.routes[0])
            return
        for core in range(2):
            pl.when(self.place.c == core)(functools.partial(act, self.routes[core]))

    def lead(self, route, stage, at):
        own = {**self.place.own, **at}
        fixed = route[: stage + 1]
        return tuple(own[d] if d in fixed else ALL for d in "XZY")

    def swap(self):
        place = self.place
        src = self.buf.at[ALL, ALL, ALL, ALL, self.cols(1 - place.c)]
        return self.remote(src, self.swapped, 0, place.device(C=1 - place.c))

    def sends(self, route, stage):
        dim = route[stage]
        mine = self.landed.at[self.lead(route, stage, {})]
        found = []
        for k, peer in enumerate(self.place.peers(dim)):
            src = self.buf.at[self.lead(route, stage, {dim: peer}) + (ALL, self.cols(self.place.c))]
            found.append(self.remote(src, mine, 1 + self.place.first_slot(dim) + k, self.place.device(**{dim: peer})))
        return found

    def arrivals(self, route, stage):
        dim = route[stage]
        found = []
        for k, peer in enumerate(self.place.sources(dim)):
            view = self.landed.at[self.lead(route, stage, {dim: peer})]
            found.append(self.remote(view, view, 1 + self.place.first_slot(dim) + k, self.place.device()))
        return found

    def blocks(self, free, body):
        total = math.prod(self.sizes[d] for d in free)

        def visit(i):
            at = dict(self.place.own)
            for d in reversed(free):
                at[d] = i % self.sizes[d]
                i = i // self.sizes[d]
            body((at["X"], at["Z"], at["Y"]), at)

        if total == 1:
            visit(0)
        else:
            pl.loop(0, total)(visit)

    def start_swap(self):
        self.swap().start()

    def add_swapped(self):
        self.swap().wait_recv()
        cols = self.cols(self.place.c)

        def body(block, at):
            there = block + (ALL, cols)
            total = self.buf[there].astype(f32) + self.swapped[block].astype(f32)
            self.buf[there] = total.astype(bf16)

        self.blocks("XZY", body)

        def act(route):
            for copy in self.sends(route, 0):
                copy.start()

        self.per_core(act)

    def add_stage(self, stage):
        cols = self.cols(self.place.c)

        def act(route):
            dim = route[stage]
            for copy in self.arrivals(route, stage):
                copy.wait_recv()
            sources = self.place.sources(dim)

            def body(block, at):
                total = self.buf[block + (ALL, cols)].astype(f32)
                for peer in sources:
                    theirs = {**at, dim: peer}
                    total = total + self.landed[theirs["X"], theirs["Z"], theirs["Y"]].astype(f32)
                if stage < 2:
                    self.buf[block + (ALL, cols)] = total.astype(bf16)
                else:
                    self.final[...] = total

            self.blocks("".join(d for d in "XZY" if d not in route[: stage + 1]), body)
            if stage < 2:
                for copy in self.sends(route, stage + 1):
                    copy.start()

        self.per_core(act)
        if stage == 2:
            for copy in self.hand_over():
                copy.start()

    def hand_over(self):
        place, count = self.place, self.core_rows
        cols = self.cols(place.c)
        mine = self.final.at[pl.ds(pl.multiple_of(place.c * count, 8), count)]
        theirs = self.final.at[pl.ds(pl.multiple_of((1 - place.c) * count, 8), count)]
        there = self.remote(theirs, self.out.at[:, cols], 1 + place.slots(), place.device(C=1 - place.c))
        here = pltpu.make_async_copy(mine, self.out.at[:, cols], self.send.at[2 + place.slots()])
        return [there, here]

    def finish(self):
        there, here = self.hand_over()
        here.wait()
        there.wait_send()
        view = self.out.at[:, self.cols(1 - self.place.c)]
        self.remote(view, view, 1 + self.place.slots(), self.place.device()).wait_recv()

    def drain(self):
        self.swap().wait_send()

        def act(route):
            for stage in range(3):
                for copy in self.sends(route, stage):
                    copy.wait_send()

        self.per_core(act)

    def event(self, number):
        if number == 0:
            self.start_swap()
        elif number == 1:
            self.add_swapped()
        elif number < 5:
            self.add_stage(number - 2)
        else:
            self.finish()


class Backward:
    def __init__(self, refs, place, sizes):
        self.__dict__.update(attributes(refs))
        self.place = place
        self.rows, self.slots, self.width, self.pairs = sizes
        self.most = self.slots // self.pairs
        self.half = place.x
        self.scale = (self.width // HEADS) ** (-0.5)
        self.tokens = self.rows * self.slots
        self.units = self.active.shape[1]

    def sizes_of(self, row, half):
        return [self.lengths[row, half, p] for p in range(self.pairs)]

    def row(self, r):
        return pl.ds(r * self.slots, self.slots)

    def vector(self, at):
        return rounded(self.vectors[at : at + 1, :])

    def lower_norm(self):
        gain, shift = self.vector(GAIN_1), self.vector(SHIFT_1)

        @pl.loop(0, self.tokens // 64, unroll=4)
        def _(i):
            rows = block_rows(i, 64)
            self.low[rows, :] = (self.norm[rows, :] * gain + shift).astype(bf16)

    def grad_outer(self):
        nz = self.d_outer.shape[1]
        parts = self.d_outer.shape[0] * nz
        size = self.units // parts

        @pl.loop(0, parts)
        def _(i):
            found = contract(self.active[:, pl.ds(pl.multiple_of(i * size, 128), size)], self.grad_low[...], 0, 0)
            self.d_outer[i // nz, i % nz] = found.astype(bf16).reshape(self.d_outer.shape[2:])

    def grad_hidden(self, first, count, size=384):
        @pl.loop(first, first + count, unroll=2)
        def _(n):
            cols = pl.ds(pl.multiple_of(n * size, size), size)
            weight = self.w_outer[cols, :]
            total = jnp.zeros((8, size), f32)
            for r in range(self.rows):
                found = contract(self.grad_low[self.row(r), :], weight, 1, 1)
                low = (found * self.slope[self.row(r), cols].astype(f32)).astype(bf16)
                self.slope[self.row(r), cols] = low
                total = total + folded(low.astype(f32))
            self.ff_sums[:, cols] = total

    def grad_inner(self, core, part, size=768):
        half = self.units // 2
        cols = pl.ds(pl.multiple_of(core * half + part * size, 128), size)
        found = contract(self.low[...], self.slope[:, cols], 0, 0).astype(bf16)
        self.d_inner[:, :, :, :, cols] = found.reshape(self.d_inner.shape[:4] + (size,))

    def first_back(self, r):
        if r < self.rows:
            rows = self.row(r)
            weight = self.w_inner[...].reshape(self.width, self.units)
            self.grad[rows, :] = self.grad[rows, :] + contract(self.slope[rows, :], weight, 1, 1)
        if r == 0:
            for at in (GAIN_1, SHIFT_1, O_BIAS):
                self.col_sums[at] = jnp.zeros((8, self.width), f32)
            return
        gain = self.vector(GAIN_1)
        kinds = (GAIN_1, SHIFT_1, O_BIAS)
        sums = [self.col_sums[at] for at in kinds]
        for i in range(0, self.slots, 32):
            there = pl.ds((r - 1) * self.slots + i, 32)
            grad = self.grad[there, :]
            norm = self.norm[there, :]
            incoming = grad * gain
            plain = jnp.mean(incoming, axis=1, keepdims=True)
            along = jnp.mean(incoming * norm, axis=1, keepdims=True)
            attn = self.inverse[there, 0:1] * (incoming - plain - norm * along)
            self.grad[there, :] = attn
            low = attn.astype(bf16)
            self.grad_low[there, :] = low
            parts = (grad * norm, grad, low.astype(f32))
            sums = [total + folded(part) for total, part in zip(sums, parts, strict=True)]
        for at, total in zip(kinds, sums, strict=True):
            self.col_sums[at] = total

    def grad_output(self):
        context = self.w_outer[2 * self.tokens : 3 * self.tokens, :]
        found = contract(context, self.grad_low[...], 0, 0).astype(bf16)
        self.d_output[...] = found.reshape(self.d_output.shape)

    def grad_context(self, r):
        rows = self.row(r)
        weight = self.w_output[...].reshape(self.width, self.width)
        self.low[rows, :] = contract(self.grad_low[rows, :], weight, 1, 1).astype(bf16)

    def attend_back(self, r, together=4):
        most, span, width, wide = self.most, 4 * (self.width // HEADS), self.width, 2 * self.most
        spread = spread_heads(wide, span)
        first = iota((most, 4 * wide), 1) % wide < most

        def tiled(v):
            return jnp.where(spread, jnp.concatenate([v] * 4, axis=0), 0).astype(bf16)

        def two_pairs(pair):
            rows = pl.ds(pl.multiple_of(r * self.slots + pair * wide, wide), wide)
            for at in range(0, width, span):
                here = [slice(part * width + at, part * width + at + span) for part in range(4)]
                queries = tiled(self.active[rows, here[0]])
                keys = jnp.concatenate([self.active[rows, here[1]], self.slope[rows, here[0]]], axis=0)
                values = jnp.concatenate([self.active[rows, here[2]], self.slope[rows, here[1]]], axis=0)
                kept = self.active[rows, here[3]].astype(f32)
                mine, theirs = kept[:most], kept[most:]
                soft = jnp.concatenate(
                    [
                        jnp.where(first, mine, 0.0), jnp.where(first, 0.0, mine),
                        jnp.where(first, theirs, 0.0), jnp.where(first, 0.0, theirs),
                    ],
                    axis=0,
                )
                grad = tiled(self.low[rows, here[0]])
                grad_soft = contract(values, grad, 1, 1)
                delta = jnp.sum(soft * grad_soft, axis=0, keepdims=True)
                grad_scores = (soft * (grad_soft - delta)).astype(bf16)
                grad_values = contract(soft.astype(bf16), grad, 1, 0).astype(bf16)
                grad_keys = (contract(grad_scores, queries, 1, 0) * self.scale).astype(bf16)
                mixed = jnp.where(spread, contract(grad_scores, keys, 0, 0), 0.0)
                grad_queries = sum(mixed[h * wide : (h + 1) * wide, :] for h in range(4)) * self.scale
                self.active[rows, here[0]] = grad_queries.astype(bf16)
                self.active[rows, here[1]] = grad_keys[:wide]
                self.active[rows, here[2]] = grad_values[:wide]
                self.slope[rows, here[0]] = grad_keys[wide:]
                self.slope[rows, here[1]] = grad_values[wide:]

        @pl.loop(0, self.pairs // (2 * together))
        def _(several):
            for k in range(together):
                two_pairs(several * together + k)

    def input_weight(self, first, last):
        weight = self.w_inner[:, :, :, :, first:last] if self.fast else self.w_input[:, :, :, :, first:last]
        return weight.reshape(self.width, last - first)

    def return_other(self, r):
        rows = self.row(r)
        weight = self.input_weight(self.width, 3 * self.width)
        self.grad_low[rows, :] = contract(self.slope[rows, : 2 * self.width], weight, 1, 1).astype(bf16)

    def token_sums(self):
        width = self.width
        self.col_sums[Q_BIAS] = jnp.zeros((8, width), f32)
        self.col_sums[V_BIAS] = jnp.zeros((8, width), f32)

        @pl.loop(0, self.tokens // 64, unroll=4)
        def _(i):
            rows = block_rows(i, 64)
            self.col_sums[Q_BIAS] += folded(self.active[rows, :width].astype(f32))
            both = self.active[rows, 2 * width : 3 * width].astype(f32) + self.slope[rows, width : 2 * width].astype(f32)
            self.col_sums[V_BIAS] += folded(both)

        self.col_sums[GAIN_2] = self.k_sums[0:8, :]
        self.col_sums[SHIFT_2] = self.k_sums[8:16, :]
        self.col_sums[OUT_BIAS] = self.k_sums[16:24, :]
        rows = [jnp.sum(self.col_sums[at], axis=0, keepdims=True) for at in range(8)]
        units = jnp.sum(self.ff_sums[...], axis=0, keepdims=True)
        count = self.units // width
        rows += [units[:, k * width : (k + 1) * width] for k in range(count)]
        rows += [jnp.zeros((VECTORS - 8 - count, width), f32)]
        self.table[0] = jnp.concatenate(rows, axis=0)

    def grad_input_weight(self, part):
        width = self.width
        cols = pl.ds(pl.multiple_of(part * width, 128), width)
        target = self.d_inner

        def keep(found):
            target[:, :, :, :, cols] = found.astype(bf16).reshape(target.shape[:4] + (width,))

        if isinstance(part, int) and part == 0:
            keep(contract(self.w_outer[: self.tokens, :], self.active[:, :width], 0, 0))
            return
        there = pl.ds(pl.multiple_of((part - 1) * width, 128), width)
        found = contract(self.w_outer[: self.tokens, :], self.active[:, cols], 0, 0)
        keep(found + contract(self.w_outer[self.tokens : 2 * self.tokens, :], self.slope[:, there], 0, 0))

    def grad_hidden_in(self, r):
        rows = self.row(r)
        found = contract(self.active[rows, : 3 * self.width], self.input_weight(0, 3 * self.width), 1, 1)
        found = found + self.grad[rows, :] + self.back[rows, :].astype(f32)
        high = found.astype(bf16)
        rest = (found - high.astype(f32)).astype(bf16)
        back = out_of_frames(self.sizes_of(r, self.half), self.slots, self.most)
        self.norm[rows, :] = contract(back, high, 1, 0) + contract(back, rest, 1, 0)


BACKWARD_VMEM = 127 * 2**19


def backward_kernel(names, fast, sizes, routes, plan, *refs):
    refs = dict(zip(names, refs, strict=True))
    rows, slots, width, pairs = sizes
    tokens = rows * slots
    place = Place(lax.axis_size("rows"))
    run = Backward(refs, place, sizes)
    run.fast = fast
    partner = place.device(X=1 - place.x)
    in_outer = [run.w_outer.at[pl.ds(k * tokens, tokens)] for k in range(3)]
    loads = {
        Key.grad: (run.k_grad, run.grad), Key.low: (run.k_low, run.grad_low), Key.active: (run.k_active, run.active), Key.outer: (run.k_outer, run.w_outer),
        Key.slope: (run.k_slope, run.slope), Key.norm: (run.k_norm, run.norm), Key.inner: (run.k_inner, run.w_inner),
        Key.inverse: (run.k_inverse, run.inverse), Key.output: (run.k_output, run.w_output),
        Key.vectors: (run.k_vectors, run.vectors),
        Key.packed: (run.k_packed, run.active.at[:, pl.ds(0, 3 * width)]),
        Key.soft: (run.k_soft, run.active.at[:, pl.ds(3 * width, width)]),
        Key.pairs: (run.k_pairs, run.slope.at[:, pl.ds(0, 2 * width)]),
        Key.own: (run.k_own, in_outer[0]), Key.other: (run.k_other, in_outer[1]), Key.context: (run.k_context, in_outer[2]),
        Key.input: (run.k_input, run.w_inner.at[:, :, :, :, pl.ds(0, 3 * width)] if fast else run.w_input),
    }
    order = {name: k for k, name in enumerate(loads)}

    def load(name):
        return pltpu.make_async_copy(*loads[name], run.local_sem.at[order[name]])

    scatters = {}
    for name in (Key.low, Key.active):
        load(name).start()
    if fast:
        greet(place, neighbours(place))
        totals = Totals(place, run.table, run.table_in, run.table_send, run.table_recv)
        targets = {Key.outer: run.d_outer, Key.inner: run.d_inner, Key.output: run.d_output, Key.input: run.d_inner}
        for name, pieces in routes.items():
            for j, (route, starts, span) in enumerate(pieces):
                at = len(scatters)
                scatters[name, j] = Scatter(
                    targets[name], place, refs[Key.swapped, name, j], refs[Key.landed, name, j],
                    refs[Key.final, name, j], refs["g", name], run.piece_send.at[at], run.piece_recv.at[at],
                    route, starts, span,
                )
    else:
        greet(place, [partner])

    def returned(r):
        view = pl.ds(r * slots, slots)
        return pltpu.make_async_remote_copy(
            src_ref=run.grad_low.at[view],
            dst_ref=run.back.at[view],
            send_sem=run.row_send.at[r],
            recv_sem=run.row_recv.at[r],
            device_id=partner,
            device_id_type=MESH,
        )

    def put(r):
        view = pl.ds(r * slots, slots)
        return pltpu.make_async_copy(run.norm.at[view], run.grad_input.at[view], run.out_sem.at[r])

    whole = {Key.outer: Key.d_outer, Key.inner: Key.d_inner, Key.output: Key.d_output, Key.input: Key.d_inner}

    def keep(name):
        src = refs[whole[name]]
        if name == Key.input:
            src = src.at[:, :, :, :, pl.ds(0, 3 * width)]
        return pltpu.make_async_copy(src, refs["g", name], run.keep_sem.at[list(whole).index(name)])

    sent, written, summed = [], [], []

    def step(what, *detail):
        if what == Key.load:
            load(detail[0]).start()
        elif what == Key.loaded:
            load(detail[0]).wait()
        elif what == Key.event:
            if fast:
                scatters[detail[0], detail[1]].event(detail[2])
        elif what == Key.drain:
            if fast:
                for (name, _), scatter in scatters.items():
                    if name == detail[0]:
                        scatter.drain()
            else:
                keep(detail[0]).wait()
        elif what == Key.keep:
            if not fast:
                keep(detail[0]).start()
        elif what == Key.grad_inner:
            core = 1 - place.c if detail[0] == 0 else place.c
            run.grad_inner(core, *detail[1:])
        elif what == Key.grad_input_weight:
            run.grad_input_weight(detail[0])
        elif what == Key.send:
            returned(detail[0]).start()
            sent.append(detail[0])
        elif what == Key.back:
            returned(detail[0]).wait_recv()
        elif what == Key.total:
            if not fast:
                return
            if detail[0] < 0:
                totals.start(0)
                summed.append(True)
            else:
                totals.advance(detail[0])
        elif what == Key.put:
            put(detail[0]).start()
            written.append(detail[0])
        else:
            getattr(run, what.name)(*detail)

    for entry in plan:
        step(*entry)
    for r in sent:
        returned(r).wait_send()
    for r in written:
        put(r).wait()
    if fast:
        if summed: totals.drain()
        table = run.table[len(totals.steps)]
        devices = 2 * lax.axis_size("rows")
        piece = width // devices
        wide = piece * (run.units // width)
        per_row = width // wide
        upper = pltpu.roll(table[:8], (devices - place.index) * piece % width, axis=1)
        lower = jnp.where(iota((8, width), 0) == place.index // per_row, table[8:], 0.0)
        lower = jnp.sum(lower, axis=0, keepdims=True)
        lower = pltpu.roll(jnp.broadcast_to(lower, (8, width)), (per_row - place.index % per_row) * wide % width, axis=1)
        run.g_small[...] = jnp.concatenate([upper[:, :128], lower[:, :128]], axis=0)
    else:
        run.g_small[...] = run.table[0]


def backward_call(mesh_rows, fast, kept, lengths, routes, plan, sizes, units):
    rows, slots, width, pairs = sizes
    tokens = rows * slots
    nz = mesh_rows // 4
    hbm, vmem, smem = (pl.BlockSpec(memory_space=s) for s in (pl.ANY, pltpu.VMEM, pltpu.SMEM))
    ins = [
        Key.k_input, Key.k_output, Key.k_inner, Key.k_outer, Key.k_own, Key.k_other, Key.k_packed, Key.k_pairs, Key.k_soft, Key.k_context,
        Key.k_norm, Key.k_inverse, Key.k_active, Key.k_slope, Key.k_grad, Key.k_vectors, Key.k_low,
    ]
    kept = dict(kept)
    kept[Key.k_outer] = kept[Key.k_outer].reshape(units, width)
    args = [kept[name] for name in ins] + [kept[Key.k_sums], lengths]
    in_specs = [hbm] * len(ins) + [vmem, smem]
    tall = {Key.outer: units, Key.inner: width, Key.output: width, Key.input: width}
    wide = {Key.outer: width, Key.inner: units, Key.output: width, Key.input: 3 * width}
    lead = (2, nz, 2) if fast else (1, 1, 1)
    blocks = math.prod(lead)
    outs = {Key.grad_input: ((tokens, width), f32)}
    for name in tall:
        if fast:
            outs["g", name] = ((tall[name] // (2 * blocks), wide[name]), f32)
        else:
            outs["g", name] = (lead + (tall[name], wide[name]), bf16)
    outs[Key.g_small] = ((VECTORS, 128 if fast else width), f32)
    out_specs = [vmem if name == Key.g_small else hbm for name in outs]
    steps, partners = (3, nz + 3) if fast else (0, 0)
    scratch = {
        Key.w_outer: pltpu.VMEM((units, width), bf16), Key.w_inner: pltpu.VMEM(lead + (width // blocks, units), bf16),
        Key.w_output: pltpu.VMEM(lead + (width // blocks, width), bf16),
        Key.active: pltpu.VMEM((tokens, units), bf16), Key.slope: pltpu.VMEM((tokens, units), bf16),
        Key.grad: pltpu.VMEM((tokens, width), f32), Key.norm: pltpu.VMEM((tokens, width), f32),
        Key.inverse: pltpu.VMEM((tokens, 128), f32), Key.vectors: pltpu.VMEM((VECTORS, width), f32),
        Key.grad_low: pltpu.VMEM((tokens, width), bf16), Key.low: pltpu.VMEM((tokens, width), bf16),
        Key.back: pltpu.VMEM((tokens, width), bf16),
        Key.col_sums: pltpu.VMEM((8, 8, width), f32),
        Key.ff_sums: pltpu.VMEM((8, units), f32),
        Key.d_outer: pltpu.VMEM(lead + (units // blocks, width), bf16),
        Key.d_inner: pltpu.VMEM(lead + (width // blocks, units), bf16),
        Key.d_output: pltpu.VMEM(lead + (width // blocks, width), bf16),
        Key.table: pltpu.VMEM((steps + 1, VECTORS, width), f32),
        Key.local_sem: pltpu.SemaphoreType.DMA((17,)), Key.out_sem: pltpu.SemaphoreType.DMA((rows,)),
        Key.row_send: pltpu.SemaphoreType.DMA((rows,)), Key.row_recv: pltpu.SemaphoreType.DMA((rows,)),
    }
    if fast:
        pieces = sum(len(v) for v in routes.values())
        scratch.update({
            Key.table_in: pltpu.VMEM((partners, VECTORS, width), f32),
            Key.table_send: pltpu.SemaphoreType.DMA((partners,)), Key.table_recv: pltpu.SemaphoreType.DMA((partners,)),
            Key.piece_send: pltpu.SemaphoreType.DMA((pieces, nz + 4)),
            Key.piece_recv: pltpu.SemaphoreType.DMA((pieces, nz + 4)),
        })
        for name, found in routes.items():
            height = tall[name] // blocks
            for j, (_, _, span) in enumerate(found):
                scratch[Key.swapped, name, j] = pltpu.VMEM(lead + (height, span), bf16)
                scratch[Key.landed, name, j] = pltpu.VMEM(lead + (height, span), bf16)
                scratch[Key.final, name, j] = pltpu.VMEM((height, span), f32)
    else:
        scratch[Key.w_input] = pltpu.VMEM(lead + (width, 3 * width), bf16)
        scratch[Key.keep_sem] = pltpu.SemaphoreType.DMA((4,))
    names = ins + [Key.k_sums, Key.lengths] + list(outs) + list(scratch)
    found = pl.pallas_call(
        functools.partial(backward_kernel, names, fast, sizes, routes, plan),
        out_shape=[jax.ShapeDtypeStruct(*s) for s in outs.values()],
        in_specs=in_specs,
        out_specs=out_specs,
        scratch_shapes=list(scratch.values()),
        compiler_params=pltpu.CompilerParams(
            collective_id=1, has_side_effects=True, vmem_limit_bytes=BACKWARD_VMEM
        ),
        name="backward",
    )(*args)
    return dict(zip(outs, found, strict=True))


def plain_forward(rows, units):
    plan = []
    for r in range(rows):
        plan += [(Key.frame, r), (Key.send, r), (Key.cot, r)]
    plan += [(Key.loaded, Key.w_input), (Key.save, Key.k_vectors)]
    plan += [(Key.project_own, part) for part in range(3)] + [(Key.loaded, Key.w_output)]
    for r in range(rows):
        plan += [(Key.other, r), (Key.project_other, r, 0), (Key.project_other, r, 1)]
        plan += [(Key.attend_pairs, r), (Key.attend_padding, r)]
    plan += [(Key.first_norm, r) for r in range(rows + 1)]
    plan += [(Key.loaded, Key.w_inner), (Key.hidden_units, 0, units // 256), (Key.loaded, Key.w_outer)]
    plan += [(Key.save, Key.k_soft), (Key.saved, Key.k_soft)] + [(Key.second_norm, r) for r in range(rows + 1)]
    saved = (Key.layer_out, Key.k_input, Key.k_output, Key.k_inner, Key.k_outer, Key.k_own, Key.k_other, Key.k_packed, Key.k_pairs)
    saved += (Key.k_context, Key.k_norm, Key.k_inverse, Key.k_active, Key.k_slope, Key.k_grad, Key.k_low)
    return plan + [(Key.save, name) for name in saved]


def plain_backward(rows, units):
    first = (Key.vectors, Key.grad, Key.outer, Key.slope, Key.norm, Key.inner, Key.inverse, Key.output)
    plan = [(Key.load, name) for name in first] + [(Key.loaded, name) for name in first + (Key.low, Key.active)]
    plan += [(Key.lower_norm,), (Key.grad_outer,)]
    plan += [(Key.grad_hidden, 0, units // 384), (Key.keep, Key.outer)]
    plan += [(Key.grad_inner, core, part) for core in range(2) for part in range(units // 1536)] + [(Key.keep, Key.inner)]
    plan += [(Key.load, name) for name in (Key.own, Key.other, Key.context, Key.packed, Key.soft)]
    plan += [(Key.first_back, r) for r in range(rows + 1)]
    plan += [(Key.load, Key.pairs), (Key.load, Key.input)]
    plan += [(Key.loaded, name) for name in (Key.own, Key.other, Key.context, Key.packed, Key.soft, Key.pairs, Key.input)]
    plan += [(Key.grad_output,), (Key.keep, Key.output)]
    plan += [(Key.grad_context, r) for r in range(rows)] + [(Key.drain, Key.inner)]
    for r in range(rows):
        plan += [(Key.attend_back, r), (Key.return_other, r), (Key.send, r)]
    plan += [(Key.token_sums,)] + [(Key.grad_input_weight, part) for part in range(3)]
    plan += [(Key.keep, Key.input)]
    for r in range(rows):
        plan += [(Key.back, r), (Key.grad_hidden_in, r), (Key.put, r)]
    return plan + [(Key.drain, Key.outer), (Key.drain, Key.output), (Key.drain, Key.input)]


GATHER = {
    Key.w_input: (
        (("ZYX", "ZXY"), 0, 640, 0, 48),
        (("XZY", "XZY"), 640, 512, 0, 48),
    ),
    Key.w_output: (
        (("ZXY", "ZXY"), 0, 384, 0, 48),
    ),
    Key.w_inner: (
        (("ZYX", "XZY"), 0, 768, 0, 48),
        (("ZYX", "XZY"), 768, 768, 0, 48),
    ),
    Key.w_outer: (
        (("XZY", "ZYX"), 0, 384, 0, 96),
        (("XZY", "XYZ"), 0, 384, 96, 96),
    ),
}
SCATTER = {
    Key.outer: (
        (("XYZ", "ZXY"), (0, 512), 256),
        (("YXZ", "YZX"), (256, 384), 128),
    ),
    Key.inner: (
        (("YZX", "XYZ"), (0, 1536), 768),
        (("XZY", "YXZ"), (768, 2304), 768),
    ),
    Key.output: (
        (("XZY", "YZX"), (0, 384), 384),
    ),
    Key.input: (
        (("ZYX", "YXZ"), (0, 1536), 768),
        (("YZX", "YXZ"), (768, 1152), 384),
    ),
}
FORWARD_PLAN = (
    (Key.lay, 0), (Key.event, Key.w_input, 0, 0), (Key.event, Key.w_input, 1, 0), (Key.frame, 0), (Key.frame, 1),
    (Key.frame, 2), (Key.frame, 3), (Key.lay, 1), (Key.lay, 2), (Key.lay, 3), (Key.cot, 0), (Key.cot, 1), (Key.total, 0),
    (Key.cot, 2), (Key.event, Key.w_output, 0, 0), (Key.event, Key.w_inner, 0, 0), (Key.cot, 3), (Key.send, 2),
    (Key.event, Key.w_input, 1, 1), (Key.event, Key.w_input, 0, 1), (Key.total, 1), (Key.event, Key.w_inner, 1, 0),
    (Key.event, Key.w_output, 0, 1), (Key.send, 0), (Key.event, Key.w_inner, 0, 1), (Key.event, Key.w_input, 0, 2),
    (Key.event, Key.w_outer, 1, 0), (Key.send, 3), (Key.event, Key.w_outer, 0, 0), (Key.event, Key.w_output, 0, 2),
    (Key.send, 1), (Key.event, Key.w_input, 1, 2), (Key.total, 2), (Key.event, Key.w_inner, 1, 1),
    (Key.event, Key.w_output, 0, 3), (Key.event, Key.w_input, 0, 3), (Key.event, Key.w_output, 0, 4),
    (Key.save, Key.k_output), (Key.event, Key.w_outer, 1, 1), (Key.event, Key.w_input, 0, 4), (Key.event, Key.w_inner, 0, 2),
    (Key.event, Key.w_input, 1, 3), (Key.event, Key.w_input, 1, 4), (Key.save, Key.k_input), (Key.save, Key.k_own),
    (Key.project_own, 0), (Key.project_own, 1), (Key.event, Key.w_outer, 0, 1), (Key.project_own, 2),
    (Key.save, Key.k_packed), (Key.save, Key.k_vectors), (Key.other, 0), (Key.project_other, 0, 0),
    (Key.project_other, 0, 1), (Key.attend_pairs, 0), (Key.event, Key.w_inner, 1, 2), (Key.attend_padding, 0),
    (Key.other, 1), (Key.project_other, 1, 0), (Key.project_other, 1, 1), (Key.attend_pairs, 1),
    (Key.attend_padding, 1), (Key.event, Key.w_outer, 1, 2), (Key.other, 2), (Key.project_other, 2, 0),
    (Key.project_other, 2, 1), (Key.attend_pairs, 2), (Key.attend_padding, 2), (Key.event, Key.w_inner, 0, 3),
    (Key.other, 3), (Key.project_other, 3, 0), (Key.project_other, 3, 1), (Key.save, Key.k_pairs), (Key.save, Key.k_other),
    (Key.attend_pairs, 3), (Key.save, Key.k_soft), (Key.event, Key.w_outer, 0, 2), (Key.event, Key.w_inner, 0, 4),
    (Key.attend_padding, 3), (Key.save, Key.k_context), (Key.first_norm, 0), (Key.first_norm, 1),
    (Key.event, Key.w_inner, 1, 3), (Key.first_norm, 2), (Key.first_norm, 3), (Key.first_norm, 4), (Key.save, Key.k_norm),
    (Key.save, Key.k_inverse), (Key.event, Key.w_inner, 1, 4), (Key.save, Key.k_inner), (Key.hidden_units, 0, 2),
    (Key.hidden_units, 2, 2), (Key.hidden_units, 4, 2), (Key.hidden_units, 6, 2), (Key.event, Key.w_outer, 0, 3),
    (Key.hidden_units, 8, 2), (Key.event, Key.w_outer, 1, 3), (Key.event, Key.w_outer, 0, 4), (Key.hidden_units, 10, 2),
    (Key.save, Key.k_active), (Key.save, Key.k_slope), (Key.event, Key.w_outer, 1, 4), (Key.save, Key.k_outer),
    (Key.saved, Key.k_soft), (Key.second_norm, 0), (Key.second_norm, 1), (Key.second_norm, 2), (Key.second_norm, 3),
    (Key.second_norm, 4), (Key.save, Key.layer_out), (Key.save, Key.k_grad), (Key.save, Key.k_low),
)
BACKWARD_PLAN = (
    (Key.loaded, Key.low), (Key.loaded, Key.active), (Key.load, Key.outer), (Key.load, Key.slope), (Key.load, Key.vectors),
    (Key.load, Key.norm), (Key.load, Key.inner), (Key.load, Key.grad), (Key.load, Key.inverse), (Key.load, Key.output),
    (Key.grad_outer,), (Key.event, Key.outer, 0, 0), (Key.loaded, Key.outer), (Key.loaded, Key.slope),
    (Key.loaded, Key.vectors), (Key.load, Key.packed), (Key.load, Key.soft), (Key.grad_hidden, 0, 2),
    (Key.grad_hidden, 2, 2), (Key.grad_hidden, 4, 2), (Key.event, Key.outer, 0, 1), (Key.grad_hidden, 6, 2),
    (Key.load, Key.own), (Key.load, Key.other), (Key.load, Key.context), (Key.loaded, Key.norm), (Key.lower_norm,),
    (Key.grad_inner, 0, 0), (Key.event, Key.inner, 0, 0), (Key.grad_inner, 1, 0), (Key.grad_inner, 0, 1),
    (Key.event, Key.inner, 1, 0), (Key.event, Key.inner, 0, 1), (Key.grad_inner, 1, 1), (Key.loaded, Key.inner),
    (Key.loaded, Key.inverse), (Key.loaded, Key.grad), (Key.first_back, 0), (Key.event, Key.inner, 1, 1),
    (Key.first_back, 1), (Key.first_back, 2), (Key.event, Key.outer, 1, 0), (Key.first_back, 3), (Key.first_back, 4),
    (Key.load, Key.pairs), (Key.load, Key.input), (Key.loaded, Key.context), (Key.loaded, Key.output), (Key.grad_output,),
    (Key.event, Key.output, 0, 0), (Key.event, Key.inner, 0, 2), (Key.event, Key.outer, 1, 1), (Key.event, Key.outer, 0, 2),
    (Key.event, Key.output, 0, 1), (Key.grad_context, 0), (Key.grad_context, 1), (Key.grad_context, 2),
    (Key.grad_context, 3), (Key.loaded, Key.packed), (Key.loaded, Key.soft), (Key.loaded, Key.pairs), (Key.loaded, Key.input),
    (Key.attend_back, 0), (Key.event, Key.inner, 1, 2), (Key.return_other, 0), (Key.send, 0), (Key.attend_back, 1),
    (Key.event, Key.inner, 0, 3), (Key.return_other, 1), (Key.send, 1), (Key.attend_back, 2), (Key.return_other, 2),
    (Key.send, 2), (Key.attend_back, 3), (Key.event, Key.inner, 1, 3), (Key.event, Key.outer, 1, 2), (Key.return_other, 3),
    (Key.send, 3), (Key.token_sums,), (Key.total, -1), (Key.loaded, Key.own), (Key.loaded, Key.other),
    (Key.event, Key.outer, 0, 3), (Key.event, Key.inner, 0, 4), (Key.event, Key.output, 0, 2), (Key.total, 0),
    (Key.event, Key.inner, 1, 4), (Key.event, Key.inner, 0, 5), (Key.drain, Key.inner), (Key.grad_input_weight, 0),
    (Key.event, Key.inner, 1, 5), (Key.grad_input_weight, 2), (Key.event, Key.input, 0, 0), (Key.grad_input_weight, 1),
    (Key.event, Key.input, 1, 0), (Key.event, Key.input, 0, 1), (Key.event, Key.outer, 0, 4), (Key.event, Key.input, 1, 1),
    (Key.back, 0), (Key.grad_hidden_in, 0), (Key.put, 0), (Key.event, Key.outer, 0, 5), (Key.back, 1),
    (Key.grad_hidden_in, 1), (Key.put, 1), (Key.event, Key.output, 0, 3), (Key.event, Key.outer, 1, 3), (Key.back, 2),
    (Key.grad_hidden_in, 2), (Key.put, 2), (Key.back, 3), (Key.grad_hidden_in, 3), (Key.put, 3),
    (Key.event, Key.input, 1, 2), (Key.event, Key.input, 0, 2), (Key.event, Key.output, 0, 4), (Key.total, 1),
    (Key.event, Key.outer, 1, 4), (Key.event, Key.output, 0, 5), (Key.event, Key.outer, 1, 5), (Key.event, Key.input, 1, 3),
    (Key.event, Key.input, 0, 3), (Key.event, Key.input, 1, 4), (Key.total, 2), (Key.event, Key.input, 1, 5),
    (Key.event, Key.input, 0, 4), (Key.event, Key.input, 0, 5), (Key.drain, Key.outer), (Key.drain, Key.output),
    (Key.drain, Key.input),
)


def gather_routes(masters):
    return {
        name: [(route, (row, count), (col, span)) for route, col, span, row, count in found]
        for name, found in GATHER.items()
    }


def scatter_routes(width, units):
    return SCATTER


def forward_steps(rows, nz, units):
    return FORWARD_PLAN


def backward_steps(rows, nz):
    return BACKWARD_PLAN


def spread(masters, vectors):
    gathered = [lax.all_gather(v.astype(bf16), ("pair", "rows"), axis=0, tiled=True) for v in masters]
    rows = [lax.all_gather(v, ("pair", "rows"), axis=0, tiled=True) for v in vectors]
    width = rows[0].shape[0]
    table = jnp.concatenate(rows).reshape(-1, width)
    return gathered, [jnp.pad(table, ((0, VECTORS - table.shape[0]), (0, 0)))]


def gather_sums(found, units):
    def summed(v):
        return lax.psum_scatter(v.astype(f32), ("pair", "rows"), scatter_dimension=0, tiled=True)

    weights = {name: summed(found[name].reshape(found[name].shape[3:])) for name in found if name != Key.g_small}
    table = found[Key.g_small]
    width = table.shape[1]
    small = [summed(table[k]) for k in range(8)] + [summed(table[8 : 8 + units // width].reshape(units))]
    return weights, small


def settle(arrays):
    parts = []
    for k, v in enumerate(arrays):
        count = 4 if v.shape[0] % 64 == 0 else 1
        size = v.shape[0] // count
        parts += [(k, pl.ds(i * size, size)) for i in range(count)]

    def kernel(*refs):
        count = len(arrays)
        ins, outs, held, sems = refs[:count], refs[count : 2 * count], refs[2 * count : 3 * count], refs[-1]
        loads = [pltpu.make_async_copy(ins[k].at[at], held[k].at[at], sems.at[0, n]) for n, (k, at) in enumerate(parts)]
        stores = [pltpu.make_async_copy(held[k].at[at], outs[k].at[at], sems.at[1, n]) for n, (k, at) in enumerate(parts)]
        for load in loads:
            load.start()
        for load, store in zip(loads, stores, strict=True):
            load.wait()
            store.start()
        for store in stores:
            store.wait()

    return pl.pallas_call(
        kernel,
        out_shape=[jax.ShapeDtypeStruct(v.shape, v.dtype) for v in arrays],
        in_specs=[pl.BlockSpec(memory_space=pl.ANY)] * len(arrays),
        out_specs=[pl.BlockSpec(memory_space=pl.ANY)] * len(arrays),
        scratch_shapes=[pltpu.VMEM(v.shape, v.dtype) for v in arrays] + [pltpu.SemaphoreType.DMA((2, len(parts)))],
        compiler_params=pltpu.CompilerParams(vmem_limit_bytes=BACKWARD_VMEM),
        name="k_settle",
    )(*arrays)


def shards(rows_axis, *args):
    (
        hidden_in, input_proj, query_bias, value_bias, output_proj, output_bias, first_gain, first_shift,
        inner_proj, inner_bias, outer_proj, outer_bias, second_gain, second_shift, cotangent, pair_lengths,
    ) = args
    row_count, _, slots, width = hidden_in.shape
    units = inner_proj.shape[1]
    share = input_proj.shape[0]
    fast = rows_axis % 4 == 0 and share % 8 == 0
    masters = (input_proj, output_proj, inner_proj, outer_proj)
    vectors = (
        query_bias, value_bias, output_bias, first_gain, first_shift, outer_bias, second_gain, second_shift,
        inner_bias,
    )
    if fast:
        routes_f, plan_f = gather_routes(masters), forward_steps(row_count, rows_axis // 4, units)
        routes_b, plan_b = scatter_routes(width, units), backward_steps(row_count, rows_axis // 4)
        small = [v.reshape(1, -1) for v in vectors]
    else:
        routes_f, routes_b = {}, {}
        plan_f, plan_b = plain_forward(row_count, units), plain_backward(row_count, units)
        masters, small = spread(masters, vectors)
    sizes = (row_count, slots, width, pair_lengths.shape[2])
    kept = forward_call(
        rows_axis, fast, hidden_in[:, 0], cotangent[:, 0], masters, small, pair_lengths, routes_f, plan_f
    )
    found = backward_call(rows_axis, fast, kept, pair_lengths, routes_b, plan_b, sizes, units)
    layer_out, grad_input = kept[Key.layer_out], found.pop(Key.grad_input)
    if fast:
        weights = (Key.input, Key.output, Key.inner, Key.outer)
        results = settle([layer_out, grad_input] + [found["g", name] for name in weights])
        layer_out, grad_input = results[:2]
        found.update(zip([("g", name) for name in weights], results[2:], strict=True))
        table = found[Key.g_small]
        sums = [table[k, :share] for k in range(8)] + [table[8, : inner_bias.shape[0]]]
    else:
        found, sums = gather_sums(found, units)
    return (
        layer_out.reshape(hidden_in.shape), grad_input.reshape(hidden_in.shape), found["g", Key.input], sums[Q_BIAS], sums[V_BIAS], found["g", Key.output], sums[O_BIAS],
        sums[GAIN_1], sums[SHIFT_1], found["g", Key.inner], sums[FF_ROW], found["g", Key.outer], sums[OUT_BIAS],
        sums[GAIN_2], sums[SHIFT_2],
    )


def solution(mesh):
    tokens = P("rows", "pair", None, None)
    matrix = P(("pair", "rows"), None)
    vector = P(("pair", "rows"))
    weights = (
        matrix, vector, vector, matrix, vector, vector, vector, matrix, vector, matrix, vector, vector, vector
    )
    return jax.shard_map(
        functools.partial(shards, mesh.shape["rows"]),
        mesh=mesh,
        in_specs=(tokens, *weights, tokens, P("rows", None, None)),
        out_specs=(tokens, tokens, *weights),
        check_vma=False,
    )
```
